32 devices in a mesh: seq: 8 (over z, y), batch: 4 (over x, core).
Axes of the slice: x: 2, y: 2, z: 4, core: 2. Of those that a mesh axis runs over, the one named last changes fastest.
Arguments:
- tokens: bfloat16 [4, 3072, 1152], P('batch', 'seq'), may hold values from -6 to 6
- skip_tokens: bfloat16 [4, 3072, 1152], P('batch', 'seq'), may hold values from -6 to 6
- segment_ids: int32 [4, 3072], P('batch'), may hold values from 0 to 11, as said below
- upstream: bfloat16 [4, 3072, 1152], P('batch', 'seq'), may hold values from -6 to 6
- skip_weight: bfloat16 [2304, 1152], replicated, may hold values from -0.125 to 0.125
- skip_bias: bfloat16 [1152], replicated, may hold values from -1.5 to 1.5
- first_gain: bfloat16 [1152], replicated, may hold values from 0.25 to 1.75
- first_shift: bfloat16 [1152], replicated, may hold values from -1.5 to 1.5
- attn_weight: bfloat16 [1152, 3456], replicated, may hold values from -0.1875 to 0.1875
- attn_bias: bfloat16 [2304], replicated, may hold values from -1.5 to 1.5
- proj_weight: bfloat16 [1152, 1152], replicated, may hold values from -1.5 to 1.5
- proj_bias: bfloat16 [1152], replicated, may hold values from -1.5 to 1.5
- second_gain: bfloat16 [1152], replicated, may hold values from 0.25 to 1.75
- second_shift: bfloat16 [1152], replicated, may hold values from -1.5 to 1.5
- expand_weight: bfloat16 [1152, 4608], replicated, may hold values from -0.1875 to 0.1875
- expand_bias: bfloat16 [4608], replicated, may hold values from -1.5 to 1.5
- shrink_weight: bfloat16 [4608, 1152], replicated, may hold values from -0.09375 to 0.09375
- shrink_bias: bfloat16 [1152], replicated, may hold values from -1.5 to 1.5
Outputs:
- result: bfloat16 [4, 3072, 1152], P('batch', 'seq')
- tokens_grad: bfloat16 [4, 3072, 1152], P('batch', 'seq')
- skip_grad: bfloat16 [4, 3072, 1152], P('batch', 'seq')
- skip_weight_grad: float32 [2304, 1152], P('seq', 'batch')
- skip_bias_grad: float32 [1152], P(('seq', 'batch'))
- first_gain_grad: float32 [1152], P(('seq', 'batch'))
- first_shift_grad: float32 [1152], P(('seq', 'batch'))
- attn_weight_grad: float32 [1152, 3456], P('seq', 'batch')
- attn_bias_grad: float32 [2304], P(('seq', 'batch'))
- proj_weight_grad: float32 [1152, 1152], P('seq', 'batch')
- proj_bias_grad: float32 [1152], P(('seq', 'batch'))
- second_gain_grad: float32 [1152], P(('seq', 'batch'))
- second_shift_grad: float32 [1152], P(('seq', 'batch'))
- expand_weight_grad: float32 [1152, 4608], P('seq', 'batch')
- expand_bias_grad: float32 [4608], P(('seq', 'batch'))
- shrink_weight_grad: float32 [4608, 1152], P('seq', 'batch')
- shrink_bias_grad: float32 [1152], P(('seq', 'batch'))
The draws below stay inside these ranges and needn't reach their ends.
Inputs may be any that keep to these rules, and one draw needn't show every extreme that they name: `segment_ids`: along each group the ids start at 0 and rise by one from item to item, and every group holds the same number of items. Every item holds 194 to 322 rows, except a group's last, which may hold fewer; each group's first item holds exactly 322.
All inputs are finite; a program needn't handle non-finite values.
Results may differ from the reference program's by a relative error of at most 0.017.
Values may be sent and summed in bfloat16 or wider, within the bound.
A program may use at most 256 MiB of HBM per device.

```python
import jax
import jax.numpy as jnp
from jax import lax

D = 1152
HEADS = 16
FF = 4608
TOK_DEV = 384
ITEM_LEAST = 194
ITEM_MOST = 322
GROUPS = 4
LENGTH = 3072


def draw_segment_ids(key, part):
    key = jax.random.fold_in(key, 11)
    pair_rows = ITEM_LEAST + ITEM_MOST
    pair_count = LENGTH // pair_rows
    firsts = jax.random.randint(key, (GROUPS, pair_count), ITEM_LEAST + 1, ITEM_MOST, dtype=jnp.int32)
    firsts = firsts.at[:, 0].set(ITEM_MOST)
    seconds = pair_rows - firsts
    paired = jnp.stack([firsts, seconds], axis=2).reshape(GROUPS, 2 * pair_count)
    tail = jnp.full((GROUPS, 2), ITEM_MOST - 1, dtype=jnp.int32)
    tail = tail.at[:, 1].set(LENGTH + 1)
    lengths = jnp.concatenate([paired, tail], axis=1)
    item_ends = jnp.cumsum(lengths, axis=1).astype(jnp.int32)
    positions = jnp.arange(LENGTH, dtype=jnp.int32)
    return jnp.sum((item_ends[:, None, :] <= positions[None, :, None]).astype(jnp.int32), axis=-1).astype(jnp.int32)


def levels(rng, extent, cuts, low, largest):
    level, own = 1.0, jax.random.fold_in(rng, 6)
    for dim, blocks in cuts:
        draws = jnp.exp(jax.random.uniform(jax.random.fold_in(own, dim), (blocks,), jnp.float32, low / len(cuts), largest / len(cuts)))
        level = level * jnp.repeat(draws, extent[dim] // blocks).reshape([-1 if axis == dim else 1 for axis in range(len(extent))])
    return level


def noise(key, extent, scale, limit, cuts=(), held_as=jnp.bfloat16):
    gain = levels(key, extent, cuts, -0.22, 0.18) if cuts else 1.0
    drawn = jax.random.normal(key, extent, jnp.float32) * scale * gain
    return jnp.minimum(jnp.maximum(drawn, -limit), limit).astype(held_as)


def setup_inputs(seed: int = 0) -> dict:
    splits = jax.random.split(jax.random.key(seed), 19)
    return {
        "tokens": noise(splits[0], (GROUPS, LENGTH, D), 1.0, 6.0, ((0, 4), (1, 8))),
        "skip_tokens": noise(splits[1], (GROUPS, LENGTH, D), 1.0, 6.0, ((0, 4), (1, 8))),
        "segment_ids": draw_segment_ids(jax.random.fold_in(splits[18], 71), 0),
        "upstream": noise(splits[3], (GROUPS, LENGTH, D), 1.0, 6.0, ((0, 4), (1, 8))),
        "skip_weight": noise(splits[4], (2 * D, D), (2 * D) ** -0.5, 0.125),
        "skip_bias": noise(splits[5], (D,), 0.3, 1.5),
        "first_gain": jnp.clip(1.0 + 0.15 * jax.random.normal(splits[6], (D,), jnp.float32), 0.25, 1.75).astype(jnp.bfloat16),
        "first_shift": noise(splits[7], (D,), 0.3, 1.5),
        "attn_weight": noise(splits[8], (D, 3 * D), D ** -0.5, 0.1875),
        "attn_bias": noise(splits[9], (2 * D,), 0.3, 1.5),
        "proj_weight": noise(splits[10], (D, D), (D // 64) ** -0.5, 1.5),
        "proj_bias": noise(splits[11], (D,), 0.3, 1.5),
        "second_gain": jnp.clip(1.0 + 0.15 * jax.random.normal(splits[12], (D,), jnp.float32), 0.25, 1.75).astype(jnp.bfloat16),
        "second_shift": noise(splits[13], (D,), 0.3, 1.5),
        "expand_weight": noise(splits[14], (D, FF), D ** -0.5, 0.1875),
        "expand_bias": noise(splits[15], (FF,), 0.3, 1.5),
        "shrink_weight": noise(splits[16], (FF, D), FF ** -0.5, 0.09375),
        "shrink_bias": noise(splits[17], (D,), 0.3, 1.5),
    }


@jax.custom_vjp
def low(v):
    return lax.optimization_barrier(v.astype(jnp.bfloat16)).astype(jnp.float32)

@jax.custom_vjp
def low_back(v):
    return v

def low_keep(v):
    return (low(v), None)

def low_pass(kept, grad):
    return (grad,)

def back_keep(v):
    return (v, None)

def back_low(kept, grad):
    return (low(grad),)
low.defvjp(low_keep, low_pass)
low_back.defvjp(back_keep, back_low)

def matmul(operand, other_op):
    return jnp.dot(operand, other_op, precision=lax.Precision.HIGHEST, preferred_element_type=jnp.float32)

def normalize(inputs, gain_vec, shift_vec):
    centred = inputs - lax.optimization_barrier(jnp.mean(inputs, axis=-1, keepdims=True))
    variance = lax.optimization_barrier(jnp.mean(centred * centred, axis=-1, keepdims=True))
    return centred * lax.rsqrt(variance + 1e-05) * gain_vec + shift_vec

def attend(queries, key_rows, value_rows, segment_row):
    length, features = queries.shape
    blocks = length // TOK_DEV
    head_dim = features // HEADS

    def windows(tensor):
        padded = jnp.pad(tensor.reshape(blocks, TOK_DEV, features), ((1, 1), (0, 0), (0, 0)))
        joined = jnp.concatenate([padded[:-2], padded[1:-1], padded[2:]], axis=1)
        return joined.reshape(blocks, 3 * TOK_DEV, HEADS, head_dim)
    padded_ids = jnp.pad(segment_row.reshape(blocks, TOK_DEV), ((1, 1), (0, 0)), constant_values=-1)
    key_ids = jnp.concatenate([padded_ids[:-2], padded_ids[1:-1], padded_ids[2:]], axis=1)
    query_ids = segment_row.reshape(blocks, TOK_DEV)
    query_blocks = queries.reshape(blocks, TOK_DEV, HEADS, head_dim)

    def one_block(pieces):
        query_block, key_block, value_block, query_row, key_row = pieces
        products = low_back(jnp.einsum('qhd,khd->hqk', query_block, key_block, precision=lax.Precision.HIGHEST))
        matching = query_row[:, None] == key_row[None, :]
        scores = jnp.where(matching[None], products * head_dim ** (-0.5), -1e+30)
        highest = lax.optimization_barrier(jnp.max(scores, axis=-1, keepdims=True))
        raised = jnp.exp(scores - highest)
        attention = raised / lax.optimization_barrier(jnp.sum(raised, axis=-1, keepdims=True))
        return jnp.einsum('hqk,khd->qhd', low(attention), value_block, precision=lax.Precision.HIGHEST)
    mixed_blocks = lax.map(jax.checkpoint(one_block), (query_blocks, windows(key_rows), windows(value_rows), query_ids, key_ids))
    return mixed_blocks.reshape(length, features)

def forward_layer(params, token_in, skip_in, segment_row):
    skip_weight, skip_bias, first_gain, first_shift, attn_weight, attn_bias, proj_weight, proj_bias, second_gain, second_shift, expand_weight, expand_bias, shrink_weight, shrink_bias = params
    features = token_in.shape[-1]
    joined = jnp.concatenate([token_in, skip_in], axis=-1)
    stream = low_back(matmul(joined, skip_weight) + skip_bias)
    normed = low(normalize(stream, first_gain, first_shift))
    triple = matmul(normed, attn_weight)
    queries = low(low_back(triple[:, :features] + attn_bias[:features]))
    key_rows = low(low_back(triple[:, features:2 * features]))
    value_rows = low(low_back(triple[:, 2 * features:] + attn_bias[features:]))
    mixed = low(low_back(attend(queries, key_rows, value_rows, segment_row)))
    branch = low_back(matmul(mixed, proj_weight) + proj_bias)
    middle = stream + branch
    second = low(normalize(middle, second_gain, second_shift))
    hidden = low_back(matmul(second, expand_weight) + expand_bias)
    active = low(jax.nn.gelu(hidden, approximate=False))
    return middle + matmul(active, shrink_weight) + shrink_bias

def reference(tokens, skip_tokens, segment_ids, upstream, skip_weight, skip_bias, first_gain, first_shift, attn_weight, attn_bias, proj_weight, proj_bias, second_gain, second_shift, expand_weight, expand_bias, shrink_weight, shrink_bias):
    params = tuple((weight_in.astype(jnp.float32) for weight_in in (skip_weight, skip_bias, first_gain, first_shift, attn_weight, attn_bias, proj_weight, proj_bias, second_gain, second_shift, expand_weight, expand_bias, shrink_weight, shrink_bias)))
    initial = jax.tree.map(jnp.zeros_like, params)

    def group_step(totals, pieces):
        token_row, skip_row, ids_row, grad_row = pieces

        def forward(params_in, token_in, skip_in):
            return forward_layer(params_in, token_in, skip_in, ids_row)
        output, pullback = jax.vjp(forward, params, token_row.astype(jnp.float32), skip_row.astype(jnp.float32))
        grads, token_grad, skip_back = pullback(grad_row.astype(jnp.float32))
        totals = jax.tree.map(jnp.add, totals, grads)
        return (totals, (output.astype(jnp.bfloat16), token_grad.astype(jnp.bfloat16), skip_back.astype(jnp.bfloat16)))
    totals, outputs = lax.scan(group_step, initial, (tokens, skip_tokens, segment_ids, upstream))
    return (outputs[0], outputs[1], outputs[2], totals[0], totals[1], totals[2], totals[3], totals[4], totals[5], totals[6], totals[7], totals[8], totals[9], totals[10], totals[11], totals[12], totals[13])
```

```python
from functools import partial

import jax
import jax.numpy as jnp
from jax import lax
from jax.experimental import pallas as pl
from jax.experimental.pallas import tpu as pltpu
from jax.sharding import PartitionSpec as P

HEADS = 16
ITEM_MOST = 322
LANES = 128
MESH = pl.DeviceIdType.MESH


def padded(value, sides, width):
    for axis, dim in sides:
        size, length = (lax.axis_size(axis), value.shape[dim])
        up = [(i, (i + 1) % size) for i in range(size - 1)]
        down = [(j, i) for i, j in up]
        last = lax.slice_in_dim(value, length - width, length, axis=dim)
        first = lax.slice_in_dim(value, 0, width, axis=dim)
        before = lax.ppermute(last, axis, up)
        after = lax.ppermute(first, axis, down)
        value = jnp.concatenate([before, value, after], axis=dim)
    return value


def shortened(value):
    return jax.tree.map(lambda a: a.astype(jnp.bfloat16) if a.dtype == jnp.float32 else a, value)


def normalize(inputs, gain_vec, shift_vec):
    centred = inputs - jnp.mean(inputs, axis=-1, keepdims=True)
    variance = jnp.mean(centred * centred, axis=-1, keepdims=True)
    return centred * lax.rsqrt(variance + 1e-05) * gain_vec + shift_vec


def matmul(operand, other_op):
    return jnp.dot(operand, other_op, preferred_element_type=jnp.float32)


def outer_sum(left, right):
    return lax.dot_general(
        left, right, (((0,), (0,)), ((), ())), preferred_element_type=jnp.float32
    )


def to_items(tensor, blocks):
    group_count, length, features = tensor.shape
    reshaped = tensor.reshape(group_count, length, blocks, features // blocks)
    return jnp.transpose(reshaped, (0, 2, 1, 3)).reshape(
        group_count * blocks, length, features // blocks
    )


def from_items(tensor, blocks):
    item_count, length, features = tensor.shape
    reshaped = tensor.reshape(item_count // blocks, blocks, length, features)
    return jnp.transpose(reshaped, (0, 2, 1, 3)).reshape(
        item_count // blocks, length, blocks * features
    )


def masked_scores(query_part, key_part, query_ids, key_ids, head_dim):
    query_heads = query_part.reshape(query_part.shape[0], -1, head_dim)
    key_heads = key_part.reshape(key_part.shape[0], -1, head_dim)
    products = jnp.einsum(
        "qhd,khd->hqk", query_heads, key_heads, preferred_element_type=jnp.float32
    )
    matching = query_ids[:, None] == key_ids[None, :]
    return jnp.where(matching[None], products * head_dim ** (-0.5), -1e30)


def forward_block(pieces, head_dim):
    query_part, key_part, value_part, query_ids, key_ids = pieces
    scores = masked_scores(query_part, key_part, query_ids, key_ids, head_dim)
    highest = jnp.max(scores, axis=-1, keepdims=True)
    raised = jnp.exp(scores - highest)
    denominator = jnp.sum(raised, axis=-1, keepdims=True)
    attention = raised / denominator
    value_heads = value_part.reshape(value_part.shape[0], -1, head_dim)
    mixed_heads = jnp.einsum(
        "hqk,khd->qhd",
        attention.astype(jnp.bfloat16),
        value_heads,
        preferred_element_type=jnp.float32,
    )
    return (mixed_heads.reshape(query_part.shape[0], -1), (highest + jnp.log(denominator))[..., 0])


def backward_block(pieces, head_dim):
    query_part, key_part, value_part, query_ids, key_ids, grad_part, lse_part = pieces
    length = query_part.shape[0]
    key_span = key_part.shape[0]
    scores = masked_scores(query_part, key_part, query_ids, key_ids, head_dim)
    attention = jnp.exp(scores - lse_part[..., None])
    query_heads = query_part.reshape(length, -1, head_dim)
    key_heads = key_part.reshape(key_span, -1, head_dim)
    value_heads = value_part.reshape(key_span, -1, head_dim)
    grad_heads = grad_part.reshape(length, -1, head_dim)
    prob_grad = jnp.einsum(
        "qhd,khd->hqk", grad_heads, value_heads, preferred_element_type=jnp.float32
    )
    row_dot = jnp.sum(attention * prob_grad, axis=-1, keepdims=True)
    score_grad = (head_dim ** (-0.5) * attention * (prob_grad - row_dot)).astype(jnp.bfloat16)
    query_grad = jnp.einsum(
        "hqk,khd->qhd", score_grad, key_heads, preferred_element_type=jnp.float32
    )
    key_grad = jnp.einsum(
        "hqk,qhd->khd", score_grad, query_heads, preferred_element_type=jnp.float32
    )
    value_grad = jnp.einsum(
        "hqk,qhd->khd",
        attention.astype(jnp.bfloat16),
        grad_heads,
        preferred_element_type=jnp.float32,
    )
    return (
        query_grad.reshape(length, -1),
        key_grad.reshape(key_span, -1),
        value_grad.reshape(key_span, -1),
    )


class Unit:
    def __init__(self, left, left_at, right, right_at, tiles, rows, blocks, out, out_at):
        self.left, self.left_at = left, left_at
        self.right, self.right_at = right, right_at
        self.tiles = tiles
        self.rows = rows
        self.blocks = blocks
        self.places = 1 + max(block[3] for block in blocks)
        self.out, self.out_at = out, out_at

    def shape(self, *lead):
        if self.tiles:
            return (*lead, self.rows, LANES)
        return (*lead, self.rows * 7 // 3, LANES)

    @property
    def x_size(self):
        return 2 * (self.tiles or 1)

    @property
    def part_shape(self):
        return self.shape(2, self.x_size, 2, self.places)

    @property
    def first_shapes(self):
        half = self.x_size // 2
        if self.tiles:
            return (self.shape(half, 2, self.places), self.shape(2 * half, self.places))
        return (self.shape(2, self.places), self.shape(2, self.places))

    @property
    def second_shape(self):
        if self.tiles:
            return self.shape(self.tiles, self.places)
        return self.shape(self.places)

    @property
    def chain_shape(self):
        return self.shape(self.tiles) if self.tiles else self.shape()

    def view(self, ref, order, x, y, place=None):
        if x is None:
            x_at = slice(None)
        elif self.tiles:
            x_at = pl.ds(x * self.tiles, self.tiles)
        else:
            x_at = x
        y_at = slice(None) if y is None else y
        if place is None:
            return ref.at[order, x_at, y_at]
        return ref.at[order, x_at, y_at, place]

    def chains(self):
        return sorted({(order, place, z) for _, order, _, place, z in self.blocks})


def make_units():
    order_of = (0, 1, 1, 0)
    place_of = (0, 0, 1, 1)
    quarter = [
        ((2 * z + y) * 144, order_of[z], y, place_of[z], z) for z in range(4) for y in range(2)
    ]
    units = []
    for z in (0, 3, 1, 2):
        blocks = [(y * 576 + h * 288, h, y, 0, z) for y in range(2) for h in range(2)]
        units.append(Unit("active", z * 1152, "upstream", 0, 0, 288, blocks, "shrink", z))
    for j in range(3):
        units.append(Unit("second", 0, "hidden", j, 3, 144, quarter, "expand", j * 3))
    units.append(Unit("mixed", 0, "branch", 0, 0, 144, quarter, "proj", 0))
    units.append(Unit("normed", 0, "triple_a", 0, 4, 144, quarter, "attn", 0))
    units.append(Unit("normed", 0, "triple_b", 0, 3, 144, quarter, "attn", 4))
    for k in range(2):
        blocks = [(h * 576 + y * 288, h, y, 0, 2 * k + h) for h in range(2) for y in range(2)]
        units.append(Unit("joined", k * 1152, "stream", 0, 0, 288, blocks, "skip", k))
    return units


LEFTS = ("active", "second", "mixed", "normed", "joined")
RIGHTS = ("upstream", "hidden", "branch", "triple_a", "triple_b", "stream")
GRADS = ("shrink", "expand", "proj", "attn", "skip")
GRAD_SHAPES = ((576, 288), (144, 1152), (144, 288), (144, 896), (288, 288))


def add_into(target, other):
    target[...] = (target[...].astype(jnp.float32) + other[...].astype(jnp.float32)).astype(
        target.dtype
    )


class Links:
    def __init__(self):
        self.ids = {}

    def id(self, key):
        return self.ids.setdefault(key, len(self.ids))


def sum_kernel(units, names, *refs):
    r = dict(zip(names, refs))
    seq, batch = lax.axis_index("seq"), lax.axis_index("batch")
    z, y = seq // 2, seq % 2
    x, c = batch // 2, batch % 2
    partner = (seq, 2 * x + (1 - c))
    x_side = (seq, 2 * (1 - x) + c)
    y_side = (2 * z + (1 - y), batch)
    above = (2 * jnp.minimum(z + 1, 3) + y, batch)
    below = (2 * jnp.maximum(z - 1, 0) + y, batch)
    links = Links()

    barrier = pltpu.get_barrier_semaphore()
    for device in (partner, x_side, y_side):
        pl.semaphore_signal(barrier, 1, device_id=device, device_id_type=MESH)

    @pl.when(z < 3)
    def _():
        pl.semaphore_signal(barrier, 1, device_id=above, device_id_type=MESH)

    @pl.when(z > 0)
    def _():
        pl.semaphore_signal(barrier, 1, device_id=below, device_id_type=MESH)

    pl.semaphore_wait(barrier, 3 + (z < 3).astype(jnp.int32) + (z > 0).astype(jnp.int32))

    def remote(key, src, dst, device):
        i = links.id(key)
        return pltpu.make_async_remote_copy(
            src_ref=src,
            dst_ref=dst,
            send_sem=r["sent"].at[i],
            recv_sem=r["came"].at[i],
            device_id=device,
            device_id_type=MESH,
        )

    swaps = {}
    for unit in units:
        key = ("left", unit.left, unit.left_at)
        if key not in swaps:
            at = pl.ds(unit.left_at, 1152)
            swaps[key] = remote(
                key, r[unit.left].at[:, at], r["far_" + unit.left].at[:, at], partner
            )
        key = ("right", unit.right, unit.right_at)
        if key not in swaps:
            swaps[key] = remote(
                key,
                r[unit.right].at[1 - c, unit.right_at],
                r["far_" + unit.right].at[unit.right_at],
                partner,
            )
    for copy in swaps.values():
        copy.start()

    slots = {}
    turns = {"left": 0, "right": 0}

    def load(unit):
        started = []
        for side, name, at in (
            ("left", unit.left, unit.left_at),
            ("right", unit.right, unit.right_at),
        ):
            key = (side, name, at)
            if key in slots:
                continue
            slot = turns[side] % 2
            turns[side] += 1
            slots[key] = slot
            swaps[key].wait_recv()
            if side == "left":
                cols = pl.ds(at, 1152)
                near, far = r[name].at[:, cols], r["far_" + name].at[:, cols]
                hold = r["lefts"].at[slot]
            else:
                near, far = r[name].at[c, at], r["far_" + name].at[at]
                hold = r["rights"].at[slot, :, pl.ds(0, near.shape[-1])]
            for half, src in ((0, near), (1, far)):
                copy = pltpu.make_async_copy(
                    src, hold.at[pl.ds(384 * half, 384)], r[side + "_sem"].at[slot, half]
                )
                copy.start()
                started.append(copy)
        return started

    def compute(u):
        unit = units[u]
        part = r["part", u]
        left = r["lefts"].at[slots["left", unit.left, unit.left_at]]
        right = r["rights"].at[slots["right", unit.right, unit.right_at]]

        def product(n):
            cols = pl.ds(pl.multiple_of(n * 256, 256), 256)
            return lax.dot_general(
                left[...],
                right[:, cols],
                (((0,), (0,)), ((), ())),
                preferred_element_type=jnp.float32,
            )

        rows = unit.rows
        if unit.tiles:

            def body(n, carry):
                tile = product(n).astype(jnp.bfloat16)
                for first, order, y_at, place, _ in unit.blocks:
                    for i in range(2):
                        part[order, 2 * n + i, y_at, place] = tile[
                            first : first + rows, i * LANES : (i + 1) * LANES
                        ]
                return carry

            lax.fori_loop(0, unit.tiles, body, 0)
            return

        def body(n, carry):
            tile = product(n).astype(jnp.bfloat16)
            for first, order, y_at, place, _ in unit.blocks:
                for i in range(2):
                    part[order, n, y_at, place, pl.ds(i * rows, rows)] = tile[
                        first : first + rows, i * LANES : (i + 1) * LANES
                    ]
            return carry

        lax.fori_loop(0, 2, body, 0)
        tile = product(2)
        third = rows // 3
        for first, order, y_at, place, _ in unit.blocks:
            for x_at in range(2):
                pieces = [
                    tile[first + s * third : first + (s + 1) * third, x_at * LANES :][:, :32]
                    for s in range(3)
                ]
                packed = jnp.concatenate(pieces + [jnp.zeros_like(pieces[0])], axis=1)
                part[order, x_at, y_at, place, pl.ds(2 * rows, third)] = packed.astype(jnp.bfloat16)

    def first_copies(u):
        unit, part = units[u], r["part", u]
        return (
            remote(("first", u, 0), unit.view(part, 0, 1 - x, None), r["first", u, 0], x_side),
            remote(("first", u, 1), unit.view(part, 1, None, 1 - y), r["first", u, 1], y_side),
        )

    def second_copies(u):
        unit, part = units[u], r["part", u]
        return (
            remote(("second", u, 0), unit.view(part, 0, x, 1 - y), r["second", u].at[0], y_side),
            remote(("second", u, 1), unit.view(part, 1, 1 - x, y), r["second", u].at[1], x_side),
        )

    def first_stage(u):
        compute(u)
        for copy in first_copies(u):
            copy.start()

    def second_stage(u):
        unit, part = units[u], r["part", u]
        keeps = (unit.view(part, 0, x, None), unit.view(part, 1, None, y))
        for order, (copy, send) in enumerate(zip(first_copies(u), second_copies(u))):
            copy.wait_recv()
            add_into(keeps[order], r["first", u, order])
            send.start()

    def third_stage(u):
        unit, part = units[u], r["part", u]
        for order, copy in enumerate(second_copies(u)):
            copy.wait_recv()
            add_into(unit.view(part, order, x, y), r["second", u].at[order])

    def chain_copy(key, src, dsts, up):
        return remote((key, up), src, dsts[up], above if up else below)

    class Chain:
        def __init__(self, key, src, up_ref, down_ref, z_at):
            self.key, self.src, self.z_at = key, src, z_at
            self.refs = {True: up_ref, False: down_ref}

        def copy(self, up):
            return remote((self.key, up), self.src, self.refs[up], above if up else below)

        def hop(self, step):
            for up, me in ((True, step - 1), (False, 4 - step)):
                if (self.z_at > me) if up else (self.z_at < me):

                    @pl.when(z == me)
                    def _():
                        if step > 1:
                            self.copy(up).wait_recv()
                            add_into(self.src, self.refs[up])
                        self.copy(up).start()

        def total(self):
            value = self.src[...].astype(jnp.float32)
            for up, have in ((True, self.z_at > 0), (False, self.z_at < 3)):
                if have:
                    self.copy(up).wait_recv()
                    value = value + self.refs[up][...].astype(jnp.float32)
            return value

        def drain(self):
            for up, some in ((True, self.z_at > 0), (False, self.z_at < 3)):
                if some:

                    @pl.when((z < self.z_at) if up else (z > self.z_at))
                    def _():
                        self.copy(up).wait_send()

    def unit_chains(u):
        unit, part = units[u], r["part", u]
        found = []
        for order, place, z_at in unit.chains():
            src = unit.view(part, order, x, y, place)
            up = r["up", u, order, place] if z_at > 0 else None
            down = r["down", u, order, place] if z_at < 3 else None
            found.append((order, place, Chain(("chain", u, order, place), src, up, down, z_at)))
        return found

    def hop_stage(u, step):
        for _, _, chain in unit_chains(u):
            chain.hop(step)

    def last_stage(u):
        unit = units[u]
        out = r["out_" + unit.out]
        rows = unit.rows
        for order, place, chain in unit_chains(u):

            @pl.when(z == chain.z_at)
            def _():
                value = chain.total()
                if unit.tiles:
                    for t in range(unit.tiles):
                        at = (unit.out_at + t) * LANES
                        out[:, at : at + LANES] = value[t]
                    return
                base = order * rows if rows == 288 and unit.out == "shrink" else 0
                third = rows // 3
                for i in range(2):
                    out[base : base + rows, i * LANES : (i + 1) * LANES] = value[
                        i * rows : (i + 1) * rows
                    ]
                for s in range(3):
                    out[base + s * third : base + (s + 1) * third, 256:288] = value[
                        2 * rows : 2 * rows + third, s * 32 : (s + 1) * 32
                    ]

    vec = r["vec"]

    def vec_copies():
        return (
            remote("vec_core", vec.at[1 - c], r["vec_core"], partner),
            remote("vec_x", vec.at[c, 1 - x], r["vec_x"], x_side),
            remote("vec_y", vec.at[c, x, 1 - y], r["vec_y"], y_side),
        )

    vec_keeps = (vec.at[c], vec.at[c, x], vec.at[c, x, y])
    vec_lands = (r["vec_core"], r["vec_x"], r["vec_y"])
    vec_chains = [
        Chain(("vec", b), vec.at[c, x, y, b], r["vec_up"].at[b], r["vec_down"].at[b], b)
        for b in range(4)
    ]

    def vec_stage(step):
        if step < 3:
            if step > 0:
                vec_copies()[step - 1].wait_recv()
                add_into(vec_keeps[step - 1], vec_lands[step - 1])
            vec_copies()[step].start()
        elif step < 6:
            if step == 3:
                vec_copies()[2].wait_recv()
                add_into(vec_keeps[2], vec_lands[2])
            for chain in vec_chains:
                chain.hop(step - 2)
        elif step == 6:
            for chain in vec_chains:

                @pl.when(z == chain.z_at)
                def _():
                    r["out_vec"][...] = chain.total()

    count = len(units)
    started = load(units[0])
    for tick in range(count + 6):
        if tick < count:
            for copy in started:
                copy.wait()
            if tick + 1 < count:
                started = load(units[tick + 1])
            first_stage(tick)
        vec_stage(tick)
        if 0 <= tick - 1 < count:
            second_stage(tick - 1)
        if 0 <= tick - 2 < count:
            third_stage(tick - 2)
            hop_stage(tick - 2, 1)
        if 0 <= tick - 3 < count:
            hop_stage(tick - 3, 2)
        if 0 <= tick - 4 < count:
            hop_stage(tick - 4, 3)
        if 0 <= tick - 5 < count:
            last_stage(tick - 5)
    for copy in swaps.values():
        copy.wait_send()
    for u in range(count):
        for copy in first_copies(u) + second_copies(u):
            copy.wait_send()
        for _, _, chain in unit_chains(u):
            chain.drain()
    for copy in vec_copies():
        copy.wait_send()
    for chain in vec_chains:
        chain.drain()


def weight_sums(lefts, rights, vec):
    units = make_units()
    low = jnp.bfloat16
    names, in_specs, operands = [], [], []
    for name, value in [*lefts.items(), *rights.items()]:
        names.append(name)
        in_specs.append(pl.BlockSpec(memory_space=pl.ANY))
        operands.append(value)
    names.append("vec_in")
    in_specs.append(pl.BlockSpec(memory_space=pltpu.VMEM))
    operands.append(vec)
    out_shape, out_specs = [], []
    for name, shape in zip(GRADS, GRAD_SHAPES):
        names.append("out_" + name)
        out_shape.append(jax.ShapeDtypeStruct(shape, jnp.float32))
        out_specs.append(pl.BlockSpec(memory_space=pltpu.VMEM))
    names.append("out_vec")
    out_shape.append(jax.ShapeDtypeStruct((4, LANES), jnp.float32))
    out_specs.append(pl.BlockSpec(memory_space=pltpu.VMEM))
    for name in LEFTS:
        names.append("far_" + name)
        out_shape.append(jax.ShapeDtypeStruct(lefts[name].shape, low))
        out_specs.append(pl.BlockSpec(memory_space=pl.ANY))
    for name in RIGHTS:
        names.append("far_" + name)
        out_shape.append(jax.ShapeDtypeStruct(rights[name].shape[1:], low))
        out_specs.append(pl.BlockSpec(memory_space=pl.ANY))
    scratch = []

    def add(name, kind):
        names.append(name)
        scratch.append(kind)

    add("lefts", pltpu.VMEM((2, 768, 1152), low))
    add("rights", pltpu.VMEM((2, 768, 1024), low))
    add("left_sem", pltpu.SemaphoreType.DMA((2, 2)))
    add("right_sem", pltpu.SemaphoreType.DMA((2, 2)))
    for u, unit in enumerate(units):
        add(("part", u), pltpu.VMEM(unit.part_shape, low))
        for order in range(2):
            add(("first", u, order), pltpu.VMEM(unit.first_shapes[order], low))
        add(("second", u), pltpu.VMEM((2, *unit.second_shape), low))
        for order, place, z_at in unit.chains():
            if z_at > 0:
                add(("up", u, order, place), pltpu.VMEM(unit.chain_shape, low))
            if z_at < 3:
                add(("down", u, order, place), pltpu.VMEM(unit.chain_shape, low))
    add("vec", pltpu.VMEM(vec.shape, jnp.float32))
    add("vec_core", pltpu.VMEM(vec.shape[1:], jnp.float32))
    add("vec_x", pltpu.VMEM(vec.shape[2:], jnp.float32))
    add("vec_y", pltpu.VMEM(vec.shape[3:], jnp.float32))
    add("vec_up", pltpu.VMEM(vec.shape[3:], jnp.float32))
    add("vec_down", pltpu.VMEM(vec.shape[3:], jnp.float32))
    add("sent", pltpu.SemaphoreType.DMA((256,)))
    add("came", pltpu.SemaphoreType.DMA((256,)))

    def kernel(*refs):
        r = dict(zip(names, refs))
        r["vec"][...] = r["vec_in"][...]
        sum_kernel(units, names, *refs)

    found = pl.pallas_call(
        kernel,
        out_shape=out_shape,
        in_specs=in_specs,
        out_specs=out_specs,
        scratch_shapes=scratch,
        compiler_params=pltpu.CompilerParams(
            collective_id=0, has_side_effects=True, vmem_limit_bytes=60 * 2**20
        ),
        name="weight_sums",
    )(*operands)
    return dict(zip([*GRADS, "vec"], found[:6]))


def by_core(value):
    rows = value.shape[0]
    cut = value.reshape(rows, 2, 2, 288).transpose(2, 0, 1, 3)
    main = cut[..., :256].reshape(2, rows, 512)
    rest = jnp.pad(cut[..., 256:], ((0, 0), (0, 0), (0, 0), (0, 96))).reshape(2, rows, 256)
    return jnp.concatenate([main, rest], axis=-1)[:, None]


def by_core_wide(value, cuts):
    rows, total = value.shape
    cut = value.reshape(rows, 2, 2, total // 4).transpose(2, 0, 1, 3)
    found = []
    for first, width, pieces in cuts:
        part = cut[..., first : first + width * pieces]
        short = width * pieces - part.shape[-1]
        if short:
            part = jnp.pad(part, ((0, 0), (0, 0), (0, 0), (0, short)))
        part = part.reshape(2, rows, 2, pieces, width).transpose(0, 3, 1, 2, 4)
        found.append(part.reshape(2, pieces, rows, 2 * width))
    return found


PAIRS = (
    ("joined", "stream"),
    ("normed", "triple"),
    ("mixed", "branch"),
    ("second", "hidden"),
    ("active", "upstream"),
)


def summed(lefts, rights, vector_list):
    local_parts = []
    for left, right in PAIRS:
        rows = lax.all_gather(lefts[left], "batch", axis=0, tiled=True)
        columns = lax.all_to_all(rights[right], "batch", split_axis=1, concat_axis=0, tiled=True)
        local_parts.append(outer_sum(rows, columns))
    weight_parts = jax.tree.map(
        lambda part: part.astype(jnp.float32),
        lax.psum_scatter(shortened(tuple(local_parts)), "seq", scatter_dimension=0, tiled=True),
    )
    vectors = tuple(
        lax.psum_scatter(vector, ("seq", "batch"), scatter_dimension=0, tiled=True)
        for vector in vector_list
    )
    return weight_parts, vectors


def summed_by_kernel(lefts, rights, vector_list):
    triple_a, triple_b = by_core_wide(rights["triple"], ((0, 512, 1), (512, 384, 1)))
    pieces = dict(
        upstream=by_core(rights["upstream"]),
        hidden=by_core_wide(rights["hidden"], ((0, 384, 3),))[0],
        branch=by_core(rights["branch"]),
        triple_a=triple_a,
        triple_b=triple_b,
        stream=by_core(rights["stream"]),
    )
    vec = jnp.concatenate([vector.reshape(32, -1) for vector in vector_list], axis=1)
    vec = jnp.pad(vec, ((0, 0), (0, 512 - vec.shape[1]))).reshape(4, 2, 2, 2, 4, LANES)
    vec = vec.transpose(3, 2, 1, 0, 4, 5)
    found = weight_sums(lefts, pieces, vec)
    flat = found["vec"].reshape(-1)
    vectors, at = [], 0
    for vector in vector_list:
        width = vector.shape[0] // 32
        vectors.append(flat[at : at + width])
        at += width
    weight_parts = (
        found["skip"],
        found["attn"][:, :864],
        found["proj"],
        found["expand"],
        found["shrink"],
    )
    return weight_parts, tuple(vectors)


def on_device(
    tokens,
    skip_tokens,
    segment_ids,
    upstream,
    skip_weight,
    skip_bias,
    first_gain,
    first_shift,
    attn_weight,
    attn_bias,
    proj_weight,
    proj_bias,
    second_gain,
    second_shift,
    expand_weight,
    expand_bias,
    shrink_weight,
    shrink_bias,
):
    groups, shard_rows, features = tokens.shape
    head_dim = features // HEADS
    blocks = 4
    row_count = groups * shard_rows
    flat_tokens = tokens.reshape(row_count, features)
    flat_skip = skip_tokens.reshape(row_count, features)
    flat_upstream = upstream.reshape(row_count, features)
    joined = jnp.concatenate([flat_tokens, flat_skip], axis=1)
    stream = matmul(joined, skip_weight) + skip_bias.astype(jnp.float32)
    normed_full, first_back = jax.vjp(
        normalize, stream, first_gain.astype(jnp.float32), first_shift.astype(jnp.float32)
    )
    normed = normed_full.astype(jnp.bfloat16)
    triple = matmul(normed, attn_weight)
    bias_full = attn_bias.astype(jnp.float32)
    query_low = (triple[:, :features] + bias_full[:features]).astype(jnp.bfloat16)
    key_low = triple[:, features : 2 * features].astype(jnp.bfloat16)
    value_low = (triple[:, 2 * features :] + bias_full[features:]).astype(jnp.bfloat16)
    rim_rows = min(shard_rows, (ITEM_MOST + 6) // 8 * 8)
    stacked = jnp.stack([key_low, value_low]).reshape(2, groups, shard_rows, features)
    widened = padded(stacked, (("seq", 2),), rim_rows)
    position = lax.axis_index("seq")
    padded_ids = jnp.pad(segment_ids, ((0, 0), (rim_rows, rim_rows)), constant_values=-1)
    key_ids = lax.dynamic_slice_in_dim(
        padded_ids, position * shard_rows, shard_rows + 2 * rim_rows, 1
    )
    query_ids = lax.dynamic_slice_in_dim(segment_ids, position * shard_rows, shard_rows, 1)
    query_items = to_items(query_low.reshape(groups, shard_rows, features), blocks)
    key_items = to_items(widened[0], blocks)
    value_items = to_items(widened[1], blocks)
    query_id_items = jnp.repeat(query_ids, blocks, axis=0)
    key_id_items = jnp.repeat(key_ids, blocks, axis=0)
    mixed_items, lse_items = lax.map(
        partial(forward_block, head_dim=head_dim),
        (query_items, key_items, value_items, query_id_items, key_id_items),
    )
    mixed = from_items(mixed_items, blocks).reshape(row_count, features).astype(jnp.bfloat16)
    middle = stream + matmul(mixed, proj_weight) + proj_bias.astype(jnp.float32)
    second_full, second_back = jax.vjp(
        normalize, middle, second_gain.astype(jnp.float32), second_shift.astype(jnp.float32)
    )
    second = second_full.astype(jnp.bfloat16)
    hidden = matmul(second, expand_weight) + expand_bias.astype(jnp.float32)
    active_full, gelu_back = jax.vjp(partial(jax.nn.gelu, approximate=False), hidden)
    active = active_full.astype(jnp.bfloat16)
    result = (middle + matmul(active, shrink_weight) + shrink_bias.astype(jnp.float32)).astype(
        jnp.bfloat16
    )
    active_grad = matmul(flat_upstream, shrink_weight.T)
    shrink_bias_grad = jnp.sum(flat_upstream, axis=0, dtype=jnp.float32)
    hidden_grad = gelu_back(active_grad)[0].astype(jnp.bfloat16)
    expand_bias_grad = jnp.sum(hidden_grad, axis=0, dtype=jnp.float32)
    second_grad = matmul(hidden_grad, expand_weight.T)
    middle_norm_grad, second_gain_grad, second_shift_grad = second_back(second_grad)
    middle_grad = flat_upstream.astype(jnp.float32) + middle_norm_grad
    branch_grad = middle_grad.astype(jnp.bfloat16)
    proj_bias_grad = jnp.sum(branch_grad, axis=0, dtype=jnp.float32)
    mixed_grad = matmul(branch_grad, proj_weight.T).astype(jnp.bfloat16)
    grad_items = to_items(mixed_grad.reshape(groups, shard_rows, features), blocks)
    query_grads, key_grads, value_grads = lax.map(
        partial(backward_block, head_dim=head_dim),
        (query_items, key_items, value_items, query_id_items, key_id_items, grad_items, lse_items),
    )
    query_grad = from_items(query_grads, blocks).reshape(row_count, features).astype(jnp.bfloat16)
    window_grad = jnp.stack([from_items(key_grads, blocks), from_items(value_grads, blocks)])
    rim_grads = jnp.concatenate(
        [window_grad[:, :, :rim_rows], window_grad[:, :, shard_rows + rim_rows :]], axis=2
    )
    returned = padded(rim_grads.astype(jnp.bfloat16), (("seq", 2),), rim_rows).astype(
        rim_grads.dtype
    )
    owned = window_grad[:, :, rim_rows : rim_rows + shard_rows]
    owned = owned + jnp.pad(
        returned[:, :, :rim_rows], ((0, 0), (0, 0), (0, shard_rows - rim_rows), (0, 0))
    )
    owned = owned + jnp.pad(
        returned[:, :, 3 * rim_rows :], ((0, 0), (0, 0), (shard_rows - rim_rows, 0), (0, 0))
    )
    key_grad = owned[0].reshape(row_count, features).astype(jnp.bfloat16)
    value_grad = owned[1].reshape(row_count, features).astype(jnp.bfloat16)
    triple_grad = jnp.concatenate([query_grad, key_grad, value_grad], axis=1)
    attn_bias_grad = jnp.concatenate(
        [
            jnp.sum(query_grad, axis=0, dtype=jnp.float32),
            jnp.sum(value_grad, axis=0, dtype=jnp.float32),
        ]
    )
    normed_grad = matmul(triple_grad, attn_weight.T)
    stream_norm_grad, first_gain_grad, first_shift_grad = first_back(normed_grad)
    stream_grad = (middle_grad + stream_norm_grad).astype(jnp.bfloat16)
    skip_bias_grad = jnp.sum(stream_grad, axis=0, dtype=jnp.float32)
    skip_full = matmul(stream_grad, skip_weight.T)
    tokens_grad = skip_full[:, :features].astype(jnp.bfloat16)
    skip_grad = skip_full[:, features:].astype(jnp.bfloat16)
    vector_list = (
        skip_bias_grad,
        first_gain_grad,
        first_shift_grad,
        attn_bias_grad,
        proj_bias_grad,
        second_gain_grad,
        second_shift_grad,
        expand_bias_grad,
        shrink_bias_grad,
    )
    lefts = dict(active=active, second=second, mixed=mixed, normed=normed, joined=joined)
    rights = dict(
        upstream=flat_upstream,
        hidden=hidden_grad,
        branch=branch_grad,
        triple=triple_grad,
        stream=stream_grad,
    )
    if lax.axis_size("seq") == 8 and lax.axis_size("batch") == 4:
        weight_parts, vectors = summed_by_kernel(lefts, rights, vector_list)
    else:
        weight_parts, vectors = summed(lefts, rights, vector_list)
    return (
        result.reshape(groups, shard_rows, features),
        tokens_grad.reshape(groups, shard_rows, features),
        skip_grad.reshape(groups, shard_rows, features),
        weight_parts[0],
        vectors[0],
        vectors[1],
        vectors[2],
        weight_parts[1],
        vectors[3],
        weight_parts[2],
        vectors[4],
        vectors[5],
        vectors[6],
        weight_parts[3],
        vectors[7],
        weight_parts[4],
        vectors[8],
    )


def solution(mesh):
    in_specs = (
        P("batch", "seq", None),
        P("batch", "seq", None),
        P("batch", None),
        P("batch", "seq", None),
        P(),
        P(),
        P(),
        P(),
        P(),
        P(),
        P(),
        P(),
        P(),
        P(),
        P(),
        P(),
        P(),
        P(),
    )
    out_specs = (
        P("batch", "seq", None),
        P("batch", "seq", None),
        P("batch", "seq", None),
        P("seq", "batch"),
        P(("seq", "batch")),
        P(("seq", "batch")),
        P(("seq", "batch")),
        P("seq", "batch"),
        P(("seq", "batch")),
        P("seq", "batch"),
        P(("seq", "batch")),
        P(("seq", "batch")),
        P(("seq", "batch")),
        P("seq", "batch"),
        P(("seq", "batch")),
        P("seq", "batch"),
        P(("seq", "batch")),
    )
    return jax.shard_map(
        on_device, mesh=mesh, in_specs=in_specs, out_specs=out_specs, check_vma=False
    )
```

```python
import jax
import jax.numpy as jnp
from jax import lax
from jax.experimental import pallas as pl
from jax.experimental.pallas import tpu as pltpu
from jax.sharding import PartitionSpec as P

HEADS = 16
HEAD_DIM = 72
ITEM_MOST = 322
LANES = 128
MESH = pl.DeviceIdType.MESH
SCALE2 = HEAD_DIM**-0.5 * 1.4426950408889634


ROOT2 = 2.0**0.5


def dot(left, right):
    return jnp.dot(left, right, preferred_element_type=jnp.float32)


def dot_nt(left, right):
    return lax.dot_general(
        left, right, (((1,), (1,)), ((), ())), preferred_element_type=jnp.float32
    )


def dot_tn(left, right):
    return lax.dot_general(
        left, right, (((0,), (0,)), ((), ())), preferred_element_type=jnp.float32
    )


def whole():
    return pl.BlockSpec(memory_space=pltpu.VMEM)


def anywhere():
    return pl.BlockSpec(memory_space=pl.ANY)


def params():
    return pltpu.CompilerParams(vmem_limit_bytes=60 * 2**20)


def erf(value):
    v = jnp.clip(value, -3.832506856900711, 3.832506856900711)
    s = v * v
    top = 0.00022905065861350646
    for a in (0.0034082910107109506, 0.050955695062380861, 0.18520832239976145, 1.128379143519084):
        top = top * s + a
    low = -1.1791602954361697e-7
    for a in (0.000023547966471313185, 0.0010179625278914885, 0.014070470171167667):
        low = low * s + a
    low = (low * s + 0.11098505178285362) * s + 0.49746925110067538
    return v * top / (low * s + 1.0)


def row_norm(value):
    centred = value - jnp.mean(value, axis=-1, keepdims=True)
    scale = lax.rsqrt(jnp.mean(centred * centred, axis=-1, keepdims=True) + 1e-05)
    return centred * scale, scale


def norm_back(unit, scale, gain, cotangent):
    inner = cotangent * gain
    mean = jnp.mean(inner, axis=-1, keepdims=True)
    along = jnp.mean(inner * unit, axis=-1, keepdims=True)
    return scale * (inner - mean - unit * along)


def column_sum(value):
    return jnp.sum(value, axis=0, keepdims=True)


def stream_kernel(tok, skp, weight, bias, gain, shift, stream, normed, held, sems):
    copies = [
        pltpu.make_async_copy(weight.at[:, pl.ds(384 * n, 384)], held.at[n], sems.at[n])
        for n in range(3)
    ]
    for copy in copies:
        copy.start()
    features = tok.shape[1]
    for n, copy in enumerate(copies):
        copy.wait()
        at = slice(384 * n, 384 * n + 384)
        stream[:, at] = (
            dot(tok[...], held[n, :features])
            + dot(skp[...], held[n, features:])
            + bias[:, at].astype(jnp.float32)
        )
    unit, _ = row_norm(stream[...])
    normed[...] = (unit * gain[...].astype(jnp.float32) + shift[...].astype(jnp.float32)).astype(
        jnp.bfloat16
    )


def stream_norm(tok, skp, weight, bias, gain, shift):
    rows, features = tok.shape
    return pl.pallas_call(
        stream_kernel,
        out_shape=(
            jax.ShapeDtypeStruct((rows, features), jnp.float32),
            jax.ShapeDtypeStruct((rows, features), jnp.bfloat16),
        ),
        in_specs=[whole(), whole(), anywhere(), whole(), whole(), whole()],
        out_specs=(whole(), whole()),
        scratch_shapes=[
            pltpu.VMEM((3, 2 * features, 384), jnp.bfloat16),
            pltpu.SemaphoreType.DMA((3,)),
        ],
        compiler_params=params(),
        cost_estimate=pl.CostEstimate(
            flops=4 * rows * features * features, bytes_accessed=10**7, transcendentals=0
        ),
        name="stream_norm",
    )(tok, skp, weight, bias[None], gain[None], shift[None])


MARKS = (HEAD_DIM, HEAD_DIM + 16, HEAD_DIM + 32)


def lanes_of(shape):
    return lax.broadcasted_iota(jnp.int32, shape, len(shape) - 1)


def marked(lane):
    return (lane == MARKS[0]) | (lane == MARKS[1]) | (lane == MARKS[2])


def head_tile(value, h, ones):
    rows = value.shape[0]
    lane = lanes_of((rows, LANES - HEAD_DIM)) + HEAD_DIM
    rest = jnp.where(marked(lane) & ones, 1.0, 0.0).astype(value.dtype)
    return jnp.concatenate([value[:, HEAD_DIM * h : HEAD_DIM * (h + 1)], rest], axis=1)


def project(rows_ref, weight_ref, bias, part, store):
    features = rows_ref.shape[1]
    value = dot(rows_ref[...], weight_ref[...])
    if part != 1:
        at = 0 if part == 0 else features
        value = value + bias[:, at : at + features].astype(jnp.float32)
    value = value.astype(jnp.bfloat16)
    for h in range(HEADS):
        store(part, h, head_tile(value, h, part > 0))


def project_kernel(normed, weight, bias, out, held, sems):
    features = normed.shape[1]
    copies = [
        pltpu.make_async_copy(weight.at[:, pl.ds(features * p, features)], held.at[p], sems.at[p])
        for p in range(3)
    ]
    for copy in copies:
        copy.start()

    def store(part, h, value):
        out[part, h] = value

    for p, copy in enumerate(copies):
        copy.wait()
        project(normed, held.at[p], bias, p, store)


def own_heads(normed, weight, bias):
    rows, features = normed.shape
    return pl.pallas_call(
        project_kernel,
        out_shape=jax.ShapeDtypeStruct((3, HEADS, rows, LANES), jnp.bfloat16),
        in_specs=[whole(), anywhere(), whole()],
        out_specs=whole(),
        scratch_shapes=[
            pltpu.VMEM((3, features, features), jnp.bfloat16),
            pltpu.SemaphoreType.DMA((3,)),
        ],
        compiler_params=params(),
        cost_estimate=pl.CostEstimate(
            flops=6 * rows * features * features, bytes_accessed=2 * 10**7, transcendentals=0
        ),
        name="own_heads",
    )(normed, weight, bias[None])


HIDE = -1e30


def attend_kernel(own, before, after, weight, bias, id_col, id_row, wins, mixed, lse, *scratch):
    window, halo, held, hide, gathered, sems, out_sems = scratch
    rim, features = before.shape
    rows = own.shape[2]
    span = 3 * rows
    copies = [
        pltpu.make_async_copy(weight.at[:, pl.ds(features * p, features)], held.at[p], sems.at[p])
        for p in range(3)
    ]
    copies.append(pltpu.make_async_copy(own, window.at[:, :, pl.ds(rows, rows)], sems.at[3]))
    for copy in copies:
        copy.start()
    pad = rows - rim
    window[:, :, 0:pad] = jnp.zeros((3, HEADS, pad, LANES), jnp.bfloat16)
    window[:, :, span - pad : span] = jnp.zeros((3, HEADS, pad, LANES), jnp.bfloat16)
    halo[0:rim] = before[...]
    halo[rim:] = after[...]

    def store(part, h, value):
        window[part, h, pad:rows] = value[:rim]
        window[part, h, 2 * rows : 2 * rows + rim] = value[rim:]

    for p in (1, 2, 0):
        copies[p].wait()
        project(halo, held.at[p], bias, p, store)
    copies[3].wait()
    out_copies = [
        pltpu.make_async_copy(window.at[p], wins.at[p], out_sems.at[p]) for p in range(3)
    ]
    for copy in out_copies:
        copy.start()
    blocks = rows // LANES
    reach = span - (blocks - 1) * LANES
    for i in range(blocks):
        same = id_col[rows + i * LANES : rows + (i + 1) * LANES] == (
            id_row[:, i * LANES : i * LANES + reach]
        )
        hide[i] = jnp.where(same, 0.0, HIDE)
    lse[...] = jnp.zeros_like(lse)

    def body(h, carry):
        for i in range(blocks):
            keys = pl.ds(i * LANES, reach)
            scores = dot_nt(
                window[0, h, rows + i * LANES : rows + (i + 1) * LANES], window[1, h, keys]
            )
            scores = scores * SCALE2 + hide[i]
            highest = jnp.max(scores, axis=-1, keepdims=True)
            raised = jnp.exp2(scores - highest).astype(jnp.bfloat16)
            total = dot(raised, window[2, h, keys])
            denominator = total[:, HEAD_DIM : HEAD_DIM + 1]
            gathered[h, i * LANES : (i + 1) * LANES] = total / denominator
            value = highest + jnp.log2(denominator)
            at = slice(i * LANES, (i + 1) * LANES)
            lse[at] = jnp.where(lanes_of((LANES, LANES)) == h, value, lse[at])
        return carry

    lax.fori_loop(0, HEADS, body, 0)
    for h in range(HEADS):
        mixed[:, HEAD_DIM * h : HEAD_DIM * (h + 1)] = gathered[h, :, :HEAD_DIM].astype(jnp.bfloat16)
    for copy in out_copies:
        copy.wait()


def attend(own, before, after, weight, bias, id_col, id_row):
    rim, features = before.shape
    rows = own.shape[2]
    span = 3 * rows
    return pl.pallas_call(
        attend_kernel,
        out_shape=(
            jax.ShapeDtypeStruct((3, HEADS, span, LANES), jnp.bfloat16),
            jax.ShapeDtypeStruct((rows, features), jnp.bfloat16),
            jax.ShapeDtypeStruct((rows, LANES), jnp.float32),
        ),
        in_specs=[anywhere(), whole(), whole(), anywhere(), whole(), whole(), whole()],
        out_specs=(anywhere(), whole(), whole()),
        scratch_shapes=[
            pltpu.VMEM((3, HEADS, span, LANES), jnp.bfloat16),
            pltpu.VMEM((2 * rim, features), jnp.bfloat16),
            pltpu.VMEM((3, features, features), jnp.bfloat16),
            pltpu.VMEM((rows // LANES, LANES, span - rows + LANES), jnp.float32),
            pltpu.VMEM((HEADS, rows, LANES), jnp.float32),
            pltpu.SemaphoreType.DMA((4,)),
            pltpu.SemaphoreType.DMA((3,)),
        ],
        compiler_params=params(),
        name="attend",
    )(own, before, after, weight, bias[None], id_col, id_row)


def by_core_store(ref, value):
    rows = value.shape[0]
    blank = jnp.zeros((rows, LANES - 32), value.dtype)
    for b in range(4):
        x, c = b // 2, b % 2
        ref[c, 0, :, 256 * x : 256 * x + 256] = value[:, 288 * b : 288 * b + 256]
        ref[c, 0, :, 512 + LANES * x : 640 + LANES * x] = jnp.concatenate(
            [value[:, 288 * b + 256 : 288 * b + 288], blank], axis=1
        )


def split3(value):
    first = value.astype(jnp.bfloat16)
    rest = value - first.astype(jnp.float32)
    second = rest.astype(jnp.bfloat16)
    return first, second, (rest - second.astype(jnp.float32)).astype(jnp.bfloat16)


def layer_kernel(
    stream, mixed, lse, upstream, proj, proj_bias, gain, shift, expand, expand_bias, shrink,
    shrink_bias, result, active, hidden_by_core, second, branch, branch_by_core, up_by_core,
    middle_grad, mixed_grad, hidden_sum, sums, middle, total, second_grad,
):
    step, steps = pl.program_id(0), pl.num_programs(0)
    low = jnp.bfloat16

    @pl.when(step == 0)
    def _():
        middle[...] = (
            stream[...] + dot(mixed[...], proj[...]) + proj_bias[...].astype(jnp.float32)
        )
        unit, _ = row_norm(middle[...])
        second[...] = (
            unit * gain[...].astype(jnp.float32) + shift[...].astype(jnp.float32)
        ).astype(low)
        total[...] = middle[...] + shrink_bias[...].astype(jnp.float32)
        second_grad[...] = jnp.zeros_like(second_grad)
        by_core_store(up_by_core, upstream[...])

    hidden = dot(second[...], expand[...]) + expand_bias[...].astype(jnp.float32)
    active_grad = dot_nt(upstream[...], shrink[...])
    cdf = 0.5 + 0.5 * erf(hidden * (1.0 / ROOT2))
    density = jnp.exp(-0.5 * hidden * hidden) * 0.3989422804014327
    raised = (hidden * cdf).astype(low)
    active[...] = raised
    hidden_grad = (active_grad * (cdf + hidden * density)).astype(low)
    for j in range(3):
        hidden_by_core[0, j] = hidden_grad[:, 384 * j : 384 * (j + 1)]
    hidden_sum[...] = column_sum(hidden_grad.astype(jnp.float32))
    total[...] += dot(raised, shrink[...])
    second_grad[...] += dot_nt(hidden_grad, expand[...])

    @pl.when(step == steps - 1)
    def _():
        result[...] = total[...].astype(low)
        unit, scale = row_norm(middle[...])
        cotangent = second_grad[...]
        above = upstream[...].astype(jnp.float32)
        grad = above + norm_back(unit, scale, gain[...].astype(jnp.float32), cotangent)
        middle_grad[...] = grad
        branched = grad.astype(low)
        branch[...] = branched
        by_core_store(branch_by_core, branched)
        sums[0:1] = column_sum(branched.astype(jnp.float32))
        sums[1:2] = column_sum(cotangent * unit)
        sums[2:3] = column_sum(cotangent)
        sums[3:4] = column_sum(above)
        back = dot_nt(branched, proj[...]).astype(low)
        features = back.shape[1]
        mixed_grad[:, :features] = back
        products = back.astype(jnp.float32) * mixed[...].astype(jnp.float32)
        shape = (features, LANES)
        member = lax.broadcasted_iota(jnp.int32, shape, 0) // HEAD_DIM == lanes_of(shape)
        member = jnp.where(member, 1.0, 0.0).astype(low)
        high = products.astype(low)
        inner = dot(high, member) + dot((products - high.astype(jnp.float32)).astype(low), member)
        pieces = [part[:, :HEADS] for part in split3(lse[...] * (-1.0 / SCALE2)) + split3(-inner)]
        blank = jnp.zeros((back.shape[0], LANES - 6 * HEADS), low)
        mixed_grad[:, features:] = jnp.concatenate(pieces + [blank], axis=1)


def layer(stream, mixed, lse, upstream, weights):
    proj, proj_bias, gain, shift, expand, expand_bias, shrink, shrink_bias = weights
    rows, features = stream.shape
    hidden = expand.shape[1]
    wide = hidden // 4
    low = jnp.bfloat16

    def held(shape):
        return pl.BlockSpec(shape, lambda t: (0,) * len(shape))

    narrow = (rows, features)
    vector = (1, features)
    split = (2, 1, rows, 768)
    return pl.pallas_call(
        layer_kernel,
        grid=(4,),
        in_specs=[
            held(narrow), held(narrow), held((rows, LANES)), held(narrow),
            held((features, features)), held(vector), held(vector), held(vector),
            pl.BlockSpec((features, wide), lambda t: (0, t)),
            pl.BlockSpec((1, wide), lambda t: (0, t)),
            pl.BlockSpec((wide, features), lambda t: (t, 0)),
            held(vector),
        ],
        out_specs=(
            held(narrow),
            pl.BlockSpec((rows, wide), lambda t: (0, t)),
            pl.BlockSpec((1, 3, rows, 384), lambda t: (t % 2, 0, 0, t // 2)),
            held(narrow), held(narrow), held(split), held(split), held(narrow),
            held((rows, features + LANES)),
            pl.BlockSpec((1, wide), lambda t: (0, t)),
            held((8, features)),
        ),
        out_shape=(
            jax.ShapeDtypeStruct(narrow, low),
            jax.ShapeDtypeStruct((rows, hidden), low),
            jax.ShapeDtypeStruct((2, 3, rows, 768), low),
            jax.ShapeDtypeStruct(narrow, low),
            jax.ShapeDtypeStruct(narrow, low),
            jax.ShapeDtypeStruct(split, low),
            jax.ShapeDtypeStruct(split, low),
            jax.ShapeDtypeStruct(narrow, jnp.float32),
            jax.ShapeDtypeStruct((rows, features + LANES), low),
            jax.ShapeDtypeStruct((1, hidden), jnp.float32),
            jax.ShapeDtypeStruct((8, features), jnp.float32),
        ),
        scratch_shapes=[pltpu.VMEM(narrow, jnp.float32)] * 3,
        compiler_params=params(),
        name="layer",
    )(
        stream, mixed, lse, upstream, proj, proj_bias[None], gain[None], shift[None], expand,
        expand_bias[None], shrink, shrink_bias[None],
    )


def back_masks(id_col, id_row, own_hide, rim_hide, rows):
    blocks = rows // LANES
    reach = own_hide.shape[2]

    def hidden(first, keys, width):
        same = id_col[first : first + LANES] == id_row[:, keys : keys + width]
        return jnp.where(same, 0.0, HIDE)

    for i in range(blocks):
        own_hide[i] = hidden(rows + i * LANES, i * LANES, reach)
    for w in range(blocks):
        rim_hide[w] = hidden(w * LANES, rows, rows)
        rim_hide[blocks + w] = hidden(2 * rows + w * LANES, rows, rows)


def with_stats(value, stats, shift):
    lane = lanes_of(value.shape)
    moved = pltpu.roll(stats, shift, 1)
    return jnp.where(marked(lane), moved, value.astype(jnp.float32)).astype(value.dtype)


def back_head(h, queries, keys, values, grads, stats, own_hide, rim_hide, probs, scored, store):
    span = queries.shape[0]
    rows = span // 3
    blocks = rows // LANES
    reach = span - rows + LANES
    low = jnp.bfloat16
    queries[...] = with_stats(queries[...], stats[...], MARKS[0] - h)
    turn = MARKS[0] - 3 * HEADS - h
    grads[...] = with_stats(grads[...], stats[...], jnp.where(turn < 0, turn + LANES, turn))

    def pair(q_at, k_at, width, hide):
        q_rows, k_rows = pl.ds(q_at, LANES), pl.ds(k_at, width)
        exponent = dot_nt(queries[q_rows], keys[k_rows]) * SCALE2 + hide
        weight = jnp.exp2(exponent)
        scored = weight * dot_nt(grads[q_rows], values[k_rows])
        return weight.astype(low), scored.astype(low)

    query_grad = []
    for i in range(blocks):
        at = rows + i * LANES
        weight, score = pair(at, i * LANES, reach, own_hide[i])
        query_grad.append(dot(score, keys[i * LANES : i * LANES + reach]))
        mine = slice(rows - i * LANES, 2 * rows - i * LANES)
        probs[at : at + LANES] = weight[:, mine]
        scored[at : at + LANES] = score[:, mine]
    for w in range(blocks):
        for at, first, width in (
            (w * LANES, 0, (w + 1) * LANES),
            (2 * rows + w * LANES, w * LANES, rows - w * LANES),
        ):
            hide = rim_hide[w if at < rows else blocks + w]
            weight, score = pair(at, rows + first, width, hide[:, first : first + width])
            probs[at : at + LANES, first : first + width] = weight
            scored[at : at + LANES, first : first + width] = score
    factor = HEAD_DIM**-0.5
    for i in range(blocks):
        store(0, i * LANES, LANES, query_grad[i] * factor)
    store(1, 0, rows, dot_tn(scored[...], queries[...]) * factor)
    store(2, 0, rows, dot_tn(probs[...], grads[...]))


def heads_apart(row_ref, out):
    value = row_ref[...]
    for h in range(HEADS):
        out[h] = head_tile(value[:, : HEADS * HEAD_DIM], h, False)


def triple_store(apart, triple, triple_a, triple_b):
    features = HEADS * HEAD_DIM
    rows = apart.shape[2]
    for p in range(3):
        for h in range(HEADS):
            at = features * p + HEAD_DIM * h
            triple[:, at : at + HEAD_DIM] = apart[p, h, :, :HEAD_DIM]
    for b in range(4):
        x, c = b // 2, b % 2
        value = triple[:, 864 * b : 864 * (b + 1)]
        triple_a[c, 0, :, 512 * x : 512 * (x + 1)] = value[:, :512]
        rest = jnp.concatenate([value[:, 512:], jnp.zeros((rows, 32), value.dtype)], axis=1)
        triple_b[c, 0, :, 384 * x : 384 * (x + 1)] = rest


def attend_back_kernel(
    wins, grads_in, stats, id_col, id_row, triple, triple_a, triple_b, sums,
    window, grads, own_hide, rim_hide, probs, scored, apart, sems,
):
    span = window.shape[2]
    rows = span // 3
    copy = pltpu.make_async_copy(wins, window, sems.at[0])
    copy.start()
    back_masks(id_col, id_row, own_hide, rim_hide, rows)
    probs[...] = jnp.zeros_like(probs)
    scored[...] = jnp.zeros_like(scored)
    heads_apart(grads_in, grads)
    copy.wait()

    def body(h, carry):
        def store(part, first, count, value):
            apart[part, h, pl.ds(first, count)] = value.astype(jnp.bfloat16)

        back_head(
            h, window.at[0, h], window.at[1, h], window.at[2, h], grads.at[h], stats, own_hide,
            rim_hide, probs, scored, store,
        )
        return carry

    lax.fori_loop(0, HEADS, body, 0)
    triple_store(apart, triple, triple_a, triple_b)
    sums[...] = column_sum(triple[...].astype(jnp.float32))


def attend_back(wins, grads_in, stats, id_col, id_row):
    span = wins.shape[2]
    rows = span // 3
    features = HEADS * HEAD_DIM
    low = jnp.bfloat16
    return pl.pallas_call(
        attend_back_kernel,
        out_shape=(
            jax.ShapeDtypeStruct((rows, 3 * features), low),
            jax.ShapeDtypeStruct((2, 1, rows, 1024), low),
            jax.ShapeDtypeStruct((2, 1, rows, 768), low),
            jax.ShapeDtypeStruct((1, 3 * features), jnp.float32),
        ),
        in_specs=[anywhere(), whole(), whole(), whole(), whole()],
        out_specs=(whole(), whole(), whole(), whole()),
        scratch_shapes=[
            pltpu.VMEM((3, HEADS, span, LANES), low),
            pltpu.VMEM((HEADS, span, LANES), low),
            pltpu.VMEM((rows // LANES, LANES, span - rows + LANES), jnp.float32),
            pltpu.VMEM((2 * rows // LANES, LANES, rows), jnp.float32),
            pltpu.VMEM((span, rows), low),
            pltpu.VMEM((span, rows), low),
            pltpu.VMEM((3, HEADS, rows, LANES), low),
            pltpu.SemaphoreType.DMA((1,)),
        ],
        compiler_params=params(),
        name="attend_back",
    )(wins, grads_in, stats, id_col, id_row)


def stream_back_kernel(
    triple, weight, stream, middle_grad, gain, skip_weight, tok_grad, skip_grad, stream_grad,
    by_core, sums, held, held_skip, grad, sems,
):
    features = stream.shape[1]
    low = jnp.bfloat16
    copies = [
        pltpu.make_async_copy(weight.at[:, pl.ds(features * p, features)], held.at[p], sems.at[p])
        for p in range(3)
    ]
    copies += [
        pltpu.make_async_copy(
            skip_weight.at[pl.ds(features * p, features)], held_skip.at[p], sems.at[3 + p]
        )
        for p in range(2)
    ]
    for copy in copies:
        copy.start()
    unit, scale = row_norm(stream[...])
    for p in range(3):
        copies[p].wait()
        part = dot_nt(triple[:, features * p : features * (p + 1)], held[p])
        if p == 0:
            grad[...] = part
        else:
            grad[...] += part
    cotangent = grad[...]
    sums[0:1] = column_sum(cotangent * unit)
    sums[1:2] = column_sum(cotangent)
    whole_grad = middle_grad[...] + norm_back(
        unit, scale, gain[...].astype(jnp.float32), cotangent
    )
    rounded = whole_grad.astype(low)
    stream_grad[...] = rounded
    by_core_store(by_core, rounded)
    sums[2:3] = column_sum(rounded.astype(jnp.float32))
    for p, out in enumerate((tok_grad, skip_grad)):
        copies[3 + p].wait()
        out[...] = dot_nt(rounded, held_skip[p]).astype(low)


def stream_back(triple, weight, stream, middle_grad, gain, skip_weight):
    rows, features = stream.shape
    low = jnp.bfloat16
    return pl.pallas_call(
        stream_back_kernel,
        out_shape=(
            jax.ShapeDtypeStruct((rows, features), low),
            jax.ShapeDtypeStruct((rows, features), low),
            jax.ShapeDtypeStruct((rows, features), low),
            jax.ShapeDtypeStruct((2, 1, rows, 768), low),
            jax.ShapeDtypeStruct((8, features), jnp.float32),
        ),
        in_specs=[whole(), anywhere(), whole(), whole(), whole(), anywhere()],
        out_specs=(whole(), whole(), whole(), whole(), whole()),
        scratch_shapes=[
            pltpu.VMEM((3, features, features), low),
            pltpu.VMEM((2, features, features), low),
            pltpu.VMEM((rows, features), jnp.float32),
            pltpu.SemaphoreType.DMA((5,)),
        ],
        compiler_params=params(),
        name="stream_back",
    )(triple, weight, stream, middle_grad, gain[None], skip_weight)


class Unit:
    def __init__(self, left, left_at, right, right_at, tiles, rows, blocks, out, out_at):
        self.left, self.left_at = left, left_at
        self.right, self.right_at = right, right_at
        self.tiles = tiles
        self.rows = rows
        self.blocks = blocks
        self.places = 1 + max(block[3] for block in blocks)
        self.out, self.out_at = out, out_at

    def shape(self, *lead):
        if self.tiles:
            return (*lead, self.rows, LANES)
        return (*lead, self.rows * 7 // 3, LANES)

    @property
    def x_size(self):
        return 2 * (self.tiles or 1)

    @property
    def part_shape(self):
        return self.shape(2, self.x_size, 2, self.places)

    @property
    def first_shapes(self):
        half = self.x_size // 2
        if self.tiles:
            return (self.shape(half, 2, self.places), self.shape(2 * half, self.places))
        return (self.shape(2, self.places), self.shape(2, self.places))

    @property
    def second_shape(self):
        if self.tiles:
            return self.shape(self.tiles, self.places)
        return self.shape(self.places)

    @property
    def chain_shape(self):
        return self.shape(self.tiles) if self.tiles else self.shape()

    def view(self, ref, order, x, y, place=None):
        if x is None:
            x_at = slice(None)
        elif self.tiles:
            x_at = pl.ds(x * self.tiles, self.tiles)
        else:
            x_at = x
        y_at = slice(None) if y is None else y
        if place is None:
            return ref.at[order, x_at, y_at]
        return ref.at[order, x_at, y_at, place]

    def chains(self):
        return sorted({(order, place, z) for _, order, _, place, z in self.blocks})


def make_units():
    order_of = (0, 1, 1, 0)
    place_of = (0, 0, 1, 1)
    quarter = [
        ((2 * z + y) * 144, order_of[z], y, place_of[z], z) for z in range(4) for y in range(2)
    ]
    units = []
    for z in (0, 3, 1, 2):
        blocks = [(y * 576 + h * 288, h, y, 0, z) for y in range(2) for h in range(2)]
        units.append(Unit("active", z * 1152, "upstream", 0, 0, 288, blocks, "shrink", z))
    for j in range(3):
        units.append(Unit("second", 0, "hidden", j, 3, 144, quarter, "expand", j * 3))
    units.append(Unit("mixed", 0, "branch", 0, 0, 144, quarter, "proj", 0))
    units.append(Unit("normed", 0, "triple_a", 0, 4, 144, quarter, "attn", 0))
    units.append(Unit("normed", 0, "triple_b", 0, 3, 144, quarter, "attn", 4))
    for k in range(2):
        blocks = [(h * 576 + y * 288, h, y, 0, 2 * k + h) for h in range(2) for y in range(2)]
        units.append(Unit("joined", k * 1152, "stream", 0, 0, 288, blocks, "skip", k))
    return units


LEFTS = ("active", "second", "mixed", "normed", "joined")
RIGHTS = ("upstream", "hidden", "branch", "triple_a", "triple_b", "stream")
GRADS = ("shrink", "expand", "proj", "attn", "skip")
GRAD_SHAPES = ((576, 288), (144, 1152), (144, 288), (144, 896), (288, 288))


def add_into(target, other):
    target[...] = (target[...].astype(jnp.float32) + other[...].astype(jnp.float32)).astype(
        target.dtype
    )


class Links:
    def __init__(self):
        self.ids = {}

    def id(self, key):
        return self.ids.setdefault(key, len(self.ids))


def sum_kernel(units, names, *refs):
    r = dict(zip(names, refs))
    seq, batch = lax.axis_index("seq"), lax.axis_index("batch")
    z, y = seq // 2, seq % 2
    x, c = batch // 2, batch % 2
    partner = (seq, 2 * x + (1 - c))
    x_side = (seq, 2 * (1 - x) + c)
    y_side = (2 * z + (1 - y), batch)
    above = (2 * jnp.minimum(z + 1, 3) + y, batch)
    below = (2 * jnp.maximum(z - 1, 0) + y, batch)
    links = Links()

    barrier = pltpu.get_barrier_semaphore()
    for device in (partner, x_side, y_side):
        pl.semaphore_signal(barrier, 1, device_id=device, device_id_type=MESH)

    @pl.when(z < 3)
    def _():
        pl.semaphore_signal(barrier, 1, device_id=above, device_id_type=MESH)

    @pl.when(z > 0)
    def _():
        pl.semaphore_signal(barrier, 1, device_id=below, device_id_type=MESH)

    pl.semaphore_wait(barrier, 3 + (z < 3).astype(jnp.int32) + (z > 0).astype(jnp.int32))

    def remote(key, src, dst, device):
        i = links.id(key)
        return pltpu.make_async_remote_copy(
            src_ref=src,
            dst_ref=dst,
            send_sem=r["sent"].at[i],
            recv_sem=r["came"].at[i],
            device_id=device,
            device_id_type=MESH,
        )

    swaps = {}
    for unit in units:
        key = ("left", unit.left, unit.left_at)
        if key not in swaps:
            at = pl.ds(unit.left_at, 1152)
            swaps[key] = remote(
                key, r[unit.left].at[:, at], r["far_" + unit.left].at[:, at], partner
            )
        key = ("right", unit.right, unit.right_at)
        if key not in swaps:
            swaps[key] = remote(
                key,
                r[unit.right].at[1 - c, unit.right_at],
                r["far_" + unit.right].at[unit.right_at],
                partner,
            )
    for copy in swaps.values():
        copy.start()

    slots = {}
    turns = {"left": 0, "right": 0}

    def load(unit):
        started = []
        for side, name, at in (
            ("left", unit.left, unit.left_at),
            ("right", unit.right, unit.right_at),
        ):
            key = (side, name, at)
            if key in slots:
                continue
            slot = turns[side] % 2
            turns[side] += 1
            slots[key] = slot
            swaps[key].wait_recv()
            if side == "left":
                cols = pl.ds(at, 1152)
                near, far = r[name].at[:, cols], r["far_" + name].at[:, cols]
                hold = r["lefts"].at[slot]
            else:
                near, far = r[name].at[c, at], r["far_" + name].at[at]
                hold = r["rights"].at[slot, :, pl.ds(0, near.shape[-1])]
            for half, src in ((0, near), (1, far)):
                copy = pltpu.make_async_copy(
                    src, hold.at[pl.ds(384 * half, 384)], r[side + "_sem"].at[slot, half]
                )
                copy.start()
                started.append(copy)
        return started

    def compute(u):
        unit = units[u]
        part = r["part", u]
        left = r["lefts"].at[slots["left", unit.left, unit.left_at]]
        right = r["rights"].at[slots["right", unit.right, unit.right_at]]

        def product(n):
            cols = pl.ds(pl.multiple_of(n * 256, 256), 256)
            return lax.dot_general(
                left[...],
                right[:, cols],
                (((0,), (0,)), ((), ())),
                preferred_element_type=jnp.float32,
            )

        rows = unit.rows
        if unit.tiles:

            def body(n, carry):
                tile = product(n).astype(jnp.bfloat16)
                for first, order, y_at, place, _ in unit.blocks:
                    for i in range(2):
                        part[order, 2 * n + i, y_at, place] = tile[
                            first : first + rows, i * LANES : (i + 1) * LANES
                        ]
                return carry

            lax.fori_loop(0, unit.tiles, body, 0)
            return

        def body(n, carry):
            tile = product(n).astype(jnp.bfloat16)
            for first, order, y_at, place, _ in unit.blocks:
                for i in range(2):
                    part[order, n, y_at, place, pl.ds(i * rows, rows)] = tile[
                        first : first + rows, i * LANES : (i + 1) * LANES
                    ]
            return carry

        lax.fori_loop(0, 2, body, 0)
        tile = product(2)
        third = rows // 3
        for first, order, y_at, place, _ in unit.blocks:
            for x_at in range(2):
                pieces = [
                    tile[first + s * third : first + (s + 1) * third, x_at * LANES :][:, :32]
                    for s in range(3)
                ]
                packed = jnp.concatenate(pieces + [jnp.zeros_like(pieces[0])], axis=1)
                part[order, x_at, y_at, place, pl.ds(2 * rows, third)] = packed.astype(jnp.bfloat16)

    def first_copies(u):
        unit, part = units[u], r["part", u]
        return (
            remote(("first", u, 0), unit.view(part, 0, 1 - x, None), r["first", u, 0], x_side),
            remote(("first", u, 1), unit.view(part, 1, None, 1 - y), r["first", u, 1], y_side),
        )

    def second_copies(u):
        unit, part = units[u], r["part", u]
        return (
            remote(("second", u, 0), unit.view(part, 0, x, 1 - y), r["second", u].at[0], y_side),
            remote(("second", u, 1), unit.view(part, 1, 1 - x, y), r["second", u].at[1], x_side),
        )

    def first_stage(u):
        compute(u)
        for copy in first_copies(u):
            copy.start()

    def second_stage(u):
        unit, part = units[u], r["part", u]
        keeps = (unit.view(part, 0, x, None), unit.view(part, 1, None, y))
        for order, (copy, send) in enumerate(zip(first_copies(u), second_copies(u))):
            copy.wait_recv()
            add_into(keeps[order], r["first", u, order])
            send.start()

    def third_stage(u):
        unit, part = units[u], r["part", u]
        for order, copy in enumerate(second_copies(u)):
            copy.wait_recv()
            add_into(unit.view(part, order, x, y), r["second", u].at[order])

    def chain_copy(key, src, dsts, up):
        return remote((key, up), src, dsts[up], above if up else below)

    class Chain:
        def __init__(self, key, src, up_ref, down_ref, z_at):
            self.key, self.src, self.z_at = key, src, z_at
            self.refs = {True: up_ref, False: down_ref}

        def copy(self, up):
            return remote((self.key, up), self.src, self.refs[up], above if up else below)

        def hop(self, step):
            for up, me in ((True, step - 1), (False, 4 - step)):
                if (self.z_at > me) if up else (self.z_at < me):

                    @pl.when(z == me)
                    def _():
                        if step > 1:
                            self.copy(up).wait_recv()
                            add_into(self.src, self.refs[up])
                        self.copy(up).start()

        def total(self):
            value = self.src[...].astype(jnp.float32)
            for up, have in ((True, self.z_at > 0), (False, self.z_at < 3)):
                if have:
                    self.copy(up).wait_recv()
                    value = value + self.refs[up][...].astype(jnp.float32)
            return value

        def drain(self):
            for up, some in ((True, self.z_at > 0), (False, self.z_at < 3)):
                if some:

                    @pl.when((z < self.z_at) if up else (z > self.z_at))
                    def _():
                        self.copy(up).wait_send()

    def unit_chains(u):
        unit, part = units[u], r["part", u]
        found = []
        for order, place, z_at in unit.chains():
            src = unit.view(part, order, x, y, place)
            up = r["up", u, order, place] if z_at > 0 else None
            down = r["down", u, order, place] if z_at < 3 else None
            found.append((order, place, Chain(("chain", u, order, place), src, up, down, z_at)))
        return found

    def hop_stage(u, step):
        for _, _, chain in unit_chains(u):
            chain.hop(step)

    def last_stage(u):
        unit = units[u]
        out = r["out_" + unit.out]
        rows = unit.rows
        for order, place, chain in unit_chains(u):

            @pl.when(z == chain.z_at)
            def _():
                value = chain.total()
                if unit.tiles:
                    for t in range(unit.tiles):
                        at = (unit.out_at + t) * LANES
                        out[:, at : at + LANES] = value[t]
                    return
                base = order * rows if rows == 288 and unit.out == "shrink" else 0
                third = rows // 3
                for i in range(2):
                    out[base : base + rows, i * LANES : (i + 1) * LANES] = value[
                        i * rows : (i + 1) * rows
                    ]
                for s in range(3):
                    out[base + s * third : base + (s + 1) * third, 256:288] = value[
                        2 * rows : 2 * rows + third, s * 32 : (s + 1) * 32
                    ]

    vec = r["vec"]

    def vec_copies():
        return (
            remote("vec_core", vec.at[1 - c], r["vec_core"], partner),
            remote("vec_x", vec.at[c, 1 - x], r["vec_x"], x_side),
            remote("vec_y", vec.at[c, x, 1 - y], r["vec_y"], y_side),
        )

    vec_keeps = (vec.at[c], vec.at[c, x], vec.at[c, x, y])
    vec_lands = (r["vec_core"], r["vec_x"], r["vec_y"])
    vec_chains = [
        Chain(("vec", b), vec.at[c, x, y, b], r["vec_up"].at[b], r["vec_down"].at[b], b)
        for b in range(4)
    ]

    def vec_stage(step):
        if step < 3:
            if step > 0:
                vec_copies()[step - 1].wait_recv()
                add_into(vec_keeps[step - 1], vec_lands[step - 1])
            vec_copies()[step].start()
        elif step < 6:
            if step == 3:
                vec_copies()[2].wait_recv()
                add_into(vec_keeps[2], vec_lands[2])
            for chain in vec_chains:
                chain.hop(step - 2)
        elif step == 6:
            for chain in vec_chains:

                @pl.when(z == chain.z_at)
                def _():
                    r["out_vec"][...] = chain.total()

    count = len(units)
    started = load(units[0])
    for tick in range(count + 6):
        if tick < count:
            for copy in started:
                copy.wait()
            if tick + 1 < count:
                started = load(units[tick + 1])
            first_stage(tick)
        vec_stage(tick)
        if 0 <= tick - 1 < count:
            second_stage(tick - 1)
        if 0 <= tick - 2 < count:
            third_stage(tick - 2)
            hop_stage(tick - 2, 1)
        if 0 <= tick - 3 < count:
            hop_stage(tick - 3, 2)
        if 0 <= tick - 4 < count:
            hop_stage(tick - 4, 3)
        if 0 <= tick - 5 < count:
            last_stage(tick - 5)
    for copy in swaps.values():
        copy.wait_send()
    for u in range(count):
        for copy in first_copies(u) + second_copies(u):
            copy.wait_send()
        for _, _, chain in unit_chains(u):
            chain.drain()
    for copy in vec_copies():
        copy.wait_send()
    for chain in vec_chains:
        chain.drain()


def weight_sums(lefts, rights, vec):
    units = make_units()
    low = jnp.bfloat16
    names, in_specs, operands = [], [], []
    for name, value in [*lefts.items(), *rights.items()]:
        names.append(name)
        in_specs.append(pl.BlockSpec(memory_space=pl.ANY))
        operands.append(value)
    names.append("vec_in")
    in_specs.append(pl.BlockSpec(memory_space=pltpu.VMEM))
    operands.append(vec)
    out_shape, out_specs = [], []
    for name, shape in zip(GRADS, GRAD_SHAPES):
        names.append("out_" + name)
        out_shape.append(jax.ShapeDtypeStruct(shape, jnp.float32))
        out_specs.append(pl.BlockSpec(memory_space=pltpu.VMEM))
    names.append("out_vec")
    out_shape.append(jax.ShapeDtypeStruct((4, LANES), jnp.float32))
    out_specs.append(pl.BlockSpec(memory_space=pltpu.VMEM))
    for name in LEFTS:
        names.append("far_" + name)
        out_shape.append(jax.ShapeDtypeStruct(lefts[name].shape, low))
        out_specs.append(pl.BlockSpec(memory_space=pl.ANY))
    for name in RIGHTS:
        names.append("far_" + name)
        out_shape.append(jax.ShapeDtypeStruct(rights[name].shape[1:], low))
        out_specs.append(pl.BlockSpec(memory_space=pl.ANY))
    scratch = []

    def add(name, kind):
        names.append(name)
        scratch.append(kind)

    add("lefts", pltpu.VMEM((2, 768, 1152), low))
    add("rights", pltpu.VMEM((2, 768, 1024), low))
    add("left_sem", pltpu.SemaphoreType.DMA((2, 2)))
    add("right_sem", pltpu.SemaphoreType.DMA((2, 2)))
    for u, unit in enumerate(units):
        add(("part", u), pltpu.VMEM(unit.part_shape, low))
        for order in range(2):
            add(("first", u, order), pltpu.VMEM(unit.first_shapes[order], low))
        add(("second", u), pltpu.VMEM((2, *unit.second_shape), low))
        for order, place, z_at in unit.chains():
            if z_at > 0:
                add(("up", u, order, place), pltpu.VMEM(unit.chain_shape, low))
            if z_at < 3:
                add(("down", u, order, place), pltpu.VMEM(unit.chain_shape, low))
    add("vec", pltpu.VMEM(vec.shape, jnp.float32))
    add("vec_core", pltpu.VMEM(vec.shape[1:], jnp.float32))
    add("vec_x", pltpu.VMEM(vec.shape[2:], jnp.float32))
    add("vec_y", pltpu.VMEM(vec.shape[3:], jnp.float32))
    add("vec_up", pltpu.VMEM(vec.shape[3:], jnp.float32))
    add("vec_down", pltpu.VMEM(vec.shape[3:], jnp.float32))
    add("sent", pltpu.SemaphoreType.DMA((256,)))
    add("came", pltpu.SemaphoreType.DMA((256,)))

    def kernel(*refs):
        r = dict(zip(names, refs))
        r["vec"][...] = r["vec_in"][...]
        sum_kernel(units, names, *refs)

    found = pl.pallas_call(
        kernel,
        out_shape=out_shape,
        in_specs=in_specs,
        out_specs=out_specs,
        scratch_shapes=scratch,
        compiler_params=pltpu.CompilerParams(
            collective_id=0, has_side_effects=True, vmem_limit_bytes=60 * 2**20
        ),
        name="weight_sums",
    )(*operands)
    return dict(zip([*GRADS, "vec"], found[:6]))


def unsplit(value):
    blocks = []
    for b in range(4):
        x, c = b // 2, b % 2
        blocks.append(value[c, 0, :, 256 * x : 256 * x + 256])
        blocks.append(value[c, 0, :, 512 + LANES * x : 544 + LANES * x])
    return jnp.concatenate(blocks, axis=1)


def outer_sum(left, right):
    return dot_tn(left, right)


def summed(lefts, rights, vector_list):
    hidden = rights["hidden"]
    _, pieces, rows, width = hidden.shape
    hidden = hidden.reshape(2, pieces, rows, 2, width // 2).transpose(2, 3, 0, 1, 4)
    columns_of = dict(
        joined=unsplit(rights["stream"]),
        normed=rights["triple"],
        mixed=unsplit(rights["branch"]),
        second=hidden.reshape(rows, -1),
        active=unsplit(rights["upstream"]),
    )
    parts = []
    for name in ("joined", "normed", "mixed", "second", "active"):
        gathered = lax.all_gather(lefts[name], "batch", axis=0, tiled=True)
        columns = lax.all_to_all(
            columns_of[name], "batch", split_axis=1, concat_axis=0, tiled=True
        )
        parts.append(outer_sum(gathered, columns).astype(jnp.bfloat16))
    parts = lax.psum_scatter(tuple(parts), "seq", scatter_dimension=0, tiled=True)
    vectors = tuple(
        lax.psum_scatter(vector, ("seq", "batch"), scatter_dimension=0, tiled=True)
        for vector in vector_list
    )
    return tuple(part.astype(jnp.float32) for part in parts), vectors


def pack_vectors(vector_list):
    vec = jnp.concatenate([vector.reshape(32, -1) for vector in vector_list], axis=1)
    vec = jnp.pad(vec, ((0, 0), (0, 512 - vec.shape[1]))).reshape(4, 2, 2, 2, 4, LANES)
    return vec.transpose(3, 2, 1, 0, 4, 5)


def summed_by_kernel(lefts, rights, vector_list):
    found = weight_sums(lefts, rights, pack_vectors(vector_list))
    flat = found["vec"].reshape(-1)
    vectors, at = [], 0
    for vector in vector_list:
        width = vector.shape[0] // 32
        vectors.append(flat[at : at + width])
        at += width
    weight_parts = (
        found["skip"],
        found["attn"][:, :864],
        found["proj"],
        found["expand"],
        found["shrink"],
    )
    return weight_parts, tuple(vectors)


def rims(value, width):
    size = lax.axis_size("seq")
    up = [(i, i + 1) for i in range(size - 1)]
    down = [(j, i) for i, j in up]
    return (
        lax.ppermute(value[-width:], "seq", up),
        lax.ppermute(value[:width], "seq", down),
    )


def on_device(
    tokens,
    skip_tokens,
    segment_ids,
    upstream,
    skip_weight,
    skip_bias,
    first_gain,
    first_shift,
    attn_weight,
    attn_bias,
    proj_weight,
    proj_bias,
    second_gain,
    second_shift,
    expand_weight,
    expand_bias,
    shrink_weight,
    shrink_bias,
):
    _, rows, features = tokens.shape
    rim = (ITEM_MOST - 1 + 15) // 16 * 16
    tok, skp, above = tokens[0], skip_tokens[0], upstream[0]
    position = lax.axis_index("seq")
    padded_ids = jnp.pad(segment_ids[0], (rows, rows), constant_values=-1)
    window_ids = lax.dynamic_slice_in_dim(padded_ids, position * rows, 3 * rows, 0)
    id_row, id_col = window_ids[None, :], window_ids[:, None]

    stream, normed = stream_norm(tok, skp, skip_weight, skip_bias, first_gain, first_shift)
    before, after = rims(normed, rim)
    own = own_heads(normed, attn_weight, attn_bias)
    wins, mixed, lse = attend(own, before, after, attn_weight, attn_bias, id_col, id_row)
    (
        result, active, hidden_by_core, second, branch, branch_by_core, up_by_core, middle_grad,
        mixed_grad, hidden_sum, sums,
    ) = layer(
        stream, mixed, lse, above,
        (
            proj_weight, proj_bias, second_gain, second_shift, expand_weight, expand_bias,
            shrink_weight, shrink_bias,
        ),
    )
    before, after = rims(mixed_grad, rim)
    blank = jnp.zeros((rows - rim, mixed_grad.shape[1]), mixed_grad.dtype)
    grad_window = jnp.concatenate([blank, before, mixed_grad, after, blank], axis=0)
    stats = grad_window[:, features:].astype(jnp.float32)
    triple, triple_a, triple_b, triple_sum = attend_back(wins, grad_window, stats, id_col, id_row)
    tok_grad, skip_grad, stream_grad, stream_by_core, stream_sums = stream_back(
        triple, attn_weight, stream, middle_grad, first_gain, skip_weight
    )
    vector_list = (
        stream_sums[2],
        stream_sums[0],
        stream_sums[1],
        jnp.concatenate([triple_sum[0, :features], triple_sum[0, 2 * features :]]),
        sums[0],
        sums[1],
        sums[2],
        hidden_sum[0],
        sums[3],
    )
    joined = jnp.concatenate([tok, skp], axis=1)
    lefts = dict(active=active, second=second, mixed=mixed, normed=normed, joined=joined)
    rights = dict(
        upstream=up_by_core,
        hidden=hidden_by_core,
        branch=branch_by_core,
        triple_a=triple_a,
        triple_b=triple_b,
        stream=stream_by_core,
    )
    if lax.axis_size("seq") == 8 and lax.axis_size("batch") == 4:
        weight_parts, vectors = summed_by_kernel(lefts, rights, vector_list)
    else:
        weight_parts, vectors = summed(lefts, dict(rights, triple=triple), vector_list)
    return (
        result[None],
        tok_grad[None],
        skip_grad[None],
        weight_parts[0],
        vectors[0],
        vectors[1],
        vectors[2],
        weight_parts[1],
        vectors[3],
        weight_parts[2],
        vectors[4],
        vectors[5],
        vectors[6],
        weight_parts[3],
        vectors[7],
        weight_parts[4],
        vectors[8],
    )


def solution(mesh):
    in_specs = (
        P("batch", "seq", None),
        P("batch", "seq", None),
        P("batch", None),
        P("batch", "seq", None),
        P(),
        P(),
        P(),
        P(),
        P(),
        P(),
        P(),
        P(),
        P(),
        P(),
        P(),
        P(),
        P(),
        P(),
    )
    out_specs = (
        P("batch", "seq", None),
        P("batch", "seq", None),
        P("batch", "seq", None),
        P("seq", "batch"),
        P(("seq", "batch")),
        P(("seq", "batch")),
        P(("seq", "batch")),
        P("seq", "batch"),
        P(("seq", "batch")),
        P("seq", "batch"),
        P(("seq", "batch")),
        P(("seq", "batch")),
        P(("seq", "batch")),
        P("seq", "batch"),
        P(("seq", "batch")),
        P("seq", "batch"),
        P(("seq", "batch")),
    )
    return jax.shard_map(
        on_device, mesh=mesh, in_specs=in_specs, out_specs=out_specs, check_vma=False
    )
```

```python
import jax
import jax.numpy as jnp
from jax import lax
from jax.experimental import pallas as pl
from jax.experimental.pallas import tpu as pltpu
from jax.sharding import PartitionSpec as P

HEADS = 16
HEAD_DIM = 72
ITEM_MOST = 322
LANES = 128
MESH = pl.DeviceIdType.MESH
SCALE2 = HEAD_DIM**-0.5 * 1.4426950408889634
VMEM_MOST = 60 * 2**20


ROOT2 = 2.0**0.5


def dot(left, right):
    return jnp.dot(left, right, preferred_element_type=jnp.float32)


def dot_nt(left, right):
    return lax.dot_general(
        left, right, (((1,), (1,)), ((), ())), preferred_element_type=jnp.float32
    )


def dot_tn(left, right):
    return lax.dot_general(
        left, right, (((0,), (0,)), ((), ())), preferred_element_type=jnp.float32
    )


def whole():
    return pl.BlockSpec(memory_space=pltpu.VMEM)


def anywhere():
    return pl.BlockSpec(memory_space=pl.ANY)


def params():
    return pltpu.CompilerParams(vmem_limit_bytes=60 * 2**20)


def erf(value):
    v = jnp.clip(value, -3.832506856900711, 3.832506856900711)
    s = v * v
    top = 0.00022905065861350646
    for a in (0.0034082910107109506, 0.050955695062380861, 0.18520832239976145, 1.128379143519084):
        top = top * s + a
    low = -1.1791602954361697e-7
    for a in (0.000023547966471313185, 0.0010179625278914885, 0.014070470171167667):
        low = low * s + a
    low = (low * s + 0.11098505178285362) * s + 0.49746925110067538
    return v * top / (low * s + 1.0)


def row_norm(value):
    centred = value - jnp.mean(value, axis=-1, keepdims=True)
    scale = lax.rsqrt(jnp.mean(centred * centred, axis=-1, keepdims=True) + 1e-05)
    return centred * scale, scale


def norm_back(unit, scale, gain, cotangent):
    inner = cotangent * gain
    mean = jnp.mean(inner, axis=-1, keepdims=True)
    along = jnp.mean(inner * unit, axis=-1, keepdims=True)
    return scale * (inner - mean - unit * along)


def column_sum(value):
    return jnp.sum(value, axis=0, keepdims=True)


def stream_kernel(tok, skp, weight, bias, gain, shift, stream, normed, held, sems):
    copies = [
        pltpu.make_async_copy(weight.at[:, pl.ds(384 * n, 384)], held.at[n], sems.at[n])
        for n in range(3)
    ]
    for copy in copies:
        copy.start()
    features = tok.shape[1]
    for n, copy in enumerate(copies):
        copy.wait()
        at = slice(384 * n, 384 * n + 384)
        stream[:, at] = (
            dot(tok[...], held[n, :features])
            + dot(skp[...], held[n, features:])
            + bias[:, at].astype(jnp.float32)
        )
    unit, _ = row_norm(stream[...])
    normed[...] = (unit * gain[...].astype(jnp.float32) + shift[...].astype(jnp.float32)).astype(
        jnp.bfloat16
    )


def stream_norm(tok, skp, weight, bias, gain, shift):
    rows, features = tok.shape
    return pl.pallas_call(
        stream_kernel,
        out_shape=(
            jax.ShapeDtypeStruct((rows, features), jnp.float32),
            jax.ShapeDtypeStruct((rows, features), jnp.bfloat16),
        ),
        in_specs=[whole(), whole(), anywhere(), whole(), whole(), whole()],
        out_specs=(whole(), whole()),
        scratch_shapes=[
            pltpu.VMEM((3, 2 * features, 384), jnp.bfloat16),
            pltpu.SemaphoreType.DMA((3,)),
        ],
        compiler_params=params(),
        cost_estimate=pl.CostEstimate(
            flops=4 * rows * features * features, bytes_accessed=10**7, transcendentals=0
        ),
        name="stream_norm",
    )(tok, skp, weight, bias[None], gain[None], shift[None])


MARKS = (HEAD_DIM, HEAD_DIM + 16, HEAD_DIM + 32)


def lanes_of(shape):
    return lax.broadcasted_iota(jnp.int32, shape, len(shape) - 1)


def marked(lane):
    return (lane == MARKS[0]) | (lane == MARKS[1]) | (lane == MARKS[2])


def head_tile(value, h, ones):
    rows = value.shape[0]
    lane = lanes_of((rows, LANES - HEAD_DIM)) + HEAD_DIM
    rest = jnp.where(marked(lane) & ones, 1.0, 0.0).astype(value.dtype)
    return jnp.concatenate([value[:, HEAD_DIM * h : HEAD_DIM * (h + 1)], rest], axis=1)


def project(rows_ref, weight_ref, bias, part, store):
    features = rows_ref.shape[1]
    value = dot(rows_ref[...], weight_ref[...])
    if part != 1:
        at = 0 if part == 0 else features
        value = value + bias[:, at : at + features].astype(jnp.float32)
    value = value.astype(jnp.bfloat16)
    for h in range(HEADS):
        store(part, h, head_tile(value, h, part > 0))


def project_kernel(normed, weight, bias, out, held, sems):
    features = normed.shape[1]
    copies = [
        pltpu.make_async_copy(weight.at[:, pl.ds(features * p, features)], held.at[p], sems.at[p])
        for p in range(3)
    ]
    for copy in copies:
        copy.start()

    def store(part, h, value):
        out[part, h] = value

    for p, copy in enumerate(copies):
        copy.wait()
        project(normed, held.at[p], bias, p, store)


def own_heads(normed, weight, bias):
    rows, features = normed.shape
    return pl.pallas_call(
        project_kernel,
        out_shape=jax.ShapeDtypeStruct((3, HEADS, rows, LANES), jnp.bfloat16),
        in_specs=[whole(), anywhere(), whole()],
        out_specs=whole(),
        scratch_shapes=[
            pltpu.VMEM((3, features, features), jnp.bfloat16),
            pltpu.SemaphoreType.DMA((3,)),
        ],
        compiler_params=params(),
        cost_estimate=pl.CostEstimate(
            flops=6 * rows * features * features, bytes_accessed=2 * 10**7, transcendentals=0
        ),
        name="own_heads",
    )(normed, weight, bias[None])


HIDE = -1e30


def attend_kernel(own, before, after, weight, bias, id_col, id_row, wins, mixed, lse, *scratch):
    window, halo, held, hide, gathered, sems, out_sems = scratch
    rim, features = before.shape
    rows = own.shape[2]
    span = 3 * rows
    copies = [
        pltpu.make_async_copy(weight.at[:, pl.ds(features * p, features)], held.at[p], sems.at[p])
        for p in range(3)
    ]
    copies.append(pltpu.make_async_copy(own, window.at[:, :, pl.ds(rows, rows)], sems.at[3]))
    for copy in copies:
        copy.start()
    pad = rows - rim
    window[:, :, 0:pad] = jnp.zeros((3, HEADS, pad, LANES), jnp.bfloat16)
    window[:, :, span - pad : span] = jnp.zeros((3, HEADS, pad, LANES), jnp.bfloat16)
    halo[0:rim] = before[...]
    halo[rim:] = after[...]

    def store(part, h, value):
        window[part, h, pad:rows] = value[:rim]
        window[part, h, 2 * rows : 2 * rows + rim] = value[rim:]

    for p in (1, 2, 0):
        copies[p].wait()
        project(halo, held.at[p], bias, p, store)
    copies[3].wait()
    out_copies = [
        pltpu.make_async_copy(window.at[p], wins.at[p], out_sems.at[p]) for p in range(3)
    ]
    for copy in out_copies:
        copy.start()
    blocks = rows // LANES
    reach = span - (blocks - 1) * LANES
    for i in range(blocks):
        same = id_col[rows + i * LANES : rows + (i + 1) * LANES] == (
            id_row[:, i * LANES : i * LANES + reach]
        )
        hide[i] = jnp.where(same, 0.0, HIDE)
    lse[...] = jnp.zeros_like(lse)

    def body(h, carry):
        for i in range(blocks):
            keys = pl.ds(i * LANES, reach)
            scores = dot_nt(
                window[0, h, rows + i * LANES : rows + (i + 1) * LANES], window[1, h, keys]
            )
            scores = scores * SCALE2 + hide[i]
            highest = jnp.max(scores, axis=-1, keepdims=True)
            raised = jnp.exp2(scores - highest).astype(jnp.bfloat16)
            total = dot(raised, window[2, h, keys])
            denominator = total[:, HEAD_DIM : HEAD_DIM + 1]
            gathered[h, i * LANES : (i + 1) * LANES] = total / denominator
            value = highest + jnp.log2(denominator)
            at = slice(i * LANES, (i + 1) * LANES)
            lse[at] = jnp.where(lanes_of((LANES, LANES)) == h, value, lse[at])
        return carry

    lax.fori_loop(0, HEADS, body, 0)
    for h in range(HEADS):
        mixed[:, HEAD_DIM * h : HEAD_DIM * (h + 1)] = gathered[h, :, :HEAD_DIM].astype(jnp.bfloat16)
    for copy in out_copies:
        copy.wait()


def attend(own, before, after, weight, bias, id_col, id_row):
    rim, features = before.shape
    rows = own.shape[2]
    span = 3 * rows
    return pl.pallas_call(
        attend_kernel,
        out_shape=(
            jax.ShapeDtypeStruct((3, HEADS, span, LANES), jnp.bfloat16),
            jax.ShapeDtypeStruct((rows, features), jnp.bfloat16),
            jax.ShapeDtypeStruct((rows, LANES), jnp.float32),
        ),
        in_specs=[anywhere(), whole(), whole(), anywhere(), whole(), whole(), whole()],
        out_specs=(anywhere(), whole(), whole()),
        scratch_shapes=[
            pltpu.VMEM((3, HEADS, span, LANES), jnp.bfloat16),
            pltpu.VMEM((2 * rim, features), jnp.bfloat16),
            pltpu.VMEM((3, features, features), jnp.bfloat16),
            pltpu.VMEM((rows // LANES, LANES, span - rows + LANES), jnp.float32),
            pltpu.VMEM((HEADS, rows, LANES), jnp.float32),
            pltpu.SemaphoreType.DMA((4,)),
            pltpu.SemaphoreType.DMA((3,)),
        ],
        compiler_params=params(),
        name="attend",
    )(own, before, after, weight, bias[None], id_col, id_row)


def by_core_store(ref, value):
    rows = value.shape[0]
    blank = jnp.zeros((rows, LANES - 32), value.dtype)
    for b in range(4):
        x, c = b // 2, b % 2
        ref[c, 0, :, 256 * x : 256 * x + 256] = value[:, 288 * b : 288 * b + 256]
        ref[c, 0, :, 512 + LANES * x : 640 + LANES * x] = jnp.concatenate(
            [value[:, 288 * b + 256 : 288 * b + 288], blank], axis=1
        )


def split3(value):
    first = value.astype(jnp.bfloat16)
    rest = value - first.astype(jnp.float32)
    second = rest.astype(jnp.bfloat16)
    return first, second, (rest - second.astype(jnp.float32)).astype(jnp.bfloat16)


def layer_kernel(
    stream, mixed, lse, upstream, proj, proj_bias, gain, shift, expand, expand_bias, shrink,
    shrink_bias, result, active, hidden_by_core, second, branch, branch_by_core, up_by_core,
    middle_grad, mixed_grad, hidden_sum, sums, middle, total, second_grad,
):
    step, steps = pl.program_id(0), pl.num_programs(0)
    low = jnp.bfloat16

    @pl.when(step == 0)
    def _():
        middle[...] = (
            stream[...] + dot(mixed[...], proj[...]) + proj_bias[...].astype(jnp.float32)
        )
        unit, _ = row_norm(middle[...])
        second[...] = (
            unit * gain[...].astype(jnp.float32) + shift[...].astype(jnp.float32)
        ).astype(low)
        total[...] = middle[...] + shrink_bias[...].astype(jnp.float32)
        second_grad[...] = jnp.zeros_like(second_grad)
        by_core_store(up_by_core, upstream[...])

    hidden = dot(second[...], expand[...]) + expand_bias[...].astype(jnp.float32)
    active_grad = dot_nt(upstream[...], shrink[...])
    cdf = 0.5 + 0.5 * erf(hidden * (1.0 / ROOT2))
    density = jnp.exp(-0.5 * hidden * hidden) * 0.3989422804014327
    raised = (hidden * cdf).astype(low)
    active[...] = raised
    hidden_grad = (active_grad * (cdf + hidden * density)).astype(low)
    for j in range(3):
        hidden_by_core[0, j] = hidden_grad[:, 384 * j : 384 * (j + 1)]
    hidden_sum[...] = column_sum(hidden_grad.astype(jnp.float32))
    total[...] += dot(raised, shrink[...])
    second_grad[...] += dot_nt(hidden_grad, expand[...])

    @pl.when(step == steps - 1)
    def _():
        result[...] = total[...].astype(low)
        unit, scale = row_norm(middle[...])
        cotangent = second_grad[...]
        above = upstream[...].astype(jnp.float32)
        grad = above + norm_back(unit, scale, gain[...].astype(jnp.float32), cotangent)
        middle_grad[...] = grad
        branched = grad.astype(low)
        branch[...] = branched
        by_core_store(branch_by_core, branched)
        sums[0:1] = column_sum(branched.astype(jnp.float32))
        sums[1:2] = column_sum(cotangent * unit)
        sums[2:3] = column_sum(cotangent)
        sums[3:4] = column_sum(above)
        back = dot_nt(branched, proj[...]).astype(low)
        features = back.shape[1]
        mixed_grad[:, :features] = back
        products = back.astype(jnp.float32) * mixed[...].astype(jnp.float32)
        shape = (features, LANES)
        member = lax.broadcasted_iota(jnp.int32, shape, 0) // HEAD_DIM == lanes_of(shape)
        member = jnp.where(member, 1.0, 0.0).astype(low)
        high = products.astype(low)
        inner = dot(high, member) + dot((products - high.astype(jnp.float32)).astype(low), member)
        pieces = [part[:, :HEADS] for part in split3(lse[...] * (-1.0 / SCALE2)) + split3(-inner)]
        blank = jnp.zeros((back.shape[0], LANES - 6 * HEADS), low)
        mixed_grad[:, features:] = jnp.concatenate(pieces + [blank], axis=1)


def layer(stream, mixed, lse, upstream, weights):
    proj, proj_bias, gain, shift, expand, expand_bias, shrink, shrink_bias = weights
    rows, features = stream.shape
    hidden = expand.shape[1]
    wide = hidden // 4
    low = jnp.bfloat16

    def held(shape):
        return pl.BlockSpec(shape, lambda t: (0,) * len(shape))

    narrow = (rows, features)
    vector = (1, features)
    split = (2, 1, rows, 768)
    return pl.pallas_call(
        layer_kernel,
        grid=(4,),
        in_specs=[
            held(narrow), held(narrow), held((rows, LANES)), held(narrow),
            held((features, features)), held(vector), held(vector), held(vector),
            pl.BlockSpec((features, wide), lambda t: (0, t)),
            pl.BlockSpec((1, wide), lambda t: (0, t)),
            pl.BlockSpec((wide, features), lambda t: (t, 0)),
            held(vector),
        ],
        out_specs=(
            held(narrow),
            pl.BlockSpec((rows, wide), lambda t: (0, t)),
            pl.BlockSpec((1, 3, rows, 384), lambda t: (t % 2, 0, 0, t // 2)),
            held(narrow), held(narrow), held(split), held(split), held(narrow),
            held((rows, features + LANES)),
            pl.BlockSpec((1, wide), lambda t: (0, t)),
            held((8, features)),
        ),
        out_shape=(
            jax.ShapeDtypeStruct(narrow, low),
            jax.ShapeDtypeStruct((rows, hidden), low),
            jax.ShapeDtypeStruct((2, 3, rows, 768), low),
            jax.ShapeDtypeStruct(narrow, low),
            jax.ShapeDtypeStruct(narrow, low),
            jax.ShapeDtypeStruct(split, low),
            jax.ShapeDtypeStruct(split, low),
            jax.ShapeDtypeStruct(narrow, jnp.float32),
            jax.ShapeDtypeStruct((rows, features + LANES), low),
            jax.ShapeDtypeStruct((1, hidden), jnp.float32),
            jax.ShapeDtypeStruct((8, features), jnp.float32),
        ),
        scratch_shapes=[pltpu.VMEM(narrow, jnp.float32)] * 3,
        compiler_params=params(),
        name="layer",
    )(
        stream, mixed, lse, upstream, proj, proj_bias[None], gain[None], shift[None], expand,
        expand_bias[None], shrink, shrink_bias[None],
    )


def back_masks(id_col, id_row, own_hide, rim_hide, rows):
    blocks = rows // LANES
    reach = own_hide.shape[2]

    def hidden(first, keys, width):
        same = id_col[first : first + LANES] == id_row[:, keys : keys + width]
        return jnp.where(same, 0.0, HIDE).astype(own_hide.dtype)

    for i in range(blocks):
        own_hide[i] = hidden(rows + i * LANES, i * LANES, reach)
    for w in range(blocks):
        rim_hide[w] = hidden(w * LANES, rows, rows)
        rim_hide[blocks + w] = hidden(2 * rows + w * LANES, rows, rows)


def with_stats(value, stats, shift):
    lane = lanes_of(value.shape)
    moved = pltpu.roll(stats, shift, 1)
    return jnp.where(marked(lane), moved, value.astype(jnp.float32)).astype(value.dtype)


def back_head(h, queries, keys, values, grads, stats, own_hide, rim_hide, probs, scored, store):
    span = queries.shape[0]
    rows = span // 3
    blocks = rows // LANES
    reach = span - rows + LANES
    low = jnp.bfloat16
    queries[...] = with_stats(queries[...], stats[...], MARKS[0] - h)
    turn = MARKS[0] - 3 * HEADS - h
    grads[...] = with_stats(grads[...], stats[...], jnp.where(turn < 0, turn + LANES, turn))

    def pair(q_at, k_at, width, hide):
        q_rows, k_rows = pl.ds(q_at, LANES), pl.ds(k_at, width)
        exponent = dot_nt(queries[q_rows], keys[k_rows]) * SCALE2 + hide.astype(jnp.float32)
        weight = jnp.exp2(exponent)
        scored = weight * dot_nt(grads[q_rows], values[k_rows])
        return weight.astype(low), scored.astype(low)

    query_grad = []
    for i in range(blocks):
        at = rows + i * LANES
        weight, score = pair(at, i * LANES, reach, own_hide[i])
        query_grad.append(dot(score, keys[i * LANES : i * LANES + reach]))
        mine = slice(rows - i * LANES, 2 * rows - i * LANES)
        probs[at : at + LANES] = weight[:, mine]
        scored[at : at + LANES] = score[:, mine]
    for w in range(blocks):
        for at, first, width in (
            (w * LANES, 0, (w + 1) * LANES),
            (2 * rows + w * LANES, w * LANES, rows - w * LANES),
        ):
            hide = rim_hide[w if at < rows else blocks + w]
            weight, score = pair(at, rows + first, width, hide[:, first : first + width])
            probs[at : at + LANES, first : first + width] = weight
            scored[at : at + LANES, first : first + width] = score
    factor = HEAD_DIM**-0.5
    for i in range(blocks):
        store(0, i * LANES, LANES, query_grad[i] * factor)
    store(1, 0, rows, dot_tn(scored[...], queries[...]) * factor)
    store(2, 0, rows, dot_tn(probs[...], grads[...]))


def heads_apart(row_ref, out):
    value = row_ref[...]
    for h in range(HEADS):
        out[h] = head_tile(value[:, : HEADS * HEAD_DIM], h, False)


def triple_store(apart, triple):
    features = HEADS * HEAD_DIM
    for p in range(3):
        for h in range(HEADS):
            at = features * p + HEAD_DIM * h
            triple[:, at : at + HEAD_DIM] = apart[p, h, :, :HEAD_DIM]


def attend_back_kernel(
    wins, grads_in, stats, id_col, id_row, triple, sums,
    window, grads, own_hide, rim_hide, probs, scored, apart, sems,
):
    span = window.shape[2]
    rows = span // 3
    copy = pltpu.make_async_copy(wins, window, sems.at[0])
    copy.start()
    back_masks(id_col, id_row, own_hide, rim_hide, rows)
    probs[...] = jnp.zeros_like(probs)
    scored[...] = jnp.zeros_like(scored)
    heads_apart(grads_in, grads)
    copy.wait()

    def body(h, carry):
        def store(part, first, count, value):
            apart[part, h, pl.ds(first, count)] = value.astype(jnp.bfloat16)

        back_head(
            h, window.at[0, h], window.at[1, h], window.at[2, h], grads.at[h], stats, own_hide,
            rim_hide, probs, scored, store,
        )
        return carry

    lax.fori_loop(0, HEADS, body, 0)
    triple_store(apart, triple)
    sums[...] = column_sum(triple[...].astype(jnp.float32))


def attend_back(wins, grads_in, stats, id_col, id_row):
    span = wins.shape[2]
    rows = span // 3
    features = HEADS * HEAD_DIM
    low = jnp.bfloat16
    return pl.pallas_call(
        attend_back_kernel,
        out_shape=(
            jax.ShapeDtypeStruct((rows, 3 * features), low),
            jax.ShapeDtypeStruct((1, 3 * features), jnp.float32),
        ),
        in_specs=[anywhere(), whole(), whole(), whole(), whole()],
        out_specs=(whole(), whole()),
        scratch_shapes=[
            pltpu.VMEM((3, HEADS, span, LANES), low),
            pltpu.VMEM((HEADS, span, LANES), low),
            pltpu.VMEM((rows // LANES, LANES, span - rows + LANES), low),
            pltpu.VMEM((2 * rows // LANES, LANES, rows), low),
            pltpu.VMEM((span, rows), low),
            pltpu.VMEM((span, rows), low),
            pltpu.VMEM((3, HEADS, rows, LANES), low),
            pltpu.SemaphoreType.DMA((1,)),
        ],
        compiler_params=params(),
        name="attend_back",
    )(wins, grads_in, stats, id_col, id_row)


def stream_back_kernel(
    triple, weight, stream, middle_grad, gain, skip_weight, tok_grad, skip_grad, by_core, sums, held, held_skip, grad, sems,
):
    features = stream.shape[1]
    low = jnp.bfloat16
    copies = [
        pltpu.make_async_copy(weight.at[:, pl.ds(features * p, features)], held.at[p], sems.at[p])
        for p in range(3)
    ]
    copies += [
        pltpu.make_async_copy(
            skip_weight.at[pl.ds(features * p, features)], held_skip.at[p], sems.at[3 + p]
        )
        for p in range(2)
    ]
    for copy in copies:
        copy.start()
    unit, scale = row_norm(stream[...])
    for p in range(3):
        copies[p].wait()
        part = dot_nt(triple[:, features * p : features * (p + 1)], held[p])
        if p == 0:
            grad[...] = part
        else:
            grad[...] += part
    cotangent = grad[...]
    sums[0:1] = column_sum(cotangent * unit)
    sums[1:2] = column_sum(cotangent)
    whole_grad = middle_grad[...] + norm_back(
        unit, scale, gain[...].astype(jnp.float32), cotangent
    )
    rounded = whole_grad.astype(low)
    by_core_store(by_core, rounded)
    sums[2:3] = column_sum(rounded.astype(jnp.float32))
    for p, out in enumerate((tok_grad, skip_grad)):
        copies[3 + p].wait()
        out[...] = dot_nt(rounded, held_skip[p]).astype(low)


def stream_back(triple, weight, stream, middle_grad, gain, skip_weight):
    rows, features = stream.shape
    low = jnp.bfloat16
    return pl.pallas_call(
        stream_back_kernel,
        out_shape=(
            jax.ShapeDtypeStruct((rows, features), low),
            jax.ShapeDtypeStruct((rows, features), low),
            jax.ShapeDtypeStruct((2, 1, rows, 768), low),
            jax.ShapeDtypeStruct((8, features), jnp.float32),
        ),
        in_specs=[whole(), anywhere(), whole(), whole(), whole(), anywhere()],
        out_specs=(whole(), whole(), whole(), whole()),
        scratch_shapes=[
            pltpu.VMEM((3, features, features), low),
            pltpu.VMEM((2, features, features), low),
            pltpu.VMEM((rows, features), jnp.float32),
            pltpu.SemaphoreType.DMA((5,)),
        ],
        compiler_params=params(),
        name="stream_back",
    )(triple, weight, stream, middle_grad, gain[None], skip_weight)


ROWS = 144
THIRD = ROWS // 3


class Unit:
    def __init__(self, left, left_at, right, right_at, tiles, blocks, out, out_at):
        self.left, self.left_at = left, left_at
        self.right, self.right_at = right, right_at
        self.tiles = tiles
        self.blocks = blocks
        self.out, self.out_at = out, out_at
        self.rows = ROWS * tiles if tiles else 2 * ROWS + THIRD
        self.z_of = {(order, place): z for _, order, _, place, z in blocks}


ORDER_OF = (0, 1, 1, 0)
QUARTERS = tuple(
    ((2 * z + y) * ROWS, ORDER_OF[z], y, z // 2, z) for z in range(4) for y in range(2)
)


def make_units():
    units = {}
    for z in range(4):
        blocks = [
            (y * 576 + q * ROWS, q // 2, y, q % 2, z) for y in range(2) for q in range(4)
        ]
        units[f"shrink{z}"] = Unit("active", z * 1152, "upstream", 0, 0, blocks, "shrink", 0)
    for j in range(3):
        units[f"expand{j}"] = Unit("second", 0, "hidden", j, 3, QUARTERS, "expand", 3 * j)
    units["proj"] = Unit("mixed", 0, "branch", 0, 0, QUARTERS, "proj", 0)
    for j, (first, tiles) in enumerate(TRIPLE_TILES):
        units[f"attn{j}"] = Unit("normed", 0, f"triple{j}", 0, tiles, QUARTERS, "attn", first)
    for k, name in enumerate(("tok", "skp")):
        blocks = [
            (h * 576 + y * 288 + i * ROWS, h, y, i, 2 * k + h)
            for h in range(2)
            for y in range(2)
            for i in range(2)
        ]
        units[f"skip{k}"] = Unit(name, 0, "stream_cols", 0, 0, blocks, "skip", 0)
    return units


TRIPLE_TILES = ((0, 3), (3, 2), (5, 2))
GRADS = (
    ("shrink", (576, 288)),
    ("expand", (144, 1152)),
    ("proj", (144, 288)),
    ("attn", (144, 896)),
    ("skip", (288, 288)),
)
PART_SLOTS, FIRST_SLOTS, SECOND_SLOTS, LAST_SLOTS = 4, 4, 4, 5
LINE_FIRST = ("expand0",)
X_FIRST = ("shrink0", "shrink1", "shrink2", "shrink3")

PLAN = (
    "start shrink0", "start expand0", "start shrink3", "start shrink1", "start shrink2",
    "line expand0 1 0", "line expand0 1 1", "line expand0 1 2", "second shrink0", "line expand0 2 0",
    "second shrink3", "line expand0 2 1", "line expand0 3 0", "halo", "heads 4", "line_end expand0",
    "second shrink1", "third shrink0", "start expand1", "third shrink3", "start expand2",
    "hop shrink0 2", "heads 2", "hop shrink3 2", "second shrink2", "hop shrink0 3", "third shrink1",
    "start proj", "line_x expand0", "heads 2", "hop shrink3 3", "hop shrink1 2", "hop shrink1 3",
    "finish shrink0", "heads 2", "second expand1", "heads 2", "second expand2", "finish shrink3",
    "finish shrink1", "third shrink2", "heads 2", "line_y expand0", "second proj", "hop shrink2 2",
    "hop shrink2 3", "heads 2", "pack", "start attn0", "finish shrink2", "third expand1", "start attn1",
    "hop expand1 2", "third expand2", "start attn2", "hop expand1 3", "back 0", "hop expand2 2",
    "second attn0", "back 1", "hop expand2 3", "finish expand1", "back 2", "second attn1", "norm",
    "vec 0", "second attn2", "vec 1", "finish expand2", "third proj", "start skip0", "hop proj 2",
    "third attn0", "start skip1", "hop proj 3", "hop attn0 2", "out 0", "vec 2", "out 1", "hop attn0 3",
    "out 2", "third attn1", "hop attn1 2", "finish proj", "second skip0", "third attn2", "hop attn1 3",
    "hop attn2 2", "hop attn2 3", "finish attn0", "vec 3", "second skip1", "finish attn1", "third skip0",
    "hop skip0 2", "finish attn2", "vec 4", "hop skip0 3", "third skip1", "hop skip1 2", "hop skip1 3",
    "finish skip0", "vec 5", "finish skip1",
)


def add_into(target, other):
    target[...] = (target[...].astype(jnp.float32) + other[...].astype(jnp.float32)).astype(
        target.dtype
    )


def gradient_kernel(r):
    seq, batch = lax.axis_index("seq"), lax.axis_index("batch")
    z, y = seq // 2, seq % 2
    x, c = batch // 2, batch % 2
    at = {
        "core": (seq, 2 * x + (1 - c)),
        "x": (seq, 2 * (1 - x) + c),
        "y": (2 * z + (1 - y), batch),
        "above": (2 * jnp.minimum(z + 1, 3) + y, batch),
        "below": (2 * jnp.maximum(z - 1, 0) + y, batch),
        "far": (2 * ((z + 2) % 4) + y, batch),
        "next": (jnp.minimum(seq + 1, 7), batch),
        "last": (jnp.maximum(seq - 1, 0), batch),
    }
    at["pair"] = (2 * (z + 1 - 2 * (z % 2)) + y, batch)
    units = make_units()
    low = jnp.bfloat16
    rows, features = r["tok"].shape
    ids = {}

    def remote(key, src, dst, side):
        i = ids.setdefault(key, len(ids))
        return pltpu.make_async_remote_copy(
            src_ref=src,
            dst_ref=dst,
            send_sem=r["sent"].at[i],
            recv_sem=r["came"].at[i],
            device_id=at[side],
            device_id_type=MESH,
        )

    barrier = pltpu.get_barrier_semaphore()

    def greet(side):
        pl.semaphore_signal(barrier, 1, device_id=at[side], device_id_type=MESH)

    for side in ("core", "x", "y", "far"):
        greet(side)
    for side, some in (
        ("above", z < 3),
        ("below", z > 0),
        ("next", (y == 1) & (z < 3)),
        ("last", (y == 0) & (z > 0)),
    ):
        pl.when(some)(lambda side=side: greet(side))
    more = (z < 3).astype(jnp.int32) + (z > 0).astype(jnp.int32)
    diagonal = jnp.where(y == 1, (z < 3).astype(jnp.int32), (z > 0).astype(jnp.int32))
    pl.semaphore_wait(barrier, 4 + more + diagonal)

    rim = (ITEM_MOST - 1 + 15) // 16 * 16
    window = r["window"]
    halo_up = remote(
        "halo_up", r["grads"].at[pl.ds(rows - rim, rim)], window.at[pl.ds(rows - rim, rim)], "next"
    )
    halo_down = remote(
        "halo_down", r["grads"].at[pl.ds(0, rim)], window.at[pl.ds(2 * rows, rim)], "last"
    )
    pl.when(seq < 7)(halo_up.start)
    pl.when(seq > 0)(halo_down.start)

    swaps = {}

    def swap(side, name, first):
        key = (side, name, first)
        if key in swaps:
            return
        if side == "left":
            cols = pl.ds(first, features)
            src, dst = r[name].at[:, cols], r["far_" + name].at[:, cols]
        else:
            src, dst = r[name].at[1 - c, first], r["far_" + name].at[first]
        swaps[key] = remote(key, src, dst, "core")
        swaps[key].start()

    def swap_unit(name):
        unit = units[name]
        swap("left", unit.left, unit.left_at)
        swap("right", unit.right, unit.right_at)

    order = [step.split()[1] for step in PLAN if step.startswith("start ")]
    for name in order:
        unit = units[name]
        swap("left", unit.left, unit.left_at)
        if not unit.right.startswith(("triple", "stream")):
            swap("right", unit.right, unit.right_at)

    slots, loads, here = {}, {}, set()

    def load(side, name, first, busy=None):
        key = (side, name, first)
        if key in slots:
            return
        slot = 1 - slots.get(busy, 1)
        for other in [k for k in slots if k[0] == side and slots[k] == slot]:
            del slots[other]
        slots[key] = slot
        if key not in here:
            swaps[key].wait_recv()
            here.add(key)
        if side == "left":
            cols = pl.ds(first, features)
            near, far = r[name].at[:, cols], r["far_" + name].at[:, cols]
            hold = r["lefts"].at[slot]
        else:
            near, far = r[name].at[c, first], r["far_" + name].at[first]
            hold = r["rights"].at[slot, :, pl.ds(0, near.shape[-1])]
        loads[key] = []
        for half, src in ((0, near), (1, far)):
            copy = pltpu.make_async_copy(
                src, hold.at[pl.ds(rows * half, rows)], r[side + "_sem"].at[slot, half]
            )
            copy.start()
            loads[key].append(copy)

    def keys_of(name):
        unit = units[name]
        return ("left", unit.left, unit.left_at), ("right", unit.right, unit.right_at)

    started = [name for name in order if name not in LINE_FIRST]
    both = slice(None)

    def axes(u, order):
        return ("x", "y") if order == 0 or started[u] in X_FIRST else ("y", "x")

    def credit(stage, order, side):
        return r["credit"].at[(stage * 2 + order) * 2 + ("x", "y").index(side)]

    def take_credit(u, stage, order):
        if u >= (FIRST_SLOTS, SECOND_SLOTS)[stage]:
            pl.semaphore_wait(credit(stage, order, axes(u, order)[stage]), 1)

    def give_credit(u, stage, order):
        then = u + (FIRST_SLOTS, SECOND_SLOTS)[stage]
        if then < len(started):
            side = axes(then, order)[stage]
            pl.semaphore_signal(
                credit(stage, order, side), 1, device_id=at[side], device_id_type=MESH
            )

    def part_of(u, order, *index):
        unit = units[started[u]]
        place = (pl.ds(0, 2), pl.ds(0, unit.rows)) if len(index) < 3 else (pl.ds(0, unit.rows),)
        return r["part"].at[(u % PART_SLOTS, order, *index, *place)]

    def moved(u, order, stage):
        land = r["land_one"] if stage == 0 else r["land_two"]
        land = land.at[u % (FIRST_SLOTS, SECOND_SLOTS)[stage], order]
        height = pl.ds(0, units[started[u]].rows)
        if stage == 1:
            send = (x, 1 - y) if axes(u, order)[1] == "y" else (1 - x, y)
            return part_of(u, order, *send), part_of(u, order, x, y), land.at[:, height]
        if axes(u, order)[0] == "x":
            send, keep = (1 - x, both), (x, both)
        else:
            send, keep = (both, 1 - y), (both, y)
        return part_of(u, order, *send), part_of(u, order, *keep), land.at[:, :, height]

    def stage_copy(u, order, stage):
        send, _, land = moved(u, order, stage)
        return remote((u, stage, order), send, land, axes(u, order)[stage])

    def compute(name, part, slot):
        unit = units[name]
        left_key, right_key = keys_of(name)
        left, right = r["lefts"].at[slots[left_key]], r["rights"].at[slots[right_key]]

        def product(n):
            cols = pl.ds(pl.multiple_of(n * 256, 256), 256)
            return dot_tn(left[...], right[:, cols])

        if unit.tiles:

            def body(n, carry):
                tile = product(n).astype(low)
                for i in range(2):
                    g = 2 * n + i
                    x_at = g // unit.tiles
                    t = pl.multiple_of((g - x_at * unit.tiles) * ROWS, 16)
                    for first, order, y_at, place, _ in unit.blocks:
                        part[slot, order, x_at, y_at, place, pl.ds(t, ROWS)] = tile[
                            first : first + ROWS, i * LANES : (i + 1) * LANES
                        ]
                return carry

            lax.fori_loop(0, unit.tiles, body, 0)
            return

        def body(n, carry):
            tile = product(n).astype(low)
            for first, order, y_at, place, _ in unit.blocks:
                for i in range(2):
                    part[slot, order, n, y_at, place, pl.ds(i * ROWS, ROWS)] = tile[
                        first : first + ROWS, i * LANES : (i + 1) * LANES
                    ]
            return carry

        lax.fori_loop(0, 2, body, 0)
        tile = product(2)
        for first, order, y_at, place, _ in unit.blocks:
            for x_at in range(2):
                pieces = [
                    tile[first + s * THIRD : first + (s + 1) * THIRD, x_at * LANES :][:, :32]
                    for s in range(3)
                ]
                packed = jnp.concatenate(pieces + [jnp.zeros_like(pieces[0])], axis=1)
                part[slot, order, x_at, y_at, place, pl.ds(2 * ROWS, THIRD)] = packed.astype(low)

    def wait_sends(u):
        for order in range(2):
            for stage in range(2):
                stage_copy(u, order, stage).wait_send()

    def fetch(name, ahead):
        for key in keys_of(name):
            load(*key)
            for copy in loads.pop(key, ()):
                copy.wait()
        if ahead is not None and not ahead.startswith("skip"):
            for key, busy in zip(keys_of(ahead), keys_of(name)):
                if key in swaps:
                    load(*key, busy)

    def first_stage(u):
        if u >= PART_SLOTS:
            wait_sends(u - PART_SLOTS)
        compute(started[u], r["part"], u % PART_SLOTS)
        for order in range(2):
            take_credit(u, 0, order)
            stage_copy(u, order, 0).start()

    def second_stage(u):
        for order in range(2):
            stage_copy(u, order, 0).wait_recv()
            _, keep, land = moved(u, order, 0)
            add_into(keep, land)
            give_credit(u, 0, order)
            take_credit(u, 1, order)
            stage_copy(u, order, 1).start()

    def last_ref(u, order, place):
        return r["ends"].at[u % LAST_SLOTS, order, place, pl.ds(0, units[started[u]].rows)]

    def third_stage(u):
        if u >= LAST_SLOTS:
            chain_sends(u - LAST_SLOTS)
        for order in range(2):
            stage_copy(u, order, 1).wait_recv()
            _, keep, land = moved(u, order, 1)
            for place in range(2):
                value = keep.at[place][...].astype(jnp.float32)
                value = value + land.at[place][...].astype(jnp.float32)
                last_ref(u, order, place)[...] = value.astype(low)
            give_credit(u, 1, order)

    def chain_copy(u, order, place, up):
        pool, i = r["chain_at"][started[u], order, place, up]
        dst = r[pool].at[i, pl.ds(0, units[started[u]].rows)]
        src = last_ref(u, order, place)
        key = (u, "chain", order, place, up)
        return remote(key, src, dst, "above" if up else "below"), dst

    def hop(u, step):
        for up, me in ((True, step - 1), (False, 4 - step)):
            todo = [
                key
                for key, z_at in sorted(
                    units[started[u]].z_of.items(), key=lambda item: -item[1] if up else item[1]
                )
                if ((z_at > me) if up else (z_at < me))
            ]

            @pl.when(z == me)
            def _():
                for order, place in todo:
                    copy, land = chain_copy(u, order, place, up)
                    if step > 1:
                        copy.wait_recv()
                        add_into(last_ref(u, order, place), land)
                    copy.start()

    def chain_sends(u):
        for (order, place), z_at in units[started[u]].z_of.items():
            for up, some in ((True, z_at > 0), (False, z_at < 3)):
                if some:

                    @pl.when((z < z_at) if up else (z > z_at))
                    def _():
                        chain_copy(u, order, place, up)[0].wait_send()

    def finish(u):
        unit = units[started[u]]
        for (order, place), z_at in unit.z_of.items():

            @pl.when(z == z_at)
            def _():
                value = last_ref(u, order, place)[...].astype(jnp.float32)
                for up, have in ((True, z_at > 0), (False, z_at < 3)):
                    if have:
                        copy, land = chain_copy(u, order, place, up)
                        copy.wait_recv()
                        value = value + land[...].astype(jnp.float32)
                store_out(unit, order, place, value)

    def store_out(unit, order, place, value):
        out = r["out_" + unit.out]
        if unit.tiles:
            for t in range(unit.tiles):
                col = (unit.out_at + t) * LANES
                out[:, col : col + LANES] = value[t * ROWS : (t + 1) * ROWS]
            return
        base = {"shrink": (2 * order + place) * ROWS, "proj": 0, "skip": place * ROWS}[unit.out]
        for i in range(2):
            out[base : base + ROWS, i * LANES : (i + 1) * LANES] = value[i * ROWS : (i + 1) * ROWS]
        for s in range(3):
            out[base + s * THIRD : base + (s + 1) * THIRD, 256:288] = value[
                2 * ROWS : 2 * ROWS + THIRD, s * 32 : (s + 1) * 32
            ]

    def line_ref(name, order, place):
        i = LINE_FIRST.index(name)
        return r["line"].at[i, order, both, both, place, pl.ds(0, units[name].rows)]

    def line_copy(name, order, place, up):
        i = r["line_at"][name, order, place, up]
        dst = r["line_land"].at[i, both, both, pl.ds(0, units[name].rows)]
        key = (name, "line", order, place, up)
        return remote(key, line_ref(name, order, place), dst, "above" if up else "below"), dst

    def line_hop(name, step, turn):
        for up, me in ((True, step - 1), (False, 4 - step)):
            todo = [
                key
                for key, z_at in sorted(
                    units[name].z_of.items(), key=lambda item: -item[1] if up else item[1]
                )
                if ((z_at > me) if up else (z_at < me))
            ][turn : turn + 1]

            @pl.when(z == me)
            def _():
                for order, place in todo:
                    copy, land = line_copy(name, order, place, up)
                    if step > 1:
                        copy.wait_recv()
                        add_into(line_ref(name, order, place), land)
                    copy.start()

    def line_copies(name):
        i = LINE_FIRST.index(name)
        height = pl.ds(0, units[name].rows)
        own = r["line_own"].at[i]
        return (
            remote((name, "line_x"), own.at[1 - x, both, height], r["line_x"].at[i, both, height], "x"),
            remote((name, "line_y"), own.at[x, 1 - y, height], r["line_y"].at[i, height], "y"),
        )

    def line_stage(name, stage):
        i = LINE_FIRST.index(name)
        unit = units[name]
        height = pl.ds(0, unit.rows)
        if stage == "end":
            for (order, place), z_at in unit.z_of.items():

                @pl.when(z == z_at)
                def _():
                    lands = []
                    for up, have in ((True, z_at > 0), (False, z_at < 3)):
                        if have:
                            copy, land = line_copy(name, order, place, up)
                            copy.wait_recv()
                            lands.append(land)
                    for x_at in range(2):
                        for y_at in range(2):
                            value = line_ref(name, order, place)[x_at, y_at].astype(jnp.float32)
                            for land in lands:
                                value = value + land[x_at, y_at].astype(jnp.float32)
                            r["line_own"][i, x_at, y_at, height] = value.astype(low)

            line_copies(name)[0].start()
        elif stage == "x":
            line_copies(name)[0].wait_recv()
            add_into(r["line_own"].at[i, x, both, height], r["line_x"].at[i, both, height])
            line_copies(name)[1].start()
        else:
            line_copies(name)[1].wait_recv()
            value = r["line_own"][i, x, y, height].astype(jnp.float32)
            value = value + r["line_y"][i, height].astype(jnp.float32)
            store_out(unit, 0, 0, value)

    def line_drain(name):
        for (order, place), z_at in units[name].z_of.items():
            for up, some in ((True, z_at > 0), (False, z_at < 3)):
                if some:

                    @pl.when((z < z_at) if up else (z > z_at))
                    def _():
                        line_copy(name, order, place, up)[0].wait_send()

        for copy in line_copies(name):
            copy.wait_send()

    def head_load(h):
        return pltpu.make_async_copy(
            r["wins"].at[:, h], r["head"].at[h % 2], r["head_sem"].at[h % 2]
        )

    done = {"heads": 0}

    def halo_work():
        head_load(0).start()
        own = pltpu.make_async_copy(r["grads"], window.at[pl.ds(rows, rows)], r["chunk_sem"].at[0])
        own.start()
        pad = rows - rim
        blank = jnp.zeros((pad, window.shape[1]), low)
        window[0:pad] = blank
        window[3 * rows - pad :] = blank

        @pl.when(seq == 0)
        def _():
            window[pad:rows] = jnp.zeros((rim, window.shape[1]), low)

        @pl.when(seq == 7)
        def _():
            window[2 * rows : 2 * rows + rim] = jnp.zeros((rim, window.shape[1]), low)

        back_masks(r["id_col"], r["id_row"], r["own_hide"], r["rim_hide"], rows)
        r["probs"][...] = jnp.zeros(r["probs"].shape, low)
        r["scored"][...] = jnp.zeros(r["scored"].shape, low)
        own.wait()
        pl.when(seq > 0)(halo_up.wait_recv)
        pl.when(seq < 7)(halo_down.wait_recv)
        r["stats"][...] = window[:, features:].astype(jnp.float32)

    def heads_work(count):
        first = done["heads"]
        done["heads"] += count

        def body(h, carry):
            head_load(h).wait()

            @pl.when(h + 1 < HEADS)
            def _():
                head_load(h + 1).start()

            tile = (h * HEAD_DIM) // LANES
            off = h * HEAD_DIM - tile * LANES
            cols = pl.ds(pl.multiple_of(tile * LANES, LANES), 2 * LANES)
            pair = pltpu.roll(window[:, cols].astype(jnp.float32), (2 * LANES - off) % (2 * LANES), 1)
            lane = lanes_of((3 * rows, LANES))
            r["grad_head"][...] = jnp.where(lane < HEAD_DIM, pair[:, :LANES], 0.0).astype(low)
            wide = lanes_of((rows, 2 * LANES))
            inside = (wide >= off) & (wide < off + HEAD_DIM)

            def store(part, at_row, count, value):
                rows_at = pl.ds(at_row, count)
                old = r["triple"][part, rows_at, cols].astype(jnp.float32)
                spread = jnp.concatenate([value, jnp.zeros_like(value)], axis=1)
                moved = pltpu.roll(spread, off, 1)
                r["triple"][part, rows_at, cols] = jnp.where(inside[:count], moved, old).astype(low)

            head = r["head"].at[h % 2]
            back_head(
                h, head.at[0], head.at[1], head.at[2], r["grad_head"], r["stats"], r["own_hide"],
                r["rim_hide"], r["probs"], r["scored"], store,
            )
            return carry

        lax.fori_loop(first, first + count, body, 0)

    sums = r["sums"]

    def pack_work():
        for p in range(3):
            if p != 1:
                row = 3 + p // 2
                sums[row : row + 1] = column_sum(r["triple"][p, :, :features].astype(jnp.float32))
        for b in range(4):
            pieces = []
            for p in range(3):
                low_at, high_at = max(864 * b, features * p), min(864 * (b + 1), features * (p + 1))
                if low_at < high_at:
                    pieces.append(
                        r["triple"][p, :, low_at - features * p : high_at - features * p]
                    )
            pieces.append(jnp.zeros((rows, 32), low))
            value = jnp.concatenate(pieces, axis=1)
            for j, (first, tiles) in enumerate(TRIPLE_TILES):
                width = tiles * LANES
                r[f"triple{j}"][b % 2, 0, :, width * (b // 2) : width * (b // 2 + 1)] = value[
                    :, first * LANES : first * LANES + width
                ]
        for j in range(len(TRIPLE_TILES)):
            swap("right", f"triple{j}", 0)

    chunks = [(p, first, count) for p in range(3) for first, count in ((0, 768), (768, 384))]

    def weight_load(i):
        slot = i % 2
        if i < 6:
            p, first, count = chunks[i]
            src = r["attn_weight"].at[pl.ds(first, count), pl.ds(features * p, features)]
        else:
            count = 768
            src = r["skip_weight"].at[pl.ds(768 * (i - 6), 768)]
        return pltpu.make_async_copy(
            src, r["lefts"].at[slot, pl.ds(0, count)], r["weight_sem"].at[slot]
        )

    def back_work(p):
        if p == 0:
            weight_load(0).start()
        for i in (2 * p, 2 * p + 1):
            _, first, count = chunks[i]
            weight_load(i).wait()
            if i < 5:
                weight_load(i + 1).start()
            part = dot_nt(r["triple"][p, :, :features], r["lefts"][i % 2, :count])
            cols = slice(first, first + count)
            if p == 0:
                r["normed_grad"][:, cols] = part
            else:
                r["normed_grad"][:, cols] += part

    def norm_work():
        gain = r["gain"][...].astype(jnp.float32)
        sums[0:3] = jnp.zeros((3, features), jnp.float32)
        chunk = r["chunk"]
        for i in range(rows // LANES):
            here = pl.ds(i * LANES, LANES)
            copies = [
                pltpu.make_async_copy(r[name].at[here], chunk.at[k], r["chunk_sem"].at[k])
                for k, name in enumerate(("stream", "middle_grad"))
            ]
            for copy in copies:
                copy.start()
            for copy in copies:
                copy.wait()
            unit, scale = row_norm(chunk[0])
            cotangent = r["normed_grad"][here]
            rounded = (chunk[1] + norm_back(unit, scale, gain, cotangent)).astype(low)
            window[here, :features] = rounded
            sums[0:1] += column_sum(rounded.astype(jnp.float32))
            sums[1:2] += column_sum(cotangent * unit)
            sums[2:3] += column_sum(cotangent)
        by_core_store(r["stream_cols"], window[0:rows, :features])
        swap("right", "stream_cols", 0)

    def out_copies():
        return [
            pltpu.make_async_copy(
                r["triple"].at[k, :, pl.ds(0, features)], r[name], r["chunk_sem"].at[k]
            )
            for k, name in enumerate(("out_tok", "out_skp"))
        ]

    def out_work(k):
        i = 6 + k
        if k == 0:
            weight_load(i).start()
        weight_load(i).wait()
        if k < 2:
            weight_load(i + 1).start()
        value = dot_nt(window[0:rows, :features], r["lefts"][i % 2, :768]).astype(low)
        for half in range(2):
            base = features * half
            first, last = max(768 * k, base), min(768 * (k + 1), base + features)
            if first < last:
                r["triple"][half, :, first - base : last - base] = value[
                    :, first - 768 * k : last - 768 * k
                ]
        if k == 2:
            for copy in out_copies():
                copy.start()

    sides = ("core", "x", "y", "pair", "far")

    def vec_work(step):
        vec, land = r["vec"], r["vec_land"]
        if step == 0:
            vec[0] = r["vec_in"][...]
            vec[0, 0:5] = sums[0:5]
        else:
            remote(("vec", step - 1), vec.at[step - 1], land.at[step - 1], sides[step - 1]).wait_recv()
            total = vec[step - 1] + land[step - 1]
            if step == len(sides):
                r["out_vec"][...] = total
            else:
                vec[step] = total
        if step < len(sides):
            remote(("vec", step), vec.at[step], land.at[step], sides[step]).start()

    def start(name):
        i = order.index(name)
        fetch(name, order[i + 1] if i + 1 < len(order) else None)
        if name in LINE_FIRST:
            compute(name, r["line"], LINE_FIRST.index(name))
        else:
            first_stage(started.index(name))

    def third(name):
        third_stage(started.index(name))
        hop(started.index(name), 1)

    steps = {
        "start": start,
        "second": lambda name: second_stage(started.index(name)),
        "third": third,
        "hop": lambda name, step: hop(started.index(name), int(step)),
        "finish": lambda name: finish(started.index(name)),
        "line": lambda name, step, turn: line_hop(name, int(step), int(turn)),
        "line_end": lambda name: line_stage(name, "end"),
        "line_x": lambda name: line_stage(name, "x"),
        "line_y": lambda name: line_stage(name, "y"),
        "halo": halo_work,
        "heads": lambda count: heads_work(int(count)),
        "pack": pack_work,
        "back": lambda p: back_work(int(p)),
        "norm": norm_work,
        "out": lambda k: out_work(int(k)),
        "vec": lambda step: vec_work(int(step)),
    }
    for step in PLAN:
        kind, *rest = step.split()
        steps[kind](*rest)
    for copy in out_copies():
        copy.wait()
    for name in LINE_FIRST:
        line_drain(name)
    for copy in swaps.values():
        copy.wait_send()
    count = len(started)
    for u in range(max(0, count - PART_SLOTS), count):
        wait_sends(u)
    for u in range(max(0, count - LAST_SLOTS), count):
        chain_sends(u)
    for step in range(len(sides)):
        remote(("vec", step), r["vec"].at[step], r["vec_land"].at[step], sides[step]).wait_send()
    pl.when(seq < 7)(halo_up.wait_send)
    pl.when(seq > 0)(halo_down.wait_send)


def gradients(values, vec):
    low, full = jnp.bfloat16, jnp.float32
    rows, features = values["tok"].shape
    names, operands, in_specs, out_shape, out_specs, scratch = [], [], [], [], [], []
    held = ("id_col", "id_row", "gain")
    for name, value in values.items():
        names.append(name)
        operands.append(value)
        in_specs.append(whole() if name in held else anywhere())
    names.append("vec_in")
    operands.append(vec)
    in_specs.append(whole())

    def out(name, shape, dtype, spec):
        names.append(name)
        out_shape.append(jax.ShapeDtypeStruct(shape, dtype))
        out_specs.append(spec)

    for name, shape in GRADS:
        out("out_" + name, shape, full, whole())
    out("out_vec", vec.shape, full, whole())
    out("out_tok", (rows, features), low, anywhere())
    out("out_skp", (rows, features), low, anywhere())
    for name in ("active", "second", "mixed", "normed", "tok", "skp"):
        out("far_" + name, values[name].shape, low, anywhere())
    for name in ("upstream", "hidden", "branch"):
        out("far_" + name, values[name].shape[1:], low, anywhere())
    cores = {f"triple{j}": 2 * LANES * tiles for j, (_, tiles) in enumerate(TRIPLE_TILES)}
    cores["stream_cols"] = 768
    for name, width in cores.items():
        out("far_" + name, (1, rows, width), low, anywhere())

    def add(name, kind):
        names.append(name)
        scratch.append(kind)

    most = 3 * ROWS
    for name, width in cores.items():
        add(name, pltpu.VMEM((2, 1, rows, width), low))
    add("lefts", pltpu.VMEM((2, 2 * rows, features), low))
    add("rights", pltpu.VMEM((2, 2 * rows, 768), low))
    add("left_sem", pltpu.SemaphoreType.DMA((2, 2)))
    add("right_sem", pltpu.SemaphoreType.DMA((2, 2)))
    add("part", pltpu.VMEM((PART_SLOTS, 2, 2, 2, 2, most, LANES), low))
    add("land_one", pltpu.VMEM((FIRST_SLOTS, 2, 2, 2, most, LANES), low))
    add("land_two", pltpu.VMEM((SECOND_SLOTS, 2, 2, most, LANES), low))
    add("ends", pltpu.VMEM((LAST_SLOTS, 2, 2, most, LANES), low))
    chain_at, sizes = {}, {"chain_short": 0, "chain_long": 0}
    for name, unit in make_units().items():
        if name in LINE_FIRST:
            continue
        pool = "chain_short" if unit.rows <= 2 * ROWS + THIRD else "chain_long"
        for (order, place), z_at in unit.z_of.items():
            for up, have in ((True, z_at > 0), (False, z_at < 3)):
                if have:
                    chain_at[name, order, place, up] = (pool, sizes[pool])
                    sizes[pool] += 1
    add("chain_short", pltpu.VMEM((sizes["chain_short"], 2 * ROWS + THIRD, LANES), low))
    add("chain_long", pltpu.VMEM((sizes["chain_long"], most, LANES), low))
    add("sent", pltpu.SemaphoreType.DMA((256,)))
    add("came", pltpu.SemaphoreType.DMA((256,)))
    span = 3 * rows
    add("window", pltpu.VMEM((span, features + LANES), low))
    add("stats", pltpu.VMEM((span, LANES), full))
    add("head", pltpu.VMEM((2, 3, span, LANES), low))
    add("head_sem", pltpu.SemaphoreType.DMA((2,)))
    add("grad_head", pltpu.VMEM((span, LANES), low))
    add("own_hide", pltpu.VMEM((rows // LANES, LANES, span - rows + LANES), low))
    add("rim_hide", pltpu.VMEM((2 * rows // LANES, LANES, rows), low))
    add("probs", pltpu.VMEM((span, rows), low))
    add("scored", pltpu.VMEM((span, rows), low))
    add("triple", pltpu.VMEM((3, rows, features + LANES), low))
    add("weight_sem", pltpu.SemaphoreType.DMA((2,)))
    add("normed_grad", pltpu.VMEM((rows, features), full))
    add("chunk", pltpu.VMEM((2, LANES, features), full))
    add("chunk_sem", pltpu.SemaphoreType.DMA((2,)))
    add("credit", pltpu.SemaphoreType.REGULAR((8,)))
    lines = len(LINE_FIRST)
    line_at = {}
    for name in LINE_FIRST:
        for (order, place), z_at in make_units()[name].z_of.items():
            for up, have in ((True, z_at > 0), (False, z_at < 3)):
                if have:
                    line_at[name, order, place, up] = len(line_at)
    add("line", pltpu.VMEM((lines, 2, 2, 2, 2, most, LANES), low))
    add("line_land", pltpu.VMEM((len(line_at), 2, 2, most, LANES), low))
    add("line_own", pltpu.VMEM((lines, 2, 2, most, LANES), low))
    add("line_x", pltpu.VMEM((lines, 2, most, LANES), low))
    add("line_y", pltpu.VMEM((lines, most, LANES), low))
    add("sums", pltpu.VMEM((8, features), full))
    add("vec", pltpu.VMEM((5, *vec.shape), full))
    add("vec_land", pltpu.VMEM((5, *vec.shape), full))

    def kernel(*refs):
        gradient_kernel(dict(zip(names, refs), chain_at=chain_at, line_at=line_at))

    found = pl.pallas_call(
        kernel,
        out_shape=out_shape,
        in_specs=in_specs,
        out_specs=out_specs,
        scratch_shapes=scratch,
        compiler_params=pltpu.CompilerParams(
            collective_id=0, has_side_effects=True, vmem_limit_bytes=VMEM_MOST
        ),
        name="gradients",
    )(*operands)
    return dict(zip([name for name, _ in GRADS] + ["vec", "tok", "skp"], found))


def unsplit(value):
    blocks = []
    for b in range(4):
        x, c = b // 2, b % 2
        blocks.append(value[c, 0, :, 256 * x : 256 * x + 256])
        blocks.append(value[c, 0, :, 512 + LANES * x : 544 + LANES * x])
    return jnp.concatenate(blocks, axis=1)


def outer_sum(left, right):
    return dot_tn(left, right)


def summed(lefts, rights, vector_list):
    hidden = rights["hidden"]
    _, pieces, rows, width = hidden.shape
    hidden = hidden.reshape(2, pieces, rows, 2, width // 2).transpose(2, 3, 0, 1, 4)
    columns_of = dict(
        joined=unsplit(rights["stream"]),
        normed=rights["triple"],
        mixed=unsplit(rights["branch"]),
        second=hidden.reshape(rows, -1),
        active=unsplit(rights["upstream"]),
    )
    parts = []
    for name in ("joined", "normed", "mixed", "second", "active"):
        gathered = lax.all_gather(lefts[name], "batch", axis=0, tiled=True)
        columns = lax.all_to_all(
            columns_of[name], "batch", split_axis=1, concat_axis=0, tiled=True
        )
        parts.append(outer_sum(gathered, columns).astype(jnp.bfloat16))
    parts = lax.psum_scatter(tuple(parts), "seq", scatter_dimension=0, tiled=True)
    vectors = tuple(
        lax.psum_scatter(vector, ("seq", "batch"), scatter_dimension=0, tiled=True)
        for vector in vector_list
    )
    return tuple(part.astype(jnp.float32) for part in parts), vectors


def rims(value, width):
    size = lax.axis_size("seq")
    up = [(i, i + 1) for i in range(size - 1)]
    down = [(j, i) for i, j in up]
    return (
        lax.ppermute(value[-width:], "seq", up),
        lax.ppermute(value[:width], "seq", down),
    )


def on_device(
    tokens,
    skip_tokens,
    segment_ids,
    upstream,
    skip_weight,
    skip_bias,
    first_gain,
    first_shift,
    attn_weight,
    attn_bias,
    proj_weight,
    proj_bias,
    second_gain,
    second_shift,
    expand_weight,
    expand_bias,
    shrink_weight,
    shrink_bias,
):
    _, rows, features = tokens.shape
    rim = (ITEM_MOST - 1 + 15) // 16 * 16
    tok, skp, above = tokens[0], skip_tokens[0], upstream[0]
    position = lax.axis_index("seq")
    padded_ids = jnp.pad(segment_ids[0], (rows, rows), constant_values=-1)
    window_ids = lax.dynamic_slice_in_dim(padded_ids, position * rows, 3 * rows, 0)
    id_row, id_col = window_ids[None, :], window_ids[:, None]

    stream, normed = stream_norm(tok, skp, skip_weight, skip_bias, first_gain, first_shift)
    before, after = rims(normed, rim)
    own = own_heads(normed, attn_weight, attn_bias)
    wins, mixed, lse = attend(own, before, after, attn_weight, attn_bias, id_col, id_row)
    (
        result, active, hidden_by_core, second, branch, branch_by_core, up_by_core, middle_grad,
        mixed_grad, hidden_sum, sums,
    ) = layer(
        stream, mixed, lse, above,
        (
            proj_weight, proj_bias, second_gain, second_shift, expand_weight, expand_bias,
            shrink_weight, shrink_bias,
        ),
    )
    if lax.axis_size("seq") == 8 and lax.axis_size("batch") == 4:
        vec = jnp.concatenate(
            [
                jnp.zeros((5, features), jnp.float32),
                sums[:4],
                hidden_sum.reshape(-1, features),
                jnp.zeros((3, features), jnp.float32),
            ],
            axis=0,
        )
        found = gradients(
            dict(
                active=active, second=second, mixed=mixed, normed=normed, tok=tok, skp=skp,
                upstream=up_by_core, hidden=hidden_by_core, branch=branch_by_core, wins=wins,
                grads=mixed_grad, id_col=id_col, id_row=id_row, stream=stream,
                middle_grad=middle_grad, gain=first_gain[None], attn_weight=attn_weight,
                skip_weight=skip_weight,
            ),
            vec,
        )
        tok_grad, skip_grad = found["tok"], found["skp"]
        weight_parts = (
            found["skip"], found["attn"][:, :864], found["proj"], found["expand"], found["shrink"]
        )
        total = found["vec"]
        place = position * lax.axis_size("batch") + lax.axis_index("batch")

        def mine(first, count):
            part = total[first : first + count].reshape(-1)
            width = part.shape[0] // 32
            return lax.dynamic_slice_in_dim(part, place * width, width, 0)

        vectors = (
            mine(0, 1), mine(1, 1), mine(2, 1), mine(3, 2), mine(5, 1), mine(6, 1), mine(7, 1),
            mine(9, 4), mine(8, 1),
        )
    else:
        before, after = rims(mixed_grad, rim)
        blank = jnp.zeros((rows - rim, mixed_grad.shape[1]), mixed_grad.dtype)
        grad_window = jnp.concatenate([blank, before, mixed_grad, after, blank], axis=0)
        stats = grad_window[:, features:].astype(jnp.float32)
        triple, triple_sum = attend_back(wins, grad_window, stats, id_col, id_row)
        tok_grad, skip_grad, stream_by_core, stream_sums = stream_back(
            triple, attn_weight, stream, middle_grad, first_gain, skip_weight
        )
        vector_list = (
            stream_sums[2],
            stream_sums[0],
            stream_sums[1],
            jnp.concatenate([triple_sum[0, :features], triple_sum[0, 2 * features :]]),
            sums[0],
            sums[1],
            sums[2],
            hidden_sum[0],
            sums[3],
        )
        joined = jnp.concatenate([tok, skp], axis=1)
        weight_parts, vectors = summed(
            dict(active=active, second=second, mixed=mixed, normed=normed, joined=joined),
            dict(
                upstream=up_by_core,
                hidden=hidden_by_core,
                branch=branch_by_core,
                triple=triple,
                stream=stream_by_core,
            ),
            vector_list,
        )
    return (
        result[None],
        tok_grad[None],
        skip_grad[None],
        weight_parts[0],
        vectors[0],
        vectors[1],
        vectors[2],
        weight_parts[1],
        vectors[3],
        weight_parts[2],
        vectors[4],
        vectors[5],
        vectors[6],
        weight_parts[3],
        vectors[7],
        weight_parts[4],
        vectors[8],
    )


def solution(mesh):
    in_specs = (
        P("batch", "seq", None),
        P("batch", "seq", None),
        P("batch", None),
        P("batch", "seq", None),
        P(),
        P(),
        P(),
        P(),
        P(),
        P(),
        P(),
        P(),
        P(),
        P(),
        P(),
        P(),
        P(),
        P(),
    )
    out_specs = (
        P("batch", "seq", None),
        P("batch", "seq", None),
        P("batch", "seq", None),
        P("seq", "batch"),
        P(("seq", "batch")),
        P(("seq", "batch")),
        P(("seq", "batch")),
        P("seq", "batch"),
        P(("seq", "batch")),
        P("seq", "batch"),
        P(("seq", "batch")),
        P(("seq", "batch")),
        P(("seq", "batch")),
        P("seq", "batch"),
        P(("seq", "batch")),
        P("seq", "batch"),
        P(("seq", "batch")),
    )
    return jax.shard_map(
        on_device, mesh=mesh, in_specs=in_specs, out_specs=out_specs, check_vma=False
    )
```

```python
import jax
import jax.numpy as jnp
from jax import lax
from jax.experimental import pallas as pl
from jax.experimental.pallas import tpu as pltpu
from jax.sharding import PartitionSpec as P

HEADS = 16
HEAD_DIM = 72
ITEM_MOST = 322
LANES = 128
MESH = pl.DeviceIdType.MESH
SCALE2 = HEAD_DIM**-0.5 * 1.4426950408889634
VMEM_MOST = 60 * 2**20


ROOT2 = 2.0**0.5


def dot(left, right):
    return jnp.dot(left, right, preferred_element_type=jnp.float32)


def dot_nt(left, right):
    return lax.dot_general(
        left, right, (((1,), (1,)), ((), ())), preferred_element_type=jnp.float32
    )


def dot_tn(left, right):
    return lax.dot_general(
        left, right, (((0,), (0,)), ((), ())), preferred_element_type=jnp.float32
    )


def vector(ref, first=0, count=None):
    count = ref.shape[0] if count is None else count
    return ref[pl.ds(first, count)].astype(jnp.float32).reshape(1, count)


def whole():
    return pl.BlockSpec(memory_space=pltpu.VMEM)


def anywhere():
    return pl.BlockSpec(memory_space=pl.ANY)


def params():
    return pltpu.CompilerParams(vmem_limit_bytes=60 * 2**20)


def erf(value):
    v = jnp.clip(value, -3.832506856900711, 3.832506856900711)
    s = v * v
    top = 0.00022905065861350646
    for a in (0.0034082910107109506, 0.050955695062380861, 0.18520832239976145, 1.128379143519084):
        top = top * s + a
    low = -1.1791602954361697e-7
    for a in (0.000023547966471313185, 0.0010179625278914885, 0.014070470171167667):
        low = low * s + a
    low = (low * s + 0.11098505178285362) * s + 0.49746925110067538
    return v * top / (low * s + 1.0)


def row_norm(value):
    centred = value - jnp.mean(value, axis=-1, keepdims=True)
    scale = lax.rsqrt(jnp.mean(centred * centred, axis=-1, keepdims=True) + 1e-05)
    return centred * scale, scale


def norm_back(unit, scale, gain, cotangent):
    inner = cotangent * gain
    mean = jnp.mean(inner, axis=-1, keepdims=True)
    along = jnp.mean(inner * unit, axis=-1, keepdims=True)
    return scale * (inner - mean - unit * along)


def column_sum(value):
    return jnp.sum(value, axis=0, keepdims=True)


def stream_kernel(tok, skp, weight, bias, gain, shift, stream, normed, held, sems):
    copies = [
        pltpu.make_async_copy(weight.at[:, pl.ds(384 * n, 384)], held.at[n], sems.at[n])
        for n in range(3)
    ]
    for copy in copies:
        copy.start()
    features = tok.shape[1]
    for n, copy in enumerate(copies):
        copy.wait()
        at = slice(384 * n, 384 * n + 384)
        stream[:, at] = (
            dot(tok[...], held[n, :features])
            + dot(skp[...], held[n, features:])
            + vector(bias, 384 * n, 384)
        )
    unit, _ = row_norm(stream[...])
    normed[...] = (unit * vector(gain) + vector(shift)).astype(jnp.bfloat16)


def stream_norm(tok, skp, weight, bias, gain, shift):
    rows, features = tok.shape
    return pl.pallas_call(
        stream_kernel,
        out_shape=(
            jax.ShapeDtypeStruct((rows, features), jnp.float32),
            jax.ShapeDtypeStruct((rows, features), jnp.bfloat16),
        ),
        in_specs=[whole(), whole(), anywhere(), whole(), whole(), whole()],
        out_specs=(whole(), whole()),
        scratch_shapes=[
            pltpu.VMEM((3, 2 * features, 384), jnp.bfloat16),
            pltpu.SemaphoreType.DMA((3,)),
        ],
        compiler_params=params(),
        cost_estimate=pl.CostEstimate(
            flops=4 * rows * features * features, bytes_accessed=10**7, transcendentals=0
        ),
        name="stream_norm",
    )(tok, skp, weight, bias, gain, shift)


MARKS = (HEAD_DIM, HEAD_DIM + 16, HEAD_DIM + 32)


def lanes_of(shape):
    return lax.broadcasted_iota(jnp.int32, shape, len(shape) - 1)


def marked(lane):
    return (lane == MARKS[0]) | (lane == MARKS[1]) | (lane == MARKS[2])


def head_tile(value, h, ones):
    rows = value.shape[0]
    lane = lanes_of((rows, LANES - HEAD_DIM)) + HEAD_DIM
    rest = jnp.where(marked(lane) & ones, 1.0, 0.0).astype(value.dtype)
    return jnp.concatenate([value[:, HEAD_DIM * h : HEAD_DIM * (h + 1)], rest], axis=1)


def project(rows_ref, weight_ref, bias, part, store):
    features = rows_ref.shape[1]
    value = dot(rows_ref[...], weight_ref[...])
    if part != 1:
        at = 0 if part == 0 else features
        value = value + vector(bias, at, features)
    value = value.astype(jnp.bfloat16)
    for h in range(HEADS):
        store(part, h, head_tile(value, h, part > 0))


def project_kernel(normed, weight, bias, out, held, sems):
    features = normed.shape[1]
    copies = [
        pltpu.make_async_copy(weight.at[:, pl.ds(features * p, features)], held.at[p], sems.at[p])
        for p in range(3)
    ]
    for copy in copies:
        copy.start()

    def store(part, h, value):
        out[part, h] = value

    for p, copy in enumerate(copies):
        copy.wait()
        project(normed, held.at[p], bias, p, store)


def own_heads(normed, weight, bias):
    rows, features = normed.shape
    return pl.pallas_call(
        project_kernel,
        out_shape=jax.ShapeDtypeStruct((3, HEADS, rows, LANES), jnp.bfloat16),
        in_specs=[whole(), anywhere(), whole()],
        out_specs=whole(),
        scratch_shapes=[
            pltpu.VMEM((3, features, features), jnp.bfloat16),
            pltpu.SemaphoreType.DMA((3,)),
        ],
        compiler_params=params(),
        cost_estimate=pl.CostEstimate(
            flops=6 * rows * features * features, bytes_accessed=2 * 10**7, transcendentals=0
        ),
        name="own_heads",
    )(normed, weight, bias)


HIDE = -1e30


def attend_kernel(own, before, after, weight, bias, id_col, id_row, wins, mixed, lse, *scratch):
    window, halo, held, hide, gathered, sems, out_sems = scratch
    rim, features = before.shape
    rows = own.shape[2]
    span = 3 * rows
    copies = [
        pltpu.make_async_copy(weight.at[:, pl.ds(features * p, features)], held.at[p], sems.at[p])
        for p in range(3)
    ]
    copies.append(pltpu.make_async_copy(own, window.at[:, :, pl.ds(rows, rows)], sems.at[3]))
    for copy in copies:
        copy.start()
    pad = rows - rim
    window[:, :, 0:pad] = jnp.zeros((3, HEADS, pad, LANES), jnp.bfloat16)
    window[:, :, span - pad : span] = jnp.zeros((3, HEADS, pad, LANES), jnp.bfloat16)
    halo[0:rim] = before[...]
    halo[rim:] = after[...]

    def store(part, h, value):
        window[part, h, pad:rows] = value[:rim]
        window[part, h, 2 * rows : 2 * rows + rim] = value[rim:]

    for p in (1, 2, 0):
        copies[p].wait()
        project(halo, held.at[p], bias, p, store)
    copies[3].wait()
    out_copies = [
        pltpu.make_async_copy(window.at[p], wins.at[p], out_sems.at[p]) for p in range(3)
    ]
    for copy in out_copies:
        copy.start()
    blocks = rows // LANES
    reach = span - (blocks - 1) * LANES
    for i in range(blocks):
        same = id_col[rows + i * LANES : rows + (i + 1) * LANES] == (
            id_row[:, i * LANES : i * LANES + reach]
        )
        hide[i] = jnp.where(same, 0.0, HIDE)
    lse[...] = jnp.zeros_like(lse)

    def body(pair, carry):
        jobs = [(2 * pair + k, i) for k in range(2) for i in range(blocks)]
        scores = [
            dot_nt(
                window[0, h, rows + i * LANES : rows + (i + 1) * LANES],
                window[1, h, pl.ds(i * LANES, reach)],
            )
            * SCALE2
            + hide[i]
            for h, i in jobs
        ]
        highest = [jnp.max(value, axis=-1, keepdims=True) for value in scores]
        raised = [
            jnp.exp2(value - most).astype(jnp.bfloat16) for value, most in zip(scores, highest)
        ]
        totals = [
            dot(value, window[2, h, pl.ds(i * LANES, reach)]) for value, (h, i) in zip(raised, jobs)
        ]
        for total, most, (h, i) in zip(totals, highest, jobs):
            at = slice(i * LANES, (i + 1) * LANES)
            denominator = total[:, HEAD_DIM : HEAD_DIM + 1]
            gathered[h, at] = total / denominator
            value = most + jnp.log2(denominator)
            lse[at] = jnp.where(lanes_of((LANES, LANES)) == h, value, lse[at])
        return carry

    lax.fori_loop(0, HEADS // 2, body, 0)
    for h in range(HEADS):
        mixed[:, HEAD_DIM * h : HEAD_DIM * (h + 1)] = gathered[h, :, :HEAD_DIM].astype(jnp.bfloat16)
    for copy in out_copies:
        copy.wait()


def attend(own, before, after, weight, bias, id_col, id_row):
    rim, features = before.shape
    rows = own.shape[2]
    span = 3 * rows
    return pl.pallas_call(
        attend_kernel,
        out_shape=(
            jax.ShapeDtypeStruct((3, HEADS, span, LANES), jnp.bfloat16),
            jax.ShapeDtypeStruct((rows, features), jnp.bfloat16),
            jax.ShapeDtypeStruct((rows, LANES), jnp.float32),
        ),
        in_specs=[anywhere(), whole(), whole(), anywhere(), whole(), whole(), whole()],
        out_specs=(anywhere(), whole(), whole()),
        scratch_shapes=[
            pltpu.VMEM((3, HEADS, span, LANES), jnp.bfloat16),
            pltpu.VMEM((2 * rim, features), jnp.bfloat16),
            pltpu.VMEM((3, features, features), jnp.bfloat16),
            pltpu.VMEM((rows // LANES, LANES, span - rows + LANES), jnp.float32),
            pltpu.VMEM((HEADS, rows, LANES), jnp.float32),
            pltpu.SemaphoreType.DMA((4,)),
            pltpu.SemaphoreType.DMA((3,)),
        ],
        compiler_params=params(),
        name="attend",
    )(own, before, after, weight, bias, id_col, id_row)


def by_core_store(ref, value):
    blank = jnp.zeros((value.shape[0], 32), value.dtype)
    for b in range(4):
        x, c = b // 2, b % 2
        ref[c, 0, :, 256 * x : 256 * x + 256] = value[:, 288 * b : 288 * b + 256]
        rest = value[:, 288 * b + 256 : 288 * b + 288]
        ref[c, 0, :, 512 + LANES * x : 640 + LANES * x] = jnp.concatenate(
            [rest, rest, rest, blank], axis=1
        )


def split3(value):
    first = value.astype(jnp.bfloat16)
    rest = value - first.astype(jnp.float32)
    second = rest.astype(jnp.bfloat16)
    return first, second, (rest - second.astype(jnp.float32)).astype(jnp.bfloat16)


def layer_kernel(
    stream, mixed, lse, upstream, proj, proj_bias, gain, shift, expand, expand_bias, shrink,
    shrink_bias, result, active, hidden_by_core, second, branch, branch_by_core, up_by_core,
    middle_grad, mixed_grad, sums, middle, total, second_grad,
    bias_rows,
):
    step, steps = pl.program_id(0), pl.num_programs(0)
    low = jnp.bfloat16
    wide = expand.shape[1]

    @pl.when(step == 0)
    def _():
        middle[...] = (
            stream[...] + dot(mixed[...], proj[...]) + vector(proj_bias)
        )
        unit, _ = row_norm(middle[...])
        second[...] = (unit * vector(gain) + vector(shift)).astype(low)
        total[...] = middle[...] + vector(shrink_bias)
        second_grad[...] = jnp.zeros_like(second_grad)
        for t in range(4):
            bias_rows[t : t + 1] = vector(expand_bias, wide * t, wide)
        by_core_store(up_by_core, upstream[...])

    hidden = dot(second[...], expand[...]) + bias_rows[pl.ds(step, 1)]
    active_grad = dot_nt(upstream[...], shrink[...])
    cdf = 0.5 + 0.5 * erf(hidden * (1.0 / ROOT2))
    density = jnp.exp(-0.5 * hidden * hidden) * 0.3989422804014327
    raised = (hidden * cdf).astype(low)
    active[...] = raised
    hidden_grad = (active_grad * (cdf + hidden * density)).astype(low)
    for j in range(3):
        hidden_by_core[0, j] = hidden_grad[:, 384 * j : 384 * (j + 1)]
    for t in range(4):

        @pl.when(step == t)
        def _():
            sums[9 + t : 10 + t] = column_sum(hidden_grad.astype(jnp.float32))

    total[...] += dot(raised, shrink[...])
    second_grad[...] += dot_nt(hidden_grad, expand[...])

    @pl.when(step == steps - 1)
    def _():
        result[...] = total[...].astype(low)
        unit, scale = row_norm(middle[...])
        cotangent = second_grad[...]
        above = upstream[...].astype(jnp.float32)
        grad = above + norm_back(unit, scale, vector(gain), cotangent)
        middle_grad[...] = grad
        branched = grad.astype(low)
        branch[...] = branched
        by_core_store(branch_by_core, branched)
        sums[0:5] = jnp.zeros((5, sums.shape[1]), jnp.float32)
        sums[5:6] = column_sum(branched.astype(jnp.float32))
        sums[6:7] = column_sum(cotangent * unit)
        sums[7:8] = column_sum(cotangent)
        sums[8:9] = column_sum(above)
        sums[13:16] = jnp.zeros((3, sums.shape[1]), jnp.float32)
        back = dot_nt(branched, proj[...]).astype(low)
        features = back.shape[1]
        mixed_grad[:, :features] = back
        products = back.astype(jnp.float32) * mixed[...].astype(jnp.float32)
        shape = (features, LANES)
        member = lax.broadcasted_iota(jnp.int32, shape, 0) // HEAD_DIM == lanes_of(shape)
        member = jnp.where(member, 1.0, 0.0).astype(low)
        high = products.astype(low)
        inner = dot(high, member) + dot((products - high.astype(jnp.float32)).astype(low), member)
        pieces = [part[:, :HEADS] for part in split3(lse[...] * (-1.0 / SCALE2)) + split3(-inner)]
        blank = jnp.zeros((back.shape[0], LANES - 6 * HEADS), low)
        mixed_grad[:, features:] = jnp.concatenate(pieces + [blank], axis=1)


def layer(stream, mixed, lse, upstream, weights):
    proj, proj_bias, gain, shift, expand, expand_bias, shrink, shrink_bias = weights
    rows, features = stream.shape
    hidden = expand.shape[1]
    wide = hidden // 4
    low = jnp.bfloat16

    def held(shape):
        return pl.BlockSpec(shape, lambda t: (0,) * len(shape))

    narrow = (rows, features)
    split = (2, 1, rows, 768)
    return pl.pallas_call(
        layer_kernel,
        grid=(4,),
        in_specs=[
            held(narrow), held(narrow), held((rows, LANES)), held(narrow),
            held((features, features)), whole(), whole(), whole(),
            pl.BlockSpec((features, wide), lambda t: (0, t)),
            whole(),
            pl.BlockSpec((wide, features), lambda t: (t, 0)),
            whole(),
        ],
        out_specs=(
            held(narrow),
            pl.BlockSpec((rows, wide), lambda t: (0, t)),
            pl.BlockSpec((1, 3, rows, 384), lambda t: (t % 2, 0, 0, t // 2)),
            held(narrow), held(narrow), held(split), held(split), held(narrow),
            held((rows, features + LANES)),
            held((16, features)),
        ),
        out_shape=(
            jax.ShapeDtypeStruct(narrow, low),
            jax.ShapeDtypeStruct((rows, hidden), low),
            jax.ShapeDtypeStruct((2, 3, rows, 768), low),
            jax.ShapeDtypeStruct(narrow, low),
            jax.ShapeDtypeStruct(narrow, low),
            jax.ShapeDtypeStruct(split, low),
            jax.ShapeDtypeStruct(split, low),
            jax.ShapeDtypeStruct(narrow, jnp.float32),
            jax.ShapeDtypeStruct((rows, features + LANES), low),
            jax.ShapeDtypeStruct((16, features), jnp.float32),
        ),
        scratch_shapes=[pltpu.VMEM(narrow, jnp.float32)] * 3
        + [pltpu.VMEM((4, wide), jnp.float32)],
        compiler_params=params(),
        name="layer",
    )(
        stream, mixed, lse, upstream, proj, proj_bias, gain, shift, expand, expand_bias, shrink,
        shrink_bias,
    )


def back_masks(id_col, id_row, own_hide, rim_hide, rows):
    blocks = rows // LANES
    reach = own_hide.shape[2]

    def hidden(first, keys, width):
        same = id_col[first : first + LANES] == id_row[:, keys : keys + width]
        return jnp.where(same, 0.0, HIDE).astype(own_hide.dtype)

    for i in range(blocks):
        own_hide[i] = hidden(rows + i * LANES, i * LANES, reach)
    for w in range(blocks):
        rim_hide[w] = hidden(w * LANES, rows, rows)
        rim_hide[blocks + w] = hidden(2 * rows + w * LANES, rows, rows)


def with_stats(value, stats, shift):
    return jnp.where(marked(lanes_of(value.shape)), pltpu.roll(stats, shift, 1), value)


def back_head(h, queries, keys, values, grads, stats, own_hide, rim_hide, probs, scored):
    span = queries.shape[0]
    rows = span // 3
    blocks = rows // LANES
    reach = span - rows + LANES
    low, full = jnp.bfloat16, jnp.float32
    queries[...] = with_stats(queries[...], stats, MARKS[0] - h)
    turn = MARKS[0] - 3 * HEADS - h
    grads[...] = with_stats(grads[...], stats, jnp.where(turn < 0, turn + LANES, turn))
    jobs = []
    for i in range(blocks):
        jobs.append(
            (rows + i * LANES, i * LANES, reach, own_hide[i], rows - i * LANES, rows, 0)
        )
    for w in range(blocks):
        width = (w + 1) * LANES
        jobs.append((w * LANES, rows, width, rim_hide[w][:, :width], 0, width, 0))
        first, width = w * LANES, rows - w * LANES
        hide = rim_hide[blocks + w][:, first:]
        jobs.append((2 * rows + first, rows + first, width, hide, 0, width, first))
    scores = [dot_nt(queries[q : q + LANES], keys[k : k + n]) for q, k, n, *_ in jobs]
    inner = [dot_nt(grads[q : q + LANES], values[k : k + n]) for q, k, n, *_ in jobs]
    weights = [
        jnp.exp2(value * SCALE2 + job[3].astype(full)) for value, job in zip(scores, jobs)
    ]
    scores = [(weight * value).astype(low) for weight, value in zip(weights, inner)]
    weights = [weight.astype(low) for weight in weights]
    for weight, score, (q, _, _, _, first, count, place) in zip(weights, scores, jobs):
        probs[q : q + LANES, place : place + count] = weight[:, first : first + count]
        scored[q : q + LANES, place : place + count] = score[:, first : first + count]
    factor = HEAD_DIM**-0.5
    query_grad = jnp.concatenate(
        [dot(scores[i], keys[i * LANES : i * LANES + reach]) * factor for i in range(blocks)], axis=0
    )
    key_grad = dot_tn(scored[...], queries[...]) * factor
    value_grad = dot_tn(probs[...], grads[...])
    return query_grad.astype(low), key_grad.astype(low), value_grad.astype(low)


def heads_apart(row_ref, out):
    value = row_ref[...]
    for h in range(HEADS):
        out[h] = head_tile(value[:, : HEADS * HEAD_DIM], h, False)


def triple_store(apart, triple):
    features = HEADS * HEAD_DIM
    for p in range(3):
        for h in range(HEADS):
            at = features * p + HEAD_DIM * h
            triple[:, at : at + HEAD_DIM] = apart[p, h, :, :HEAD_DIM]


def attend_back_kernel(
    wins, grads_in, stats, id_col, id_row, triple, sums,
    window, grads, own_hide, rim_hide, probs, scored, apart, sems,
):
    span = window.shape[2]
    rows = span // 3
    copy = pltpu.make_async_copy(wins, window, sems.at[0])
    copy.start()
    back_masks(id_col, id_row, own_hide, rim_hide, rows)
    probs[...] = jnp.zeros_like(probs)
    scored[...] = jnp.zeros_like(scored)
    heads_apart(grads_in, grads)
    copy.wait()

    def body(h, carry):
        found = back_head(
            h, window.at[0, h], window.at[1, h], window.at[2, h], grads.at[h], stats[...],
            own_hide, rim_hide, probs, scored,
        )
        for part, value in enumerate(found):
            apart[part, h] = value
        return carry

    lax.fori_loop(0, HEADS, body, 0)
    triple_store(apart, triple)
    sums[...] = column_sum(triple[...].astype(jnp.float32))


def attend_back(wins, grads_in, stats, id_col, id_row):
    span = wins.shape[2]
    rows = span // 3
    features = HEADS * HEAD_DIM
    low = jnp.bfloat16
    return pl.pallas_call(
        attend_back_kernel,
        out_shape=(
            jax.ShapeDtypeStruct((rows, 3 * features), low),
            jax.ShapeDtypeStruct((1, 3 * features), jnp.float32),
        ),
        in_specs=[anywhere(), whole(), whole(), whole(), whole()],
        out_specs=(whole(), whole()),
        scratch_shapes=[
            pltpu.VMEM((3, HEADS, span, LANES), low),
            pltpu.VMEM((HEADS, span, LANES), low),
            pltpu.VMEM((rows // LANES, LANES, span - rows + LANES), low),
            pltpu.VMEM((2 * rows // LANES, LANES, rows), low),
            pltpu.VMEM((span, rows), low),
            pltpu.VMEM((span, rows), low),
            pltpu.VMEM((3, HEADS, rows, LANES), low),
            pltpu.SemaphoreType.DMA((1,)),
        ],
        compiler_params=params(),
        name="attend_back",
    )(wins, grads_in, stats, id_col, id_row)


def stream_back_kernel(
    triple, weight, stream, middle_grad, gain, skip_weight, tok_grad, skip_grad, by_core, sums, held, held_skip, grad, sems,
):
    features = stream.shape[1]
    low = jnp.bfloat16
    copies = [
        pltpu.make_async_copy(weight.at[:, pl.ds(features * p, features)], held.at[p], sems.at[p])
        for p in range(3)
    ]
    copies += [
        pltpu.make_async_copy(
            skip_weight.at[pl.ds(features * p, features)], held_skip.at[p], sems.at[3 + p]
        )
        for p in range(2)
    ]
    for copy in copies:
        copy.start()
    unit, scale = row_norm(stream[...])
    for p in range(3):
        copies[p].wait()
        part = dot_nt(triple[:, features * p : features * (p + 1)], held[p])
        if p == 0:
            grad[...] = part
        else:
            grad[...] += part
    cotangent = grad[...]
    sums[0:1] = column_sum(cotangent * unit)
    sums[1:2] = column_sum(cotangent)
    whole_grad = middle_grad[...] + norm_back(unit, scale, vector(gain), cotangent)
    rounded = whole_grad.astype(low)
    by_core_store(by_core, rounded)
    sums[2:3] = column_sum(rounded.astype(jnp.float32))
    for p, out in enumerate((tok_grad, skip_grad)):
        copies[3 + p].wait()
        out[...] = dot_nt(rounded, held_skip[p]).astype(low)


def stream_back(triple, weight, stream, middle_grad, gain, skip_weight):
    rows, features = stream.shape
    low = jnp.bfloat16
    return pl.pallas_call(
        stream_back_kernel,
        out_shape=(
            jax.ShapeDtypeStruct((rows, features), low),
            jax.ShapeDtypeStruct((rows, features), low),
            jax.ShapeDtypeStruct((2, 1, rows, 768), low),
            jax.ShapeDtypeStruct((8, features), jnp.float32),
        ),
        in_specs=[whole(), anywhere(), whole(), whole(), whole(), anywhere()],
        out_specs=(whole(), whole(), whole(), whole()),
        scratch_shapes=[
            pltpu.VMEM((3, features, features), low),
            pltpu.VMEM((2, features, features), low),
            pltpu.VMEM((rows, features), jnp.float32),
            pltpu.SemaphoreType.DMA((5,)),
        ],
        compiler_params=params(),
        name="stream_back",
    )(triple, weight, stream, middle_grad, gain, skip_weight)


ROWS = 144
THIRD = ROWS // 3


class Unit:
    def __init__(self, left, left_at, right, right_at, tiles, blocks, out, out_at):
        self.left, self.left_at = left, left_at
        self.right, self.right_at = right, right_at
        self.tiles = tiles
        self.blocks = blocks
        self.out, self.out_at = out, out_at
        self.rows = ROWS * tiles if tiles else 2 * ROWS + THIRD
        self.z_of = {(order, place): z for _, order, _, place, z in blocks}


ORDER_OF = (0, 1, 1, 0)
QUARTERS = tuple(
    ((2 * z + y) * ROWS, ORDER_OF[z], y, z // 2, z) for z in range(4) for y in range(2)
)


SHRINK, EXPAND, PROJ, ATTN, SKIP = (0, 1, 2, 3), (4, 5, 6), 7, (8, 9, 10), (11, 12)
START, TURN, SETTLE, HOP, FINISH, LINE, LINE_END, LINE_X, LINE_Y = range(9)
HALO, HEAD, PACK, BACK, NORM, OUT, VECTOR = range(9, 16)


def make_units():
    units = {}
    for z in range(4):
        blocks = [
            (y * 576 + q * ROWS, q // 2, y, q % 2, z) for y in range(2) for q in range(4)
        ]
        units[SHRINK[z]] = Unit("active", z * 1152, "upstream", 0, 0, blocks, "shrink", 0)
    for j in range(3):
        units[EXPAND[j]] = Unit("second", 0, "hidden", j, 3, QUARTERS, "expand", 3 * j)
    units[PROJ] = Unit("mixed", 0, "branch", 0, 0, QUARTERS, "proj", 0)
    for j, (first, tiles) in enumerate(TRIPLE_TILES):
        units[ATTN[j]] = Unit("normed", 0, f"triple{j}", 0, tiles, QUARTERS, "attn", first)
    for k, name in enumerate(("tok", "skp")):
        blocks = [
            (h * 576 + y * 288 + i * ROWS, h, y, i, 2 * k + h)
            for h in range(2)
            for y in range(2)
            for i in range(2)
        ]
        units[SKIP[k]] = Unit(name, 0, "stream_cols", 0, 0, blocks, "skip", 0)
    return units


TRIPLE_TILES = ((0, 3), (3, 2), (5, 2))
GRADS = (
    ("shrink", (576, 288)),
    ("expand", (144, 1152)),
    ("proj", (144, 288)),
    ("attn", (144, 864)),
    ("skip", (288, 288)),
)
PART_SLOTS, FIRST_SLOTS, SECOND_SLOTS, LAST_SLOTS = 4, 4, 4, 5
LINE_FIRST = (EXPAND[0], ATTN[0])
X_FIRST = (SHRINK[0], SHRINK[1], SHRINK[2], SHRINK[3])
PLAN = (
    (START, SHRINK[0]), (START, EXPAND[0]), (LINE, EXPAND[0], 1, 0), (LINE, EXPAND[0], 1, 1),
    (LINE, EXPAND[0], 1, 2), (START, SHRINK[3]), (START, SHRINK[1]), (START, SHRINK[2]),
    (LINE, EXPAND[0], 2, 0), (TURN, SHRINK[0]), (TURN, SHRINK[3]), (LINE, EXPAND[0], 2, 1),
    (LINE, EXPAND[0], 3, 0), (HALO,), (HEAD, 4), (SETTLE, SHRINK[0]), (START, EXPAND[1]),
    (TURN, SHRINK[1]), (LINE_END, EXPAND[0]), (HEAD, 2), (SETTLE, SHRINK[3]), (HOP, SHRINK[0], 2),
    (START, EXPAND[2]), (HEAD, 2), (TURN, SHRINK[2]), (HOP, SHRINK[0], 3), (HOP, SHRINK[3], 2),
    (HEAD, 4), (TURN, EXPAND[1]), (SETTLE, SHRINK[1]), (HOP, SHRINK[3], 3), (START, PROJ),
    (FINISH, SHRINK[0]), (LINE_X, EXPAND[0]), (HEAD, 2), (HOP, SHRINK[1], 2), (HOP, SHRINK[1], 3),
    (HEAD, 2), (TURN, EXPAND[2]), (SETTLE, SHRINK[2]), (FINISH, SHRINK[3]), (PACK,), (START, ATTN[0]),
    (SETTLE, EXPAND[1]), (START, ATTN[1]), (HOP, SHRINK[2], 2), (START, ATTN[2]), (TURN, PROJ),
    (LINE_Y, EXPAND[0]), (HOP, EXPAND[1], 2), (HOP, SHRINK[2], 3), (LINE, ATTN[0], 1, 0),
    (LINE, ATTN[0], 1, 1), (LINE, ATTN[0], 1, 2), (FINISH, SHRINK[1]), (BACK, 0), (SETTLE, EXPAND[2]),
    (FINISH, SHRINK[2]), (BACK, 1), (HOP, EXPAND[1], 3), (BACK, 2), (TURN, ATTN[1]),
    (LINE, ATTN[0], 2, 0), (FINISH, EXPAND[1]), (NORM,), (TURN, ATTN[2]), (START, SKIP[0]),
    (SETTLE, PROJ), (START, SKIP[1]), (LINE, ATTN[0], 2, 1), (LINE, ATTN[0], 3, 0), (SETTLE, ATTN[1]),
    (VECTOR, 0), (OUT, 0), (SETTLE, ATTN[2]), (VECTOR, 1), (OUT, 1), (OUT, 2), (TURN, SKIP[0]),
    (HOP, EXPAND[2], 2), (LINE_END, ATTN[0]), (HOP, EXPAND[2], 3), (TURN, SKIP[1]), (HOP, PROJ, 2),
    (VECTOR, 2), (FINISH, EXPAND[2]), (HOP, ATTN[1], 2), (HOP, PROJ, 3), (HOP, ATTN[1], 3),
    (HOP, ATTN[2], 2), (HOP, ATTN[2], 3), (SETTLE, SKIP[0]), (HOP, SKIP[0], 2), (SETTLE, SKIP[1]),
    (VECTOR, 3), (FINISH, PROJ), (LINE_X, ATTN[0]), (FINISH, ATTN[1]), (FINISH, ATTN[2]),
    (HOP, SKIP[0], 3), (HOP, SKIP[1], 2), (HOP, SKIP[1], 3), (LINE_Y, ATTN[0]), (FINISH, SKIP[0]),
    (VECTOR, 4), (FINISH, SKIP[1]), (VECTOR, 5),
)


def add_into(target, other):
    target[...] = (target[...].astype(jnp.float32) + other[...].astype(jnp.float32)).astype(
        target.dtype
    )


def gradient_kernel(r):
    seq, batch = lax.axis_index("seq"), lax.axis_index("batch")
    z, y = seq // 2, seq % 2
    x, c = batch // 2, batch % 2
    at = {
        "core": (seq, 2 * x + (1 - c)),
        "x": (seq, 2 * (1 - x) + c),
        "y": (2 * z + (1 - y), batch),
        "above": (2 * jnp.minimum(z + 1, 3) + y, batch),
        "below": (2 * jnp.maximum(z - 1, 0) + y, batch),
        "far": (2 * ((z + 2) % 4) + y, batch),
        "next": (jnp.minimum(seq + 1, 7), batch),
        "last": (jnp.maximum(seq - 1, 0), batch),
    }
    at["pair"] = (2 * (z + 1 - 2 * (z % 2)) + y, batch)
    units = make_units()
    low = jnp.bfloat16
    rows, features = r["tok"].shape
    ids = {}

    def remote(key, src, dst, side):
        i = ids.setdefault(key, len(ids))
        return pltpu.make_async_remote_copy(
            src_ref=src,
            dst_ref=dst,
            send_sem=r["sent"].at[i],
            recv_sem=r["came"].at[i],
            device_id=at[side],
            device_id_type=MESH,
        )

    barrier = pltpu.get_barrier_semaphore()

    def greet(side):
        pl.semaphore_signal(barrier, 1, device_id=at[side], device_id_type=MESH)

    for side in ("core", "x", "y", "far"):
        greet(side)
    for side, some in (
        ("above", z < 3),
        ("below", z > 0),
        ("next", (y == 1) & (z < 3)),
        ("last", (y == 0) & (z > 0)),
    ):
        pl.when(some)(lambda side=side: greet(side))
    more = (z < 3).astype(jnp.int32) + (z > 0).astype(jnp.int32)
    diagonal = jnp.where(y == 1, (z < 3).astype(jnp.int32), (z > 0).astype(jnp.int32))
    pl.semaphore_wait(barrier, 4 + more + diagonal)

    rim = (ITEM_MOST - 1 + 15) // 16 * 16
    window = r["window"]
    halo_up = remote(
        "halo_up", r["grads"].at[pl.ds(rows - rim, rim)], window.at[pl.ds(rows - rim, rim)], "next"
    )
    halo_down = remote(
        "halo_down", r["grads"].at[pl.ds(0, rim)], window.at[pl.ds(2 * rows, rim)], "last"
    )
    pl.when(seq < 7)(halo_up.start)
    pl.when(seq > 0)(halo_down.start)

    swaps = {}

    def swap(side, name, first):
        key = (side, name, first)
        if key in swaps:
            return
        if side == "left":
            cols = pl.ds(first, features)
            src, dst = r[name].at[:, cols], r["far_" + name].at[:, cols]
        else:
            src, dst = r[name].at[1 - c, first], r["far_" + name].at[first]
        swaps[key] = remote(key, src, dst, "core")
        swaps[key].start()

    def swap_unit(name):
        unit = units[name]
        swap("left", unit.left, unit.left_at)
        swap("right", unit.right, unit.right_at)

    order = [rest[0] for kind, *rest in PLAN if kind == START]
    for name in order:
        unit = units[name]
        swap("left", unit.left, unit.left_at)
        if not unit.right.startswith(("triple", "stream")):
            swap("right", unit.right, unit.right_at)

    slots, loads, here = {}, {}, set()

    def load(side, name, first, busy=None):
        key = (side, name, first)
        if key in slots:
            return
        slot = 1 - slots.get(busy, 1)
        for other in [k for k in slots if k[0] == side and slots[k] == slot]:
            del slots[other]
        slots[key] = slot
        if key not in here:
            swaps[key].wait_recv()
            here.add(key)
        if side == "left":
            cols = pl.ds(first, features)
            near, far = r[name].at[:, cols], r["far_" + name].at[:, cols]
            hold = r["lefts"].at[slot]
        else:
            near, far = r[name].at[c, first], r["far_" + name].at[first]
            hold = r["rights"].at[slot, :, pl.ds(0, near.shape[-1])]
        loads[key] = []
        for half, src in ((0, near), (1, far)):
            copy = pltpu.make_async_copy(
                src, hold.at[pl.ds(rows * half, rows)], r[side + "_sem"].at[slot, half]
            )
            copy.start()
            loads[key].append(copy)

    def keys_of(name):
        unit = units[name]
        return ("left", unit.left, unit.left_at), ("right", unit.right, unit.right_at)

    started = [name for name in order if name not in LINE_FIRST]
    both = slice(None)

    def axes(u, order):
        return ("x", "y") if order == 0 or started[u] in X_FIRST else ("y", "x")

    def credit(stage, order, side):
        return r["credit"].at[(stage * 2 + order) * 2 + ("x", "y").index(side)]

    def take_credit(u, stage, order):
        if u >= (FIRST_SLOTS, SECOND_SLOTS)[stage]:
            pl.semaphore_wait(credit(stage, order, axes(u, order)[stage]), 1)

    def give_credit(u, stage, order):
        then = u + (FIRST_SLOTS, SECOND_SLOTS)[stage]
        if then < len(started):
            side = axes(then, order)[stage]
            pl.semaphore_signal(
                credit(stage, order, side), 1, device_id=at[side], device_id_type=MESH
            )

    def part_of(u, order, *index):
        unit = units[started[u]]
        place = (pl.ds(0, 2), pl.ds(0, unit.rows)) if len(index) < 3 else (pl.ds(0, unit.rows),)
        return r["part"].at[(u % PART_SLOTS, order, *index, *place)]

    def moved(u, order, stage):
        land = r["land_one"] if stage == 0 else r["land_two"]
        land = land.at[u % (FIRST_SLOTS, SECOND_SLOTS)[stage], order]
        height = pl.ds(0, units[started[u]].rows)
        if stage == 1:
            send = (x, 1 - y) if axes(u, order)[1] == "y" else (1 - x, y)
            return part_of(u, order, *send), part_of(u, order, x, y), land.at[:, height]
        if axes(u, order)[0] == "x":
            send, keep = (1 - x, both), (x, both)
        else:
            send, keep = (both, 1 - y), (both, y)
        return part_of(u, order, *send), part_of(u, order, *keep), land.at[:, :, height]

    def stage_copy(u, order, stage):
        send, _, land = moved(u, order, stage)
        return remote((u, stage, order), send, land, axes(u, order)[stage])

    def compute(name, part, slot):
        unit = units[name]
        left_key, right_key = keys_of(name)
        left, right = r["lefts"].at[slots[left_key]], r["rights"].at[slots[right_key]]

        def product(n):
            cols = pl.ds(pl.multiple_of(n * 256, 256), 256)
            return dot_tn(left[...], right[:, cols])

        if unit.tiles:

            def body(n, carry):
                tile = product(n).astype(low)
                for i in range(2):
                    g = 2 * n + i
                    x_at = g // unit.tiles
                    t = pl.multiple_of((g - x_at * unit.tiles) * ROWS, 16)
                    for first, order, y_at, place, _ in unit.blocks:
                        part[slot, order, x_at, y_at, place, pl.ds(t, ROWS)] = tile[
                            first : first + ROWS, i * LANES : (i + 1) * LANES
                        ]
                return carry

            lax.fori_loop(0, unit.tiles, body, 0)
            return

        def body(n, carry):
            tile = product(n).astype(low)
            for first, order, y_at, place, _ in unit.blocks:
                for i in range(2):
                    part[slot, order, n, y_at, place, pl.ds(i * ROWS, ROWS)] = tile[
                        first : first + ROWS, i * LANES : (i + 1) * LANES
                    ]
            return carry

        lax.fori_loop(0, 2, body, 0)
        tile = product(2).astype(low)
        lane = lanes_of((THIRD, LANES))
        for first, order, y_at, place, _ in unit.blocks:
            for x_at in range(2):
                pieces = [
                    tile[first + s * THIRD : first + (s + 1) * THIRD, x_at * LANES :][:, :LANES]
                    for s in range(3)
                ]
                packed = jnp.where(
                    lane < 32, pieces[0], jnp.where(lane < 64, pieces[1], pieces[2])
                )
                part[slot, order, x_at, y_at, place, pl.ds(2 * ROWS, THIRD)] = packed

    def wait_sends(u):
        for order in range(2):
            for stage in range(2):
                stage_copy(u, order, stage).wait_send()

    def fetch(name, ahead):
        for key in keys_of(name):
            load(*key)
            for copy in loads.pop(key, ()):
                copy.wait()
        if ahead is not None and ahead not in SKIP:
            for key, busy in zip(keys_of(ahead), keys_of(name)):
                if key in swaps:
                    load(*key, busy)

    def first_stage(u):
        if u >= PART_SLOTS:
            wait_sends(u - PART_SLOTS)
        compute(started[u], r["part"], u % PART_SLOTS)
        for order in range(2):
            take_credit(u, 0, order)
            stage_copy(u, order, 0).start()

    def second_stage(u):
        for order in range(2):
            stage_copy(u, order, 0).wait_recv()
            _, keep, land = moved(u, order, 0)
            add_into(keep, land)
            give_credit(u, 0, order)
            take_credit(u, 1, order)
            stage_copy(u, order, 1).start()

    def last_ref(u, order, place):
        return r["ends"].at[u % LAST_SLOTS, order, place, pl.ds(0, units[started[u]].rows)]

    def third_stage(u):
        if u >= LAST_SLOTS:
            chain_sends(u - LAST_SLOTS)
        for order in range(2):
            stage_copy(u, order, 1).wait_recv()
            _, keep, land = moved(u, order, 1)
            for place in range(2):
                value = keep.at[place][...].astype(jnp.float32)
                value = value + land.at[place][...].astype(jnp.float32)
                last_ref(u, order, place)[...] = value.astype(low)
            give_credit(u, 1, order)

    def chain_copy(u, order, place, up):
        pool, i = r["chain_at"][started[u], order, place, up]
        dst = r[pool].at[i, pl.ds(0, units[started[u]].rows)]
        src = last_ref(u, order, place)
        key = (u, "chain", order, place, up)
        return remote(key, src, dst, "above" if up else "below"), dst

    def hop(u, step):
        for up, me in ((True, step - 1), (False, 4 - step)):
            todo = [
                key
                for key, z_at in sorted(
                    units[started[u]].z_of.items(), key=lambda item: -item[1] if up else item[1]
                )
                if ((z_at > me) if up else (z_at < me))
            ]

            @pl.when(z == me)
            def _():
                for order, place in todo:
                    copy, land = chain_copy(u, order, place, up)
                    if step > 1:
                        copy.wait_recv()
                        add_into(last_ref(u, order, place), land)
                    copy.start()

    def chain_sends(u):
        for (order, place), z_at in units[started[u]].z_of.items():
            for up, some in ((True, z_at > 0), (False, z_at < 3)):
                if some:

                    @pl.when((z < z_at) if up else (z > z_at))
                    def _():
                        chain_copy(u, order, place, up)[0].wait_send()

    def finish(u):
        unit = units[started[u]]
        for (order, place), z_at in unit.z_of.items():

            @pl.when(z == z_at)
            def _():
                value = last_ref(u, order, place)[...].astype(jnp.float32)
                for up, have in ((True, z_at > 0), (False, z_at < 3)):
                    if have:
                        copy, land = chain_copy(u, order, place, up)
                        copy.wait_recv()
                        value = value + land[...].astype(jnp.float32)
                store_out(unit, order, place, value)

    def store_out(unit, order, place, value):
        out = r["out_" + unit.out]
        if unit.tiles:
            for t in range(unit.tiles):
                col = (unit.out_at + t) * LANES
                width = min(LANES, out.shape[1] - col)
                out[:, col : col + width] = value[t * ROWS : (t + 1) * ROWS, :width]
            return
        base = {"shrink": (2 * order + place) * ROWS, "proj": 0, "skip": place * ROWS}[unit.out]
        for i in range(2):
            out[base : base + ROWS, i * LANES : (i + 1) * LANES] = value[i * ROWS : (i + 1) * ROWS]
        for s in range(3):
            out[base + s * THIRD : base + (s + 1) * THIRD, 256:288] = value[
                2 * ROWS : 2 * ROWS + THIRD, s * 32 : (s + 1) * 32
            ]

    def line_ref(name, order, place):
        return r["line"].at[0, order, both, both, place, pl.ds(0, units[name].rows)]

    def line_copy(name, order, place, up):
        i = r["line_at"][name, order, place, up]
        dst = r["line_land"].at[i, both, both, pl.ds(0, units[name].rows)]
        key = (name, "line", order, place, up)
        return remote(key, line_ref(name, order, place), dst, "above" if up else "below"), dst

    def line_hop(name, step, turn):
        for up, me in ((True, step - 1), (False, 4 - step)):
            todo = [
                key
                for key, z_at in sorted(
                    units[name].z_of.items(), key=lambda item: -item[1] if up else item[1]
                )
                if ((z_at > me) if up else (z_at < me))
            ][turn : turn + 1]

            @pl.when(z == me)
            def _():
                for order, place in todo:
                    copy, land = line_copy(name, order, place, up)
                    if step > 1:
                        copy.wait_recv()
                        add_into(line_ref(name, order, place), land)
                    copy.start()

    def line_credit(act):
        for some, side, here, there in ((z < 3, "above", 8, 9), (z > 0, "below", 9, 8)):

            @pl.when(some)
            def _():
                if act is pl.semaphore_wait:
                    pl.semaphore_wait(r["credit"].at[here], 1)
                else:
                    pl.semaphore_signal(
                        r["credit"].at[there], 1, device_id=at[side], device_id_type=MESH
                    )

    def line_copies(name):
        i = LINE_FIRST.index(name)
        height = pl.ds(0, units[name].rows)
        own = r["line_own"].at[i]
        return (
            remote((name, "line_x"), own.at[1 - x, both, height], r["line_x"].at[i, both, height], "x"),
            remote((name, "line_y"), own.at[x, 1 - y, height], r["line_y"].at[i, height], "y"),
        )

    def line_stage(name, stage):
        i = LINE_FIRST.index(name)
        unit = units[name]
        height = pl.ds(0, unit.rows)
        if stage == "end":
            for (order, place), z_at in unit.z_of.items():

                @pl.when(z == z_at)
                def _():
                    lands = []
                    for up, have in ((True, z_at > 0), (False, z_at < 3)):
                        if have:
                            copy, land = line_copy(name, order, place, up)
                            copy.wait_recv()
                            lands.append(land)
                    for x_at in range(2):
                        for y_at in range(2):
                            value = line_ref(name, order, place)[x_at, y_at].astype(jnp.float32)
                            for land in lands:
                                value = value + land[x_at, y_at].astype(jnp.float32)
                            r["line_own"][i, x_at, y_at, height] = value.astype(low)

            line_copies(name)[0].start()
            if i + 1 < len(LINE_FIRST):
                line_credit(pl.semaphore_signal)
        elif stage == "x":
            line_copies(name)[0].wait_recv()
            add_into(r["line_own"].at[i, x, both, height], r["line_x"].at[i, both, height])
            line_copies(name)[1].start()
        else:
            line_copies(name)[1].wait_recv()
            value = r["line_own"][i, x, y, height].astype(jnp.float32)
            value = value + r["line_y"][i, height].astype(jnp.float32)
            store_out(unit, 0, 0, value)

    def line_drain(name):
        for (order, place), z_at in units[name].z_of.items():
            for up, some in ((True, z_at > 0), (False, z_at < 3)):
                if some:

                    @pl.when((z < z_at) if up else (z > z_at))
                    def _():
                        line_copy(name, order, place, up)[0].wait_send()

    def head_load(h):
        return pltpu.make_async_copy(
            r["wins"].at[:, h], r["head"].at[h % 2], r["head_sem"].at[h % 2]
        )

    done = {"heads": 0}

    def halo_work():
        head_load(0).start()
        own = pltpu.make_async_copy(r["grads"], window.at[pl.ds(rows, rows)], r["chunk_sem"].at[0])
        own.start()
        pad = rows - rim
        blank = jnp.zeros((pad, window.shape[1]), low)
        window[0:pad] = blank
        window[3 * rows - pad :] = blank

        @pl.when(seq == 0)
        def _():
            window[pad:rows] = jnp.zeros((rim, window.shape[1]), low)

        @pl.when(seq == 7)
        def _():
            window[2 * rows : 2 * rows + rim] = jnp.zeros((rim, window.shape[1]), low)

        back_masks(r["id_col"], r["id_row"], r["own_hide"], r["rim_hide"], rows)
        r["probs"][...] = jnp.zeros(r["probs"].shape, low)
        r["scored"][...] = jnp.zeros(r["scored"].shape, low)
        own.wait()
        pl.when(seq > 0)(halo_up.wait_recv)
        pl.when(seq < 7)(halo_down.wait_recv)
        r["stats"][...] = window[:, features:]

    def heads_work(count):
        first = done["heads"]
        done["heads"] += count

        def body(h, carry):
            head_load(h).wait()

            @pl.when(h + 1 < HEADS)
            def _():
                head_load(h + 1).start()

            tile = (h * HEAD_DIM) // LANES
            off = h * HEAD_DIM - tile * LANES
            cols = pl.ds(pl.multiple_of(tile * LANES, LANES), 2 * LANES)
            pair = pltpu.roll(window[:, cols], (2 * LANES - off) % (2 * LANES), 1)[:, :LANES]
            r["grad_head"][...] = jnp.where(
                lanes_of((3 * rows, LANES)) < HEAD_DIM, pair, jnp.zeros_like(pair)
            )
            head = r["head"].at[h % 2]
            found = back_head(
                h, head.at[0], head.at[1], head.at[2], r["grad_head"], r["stats"][...],
                r["own_hide"], r["rim_hide"], r["probs"], r["scored"],
            )
            wide = lanes_of((rows, 2 * LANES))
            inside = (wide >= off) & (wide < off + HEAD_DIM)
            for part, value in enumerate(found):
                moved = pltpu.roll(jnp.concatenate([value, jnp.zeros_like(value)], axis=1), off, 1)
                r["triple"][part, :, cols] = jnp.where(inside, moved, r["triple"][part, :, cols])
            return carry

        lax.fori_loop(first, first + count, body, 0)

    sums = r["sums"]

    def pack_work():
        for p in range(3):
            if p != 1:
                row = 3 + p // 2
                sums[row : row + 1] = column_sum(r["triple"][p, :, :features].astype(jnp.float32))
        for b in range(4):
            pieces = []
            for p in range(3):
                low_at, high_at = max(864 * b, features * p), min(864 * (b + 1), features * (p + 1))
                if low_at < high_at:
                    pieces.append(
                        r["triple"][p, :, low_at - features * p : high_at - features * p]
                    )
            pieces.append(jnp.zeros((rows, 32), low))
            value = jnp.concatenate(pieces, axis=1)
            for j, (first, tiles) in enumerate(TRIPLE_TILES):
                width = tiles * LANES
                r[f"triple{j}"][b % 2, 0, :, width * (b // 2) : width * (b // 2 + 1)] = value[
                    :, first * LANES : first * LANES + width
                ]
        for j in range(len(TRIPLE_TILES)):
            swap("right", f"triple{j}", 0)

    chunks = [(p, first, count) for p in range(3) for first, count in ((0, 768), (768, 384))]

    def weight_load(i):
        slot = i % 2
        if i < 6:
            p, first, count = chunks[i]
            src = r["attn_weight"].at[pl.ds(first, count), pl.ds(features * p, features)]
        else:
            count = 768
            src = r["skip_weight"].at[pl.ds(768 * (i - 6), 768)]
        return pltpu.make_async_copy(
            src, r["lefts"].at[slot, pl.ds(0, count)], r["weight_sem"].at[slot]
        )

    def back_work(p):
        if p == 0:
            weight_load(0).start()
        for i in (2 * p, 2 * p + 1):
            _, first, count = chunks[i]
            weight_load(i).wait()
            if i < 5:
                weight_load(i + 1).start()
            part = dot_nt(r["triple"][p, :, :features], r["lefts"][i % 2, :count])
            cols = slice(first, first + count)
            if p == 0:
                r["normed_grad"][:, cols] = part
            else:
                r["normed_grad"][:, cols] += part

    def norm_work():
        gain = vector(r["gain"])
        sums[0:3] = jnp.zeros((3, features), jnp.float32)
        chunk = r["chunk"]
        for i in range(rows // LANES):
            here = pl.ds(i * LANES, LANES)
            copies = [
                pltpu.make_async_copy(r[name].at[here], chunk.at[k], r["chunk_sem"].at[k])
                for k, name in enumerate(("stream", "middle_grad"))
            ]
            for copy in copies:
                copy.start()
            for copy in copies:
                copy.wait()
            unit, scale = row_norm(chunk[0])
            cotangent = r["normed_grad"][here]
            rounded = (chunk[1] + norm_back(unit, scale, gain, cotangent)).astype(low)
            window[here, :features] = rounded
            sums[0:1] += column_sum(rounded.astype(jnp.float32))
            sums[1:2] += column_sum(cotangent * unit)
            sums[2:3] += column_sum(cotangent)
        by_core_store(r["stream_cols"], window[0:rows, :features])
        swap("right", "stream_cols", 0)

    def out_copies():
        return [
            pltpu.make_async_copy(
                r["triple"].at[k, :, pl.ds(0, features)], r[name], r["chunk_sem"].at[k]
            )
            for k, name in enumerate(("out_tok", "out_skp"))
        ]

    def out_work(k):
        i = 6 + k
        if k == 0:
            weight_load(i).start()
        weight_load(i).wait()
        if k < 2:
            weight_load(i + 1).start()
        value = dot_nt(window[0:rows, :features], r["lefts"][i % 2, :768]).astype(low)
        for half in range(2):
            base = features * half
            first, last = max(768 * k, base), min(768 * (k + 1), base + features)
            if first < last:
                r["triple"][half, :, first - base : last - base] = value[
                    :, first - 768 * k : last - 768 * k
                ]
        if k == 2:
            for copy in out_copies():
                copy.start()

    sides = ("core", "x", "y", "pair", "far")

    def vec_work(step):
        vec, land = r["vec"], r["vec_land"]
        if step == 0:
            vec[0] = r["vec_in"][...]
            vec[0, 0:5] = sums[0:5]
        else:
            remote(("vec", step - 1), vec.at[step - 1], land.at[step - 1], sides[step - 1]).wait_recv()
            total = vec[step - 1] + land[step - 1]
            if step == len(sides):
                r["out_vec"][...] = total
            else:
                vec[step] = total
        if step < len(sides):
            remote(("vec", step), vec.at[step], land.at[step], sides[step]).start()

    def start(name):
        i = order.index(name)
        fetch(name, order[i + 1] if i + 1 < len(order) else None)
        if name in LINE_FIRST:
            i = LINE_FIRST.index(name)
            if i > 0:
                line_drain(LINE_FIRST[i - 1])
                line_credit(pl.semaphore_wait)
            compute(name, r["line"], 0)
        else:
            first_stage(started.index(name))

    def third(name):
        third_stage(started.index(name))
        hop(started.index(name), 1)

    steps = {
        START: start,
        TURN: lambda name: second_stage(started.index(name)),
        SETTLE: third,
        HOP: lambda name, step: hop(started.index(name), step),
        FINISH: lambda name: finish(started.index(name)),
        LINE: line_hop,
        LINE_END: lambda name: line_stage(name, "end"),
        LINE_X: lambda name: line_stage(name, "x"),
        LINE_Y: lambda name: line_stage(name, "y"),
        HALO: halo_work,
        HEAD: heads_work,
        PACK: pack_work,
        BACK: back_work,
        NORM: norm_work,
        OUT: out_work,
        VECTOR: vec_work,
    }
    for kind, *rest in PLAN:
        steps[kind](*rest)
    for copy in out_copies():
        copy.wait()
    for name in LINE_FIRST[-1:]:
        line_drain(name)
    for name in LINE_FIRST:
        for copy in line_copies(name):
            copy.wait_send()
    for copy in swaps.values():
        copy.wait_send()
    count = len(started)
    for u in range(max(0, count - PART_SLOTS), count):
        wait_sends(u)
    for u in range(max(0, count - LAST_SLOTS), count):
        chain_sends(u)
    for step in range(len(sides)):
        remote(("vec", step), r["vec"].at[step], r["vec_land"].at[step], sides[step]).wait_send()
    pl.when(seq < 7)(halo_up.wait_send)
    pl.when(seq > 0)(halo_down.wait_send)


def gradients(values, vec):
    low, full = jnp.bfloat16, jnp.float32
    rows, features = values["tok"].shape
    names, operands, in_specs, out_shape, out_specs, scratch = [], [], [], [], [], []
    held = ("id_col", "id_row", "gain")
    for name, value in values.items():
        names.append(name)
        operands.append(value)
        in_specs.append(whole() if name in held else anywhere())
    names.append("vec_in")
    operands.append(vec)
    in_specs.append(whole())

    def out(name, shape, dtype, spec):
        names.append(name)
        out_shape.append(jax.ShapeDtypeStruct(shape, dtype))
        out_specs.append(spec)

    for name, shape in GRADS:
        out("out_" + name, shape, full, whole())
    out("out_vec", vec.shape, full, whole())
    out("out_tok", (rows, features), low, anywhere())
    out("out_skp", (rows, features), low, anywhere())
    for name in ("active", "second", "mixed", "normed", "tok", "skp"):
        out("far_" + name, values[name].shape, low, anywhere())
    for name in ("upstream", "hidden", "branch"):
        out("far_" + name, values[name].shape[1:], low, anywhere())
    cores = {f"triple{j}": 2 * LANES * tiles for j, (_, tiles) in enumerate(TRIPLE_TILES)}
    cores["stream_cols"] = 768
    for name, width in cores.items():
        out("far_" + name, (1, rows, width), low, anywhere())

    def add(name, kind):
        names.append(name)
        scratch.append(kind)

    most = 3 * ROWS
    for name, width in cores.items():
        add(name, pltpu.VMEM((2, 1, rows, width), low))
    add("lefts", pltpu.VMEM((2, 2 * rows, features), low))
    add("rights", pltpu.VMEM((2, 2 * rows, 768), low))
    add("left_sem", pltpu.SemaphoreType.DMA((2, 2)))
    add("right_sem", pltpu.SemaphoreType.DMA((2, 2)))
    add("part", pltpu.VMEM((PART_SLOTS, 2, 2, 2, 2, most, LANES), low))
    add("land_one", pltpu.VMEM((FIRST_SLOTS, 2, 2, 2, most, LANES), low))
    add("land_two", pltpu.VMEM((SECOND_SLOTS, 2, 2, most, LANES), low))
    add("ends", pltpu.VMEM((LAST_SLOTS, 2, 2, most, LANES), low))
    chain_at, sizes = {}, {"chain_short": 0, "chain_long": 0}
    for name, unit in make_units().items():
        if name in LINE_FIRST:
            continue
        pool = "chain_short" if unit.rows <= 2 * ROWS + THIRD else "chain_long"
        for (order, place), z_at in unit.z_of.items():
            for up, have in ((True, z_at > 0), (False, z_at < 3)):
                if have:
                    chain_at[name, order, place, up] = (pool, sizes[pool])
                    sizes[pool] += 1
    add("chain_short", pltpu.VMEM((sizes["chain_short"], 2 * ROWS + THIRD, LANES), low))
    add("chain_long", pltpu.VMEM((sizes["chain_long"], most, LANES), low))
    add("sent", pltpu.SemaphoreType.DMA((256,)))
    add("came", pltpu.SemaphoreType.DMA((256,)))
    span = 3 * rows
    add("window", pltpu.VMEM((span, features + LANES), low))
    add("stats", pltpu.VMEM((span, LANES), low))
    add("head", pltpu.VMEM((2, 3, span, LANES), low))
    add("head_sem", pltpu.SemaphoreType.DMA((2,)))
    add("grad_head", pltpu.VMEM((span, LANES), low))
    add("own_hide", pltpu.VMEM((rows // LANES, LANES, span - rows + LANES), low))
    add("rim_hide", pltpu.VMEM((2 * rows // LANES, LANES, rows), low))
    add("probs", pltpu.VMEM((span, rows), low))
    add("scored", pltpu.VMEM((span, rows), low))
    add("triple", pltpu.VMEM((3, rows, features + LANES), low))
    add("weight_sem", pltpu.SemaphoreType.DMA((2,)))
    add("normed_grad", pltpu.VMEM((rows, features), full))
    add("chunk", pltpu.VMEM((2, LANES, features), full))
    add("chunk_sem", pltpu.SemaphoreType.DMA((2,)))
    add("credit", pltpu.SemaphoreType.REGULAR((10,)))
    lines = len(LINE_FIRST)
    line_at = {}
    for name in LINE_FIRST:
        for (order, place), z_at in make_units()[name].z_of.items():
            for up, have in ((True, z_at > 0), (False, z_at < 3)):
                if have:
                    line_at[name, order, place, up] = len(
                        [key for key in line_at if key[0] == name]
                    )
    add("line", pltpu.VMEM((1, 2, 2, 2, 2, most, LANES), low))
    add("line_land", pltpu.VMEM((6, 2, 2, most, LANES), low))
    add("line_own", pltpu.VMEM((lines, 2, 2, most, LANES), low))
    add("line_x", pltpu.VMEM((lines, 2, most, LANES), low))
    add("line_y", pltpu.VMEM((lines, most, LANES), low))
    add("sums", pltpu.VMEM((8, features), full))
    add("vec", pltpu.VMEM((5, *vec.shape), full))
    add("vec_land", pltpu.VMEM((5, *vec.shape), full))

    def kernel(*refs):
        gradient_kernel(dict(zip(names, refs), chain_at=chain_at, line_at=line_at))

    found = pl.pallas_call(
        kernel,
        out_shape=out_shape,
        in_specs=in_specs,
        out_specs=out_specs,
        scratch_shapes=scratch,
        compiler_params=pltpu.CompilerParams(
            collective_id=0, has_side_effects=True, vmem_limit_bytes=VMEM_MOST
        ),
        name="gradients",
    )(*operands)
    return dict(zip([name for name, _ in GRADS] + ["vec", "tok", "skp"], found))


VECTORS = ((0, 1), (1, 1), (2, 1), (3, 2), (5, 1), (6, 1), (7, 1), (9, 4), (8, 1))


def results_kernel(*refs):
    count = len(GRADS) + 2
    total, sources, targets = refs[0], refs[1 : 1 + count], refs[1 + count :]
    for source, target in zip(sources, targets):
        target[...] = source[...].T if source.shape != target.shape else source[...]
    features = total.shape[1]
    place = lax.axis_index("seq") * lax.axis_size("batch") + lax.axis_index("batch")
    for (first, rows), target in zip(VECTORS, targets[count:]):
        width = target.shape[0]
        row = place * width // features
        off = place * width - row * features
        line = jnp.broadcast_to(total[pl.ds(first + row, 1)], (8, features))
        target[...] = pltpu.roll(line, (features - off) % features, 1)[0, :width]


def results(found):
    values = [found[name] for name in [*(name for name, _ in GRADS), "tok", "skp"]]
    devices = lax.axis_size("seq") * lax.axis_size("batch")
    features = found["vec"].shape[1]
    shapes = [values[0].shape[::-1], *(value.shape for value in values[1:])]
    out = [jax.ShapeDtypeStruct(shape, value.dtype) for shape, value in zip(shapes, values)]
    out += [
        jax.ShapeDtypeStruct((rows * features // devices,), jnp.float32) for _, rows in VECTORS
    ]
    got = pl.pallas_call(
        results_kernel,
        out_shape=out,
        in_specs=[whole()] * (1 + len(values)),
        out_specs=[whole()] * len(out),
        compiler_params=params(),
        name="results",
    )(found["vec"], *values)
    return (got[0].T, *got[1 : len(values)]), got[len(values) :]


def unsplit(value):
    blocks = []
    for b in range(4):
        x, c = b // 2, b % 2
        blocks.append(value[c, 0, :, 256 * x : 256 * x + 256])
        blocks.append(value[c, 0, :, 512 + LANES * x : 544 + LANES * x])
    return jnp.concatenate(blocks, axis=1)


def outer_sum(left, right):
    return dot_tn(left, right)


def summed(lefts, rights, vector_list):
    hidden = rights["hidden"]
    _, pieces, rows, width = hidden.shape
    hidden = hidden.reshape(2, pieces, rows, 2, width // 2).transpose(2, 3, 0, 1, 4)
    columns_of = dict(
        joined=unsplit(rights["stream"]),
        normed=rights["triple"],
        mixed=unsplit(rights["branch"]),
        second=hidden.reshape(rows, -1),
        active=unsplit(rights["upstream"]),
    )
    parts = []
    for name in ("joined", "normed", "mixed", "second", "active"):
        gathered = lax.all_gather(lefts[name], "batch", axis=0, tiled=True)
        columns = lax.all_to_all(
            columns_of[name], "batch", split_axis=1, concat_axis=0, tiled=True
        )
        parts.append(outer_sum(gathered, columns).astype(jnp.bfloat16))
    parts = lax.psum_scatter(tuple(parts), "seq", scatter_dimension=0, tiled=True)
    vectors = tuple(
        lax.psum_scatter(vector, ("seq", "batch"), scatter_dimension=0, tiled=True)
        for vector in vector_list
    )
    return tuple(part.astype(jnp.float32) for part in parts), vectors


def rims(value, width):
    size = lax.axis_size("seq")
    up = [(i, i + 1) for i in range(size - 1)]
    down = [(j, i) for i, j in up]
    return (
        lax.ppermute(value[-width:], "seq", up),
        lax.ppermute(value[:width], "seq", down),
    )


def on_device(
    tokens,
    skip_tokens,
    segment_ids,
    upstream,
    skip_weight,
    skip_bias,
    first_gain,
    first_shift,
    attn_weight,
    attn_bias,
    proj_weight,
    proj_bias,
    second_gain,
    second_shift,
    expand_weight,
    expand_bias,
    shrink_weight,
    shrink_bias,
):
    _, rows, features = tokens.shape
    rim = (ITEM_MOST - 1 + 15) // 16 * 16
    tok, skp, above = tokens[0], skip_tokens[0], upstream[0]
    position = lax.axis_index("seq")
    padded_ids = jnp.pad(segment_ids[0], (rows, rows), constant_values=-1)
    window_ids = lax.dynamic_slice_in_dim(padded_ids, position * rows, 3 * rows, 0)
    id_row, id_col = window_ids[None, :], window_ids[:, None]

    stream, normed = stream_norm(tok, skp, skip_weight, skip_bias, first_gain, first_shift)
    before, after = rims(normed, rim)
    own = own_heads(normed, attn_weight, attn_bias)
    wins, mixed, lse = attend(own, before, after, attn_weight, attn_bias, id_col, id_row)
    (
        result, active, hidden_by_core, second, branch, branch_by_core, up_by_core, middle_grad,
        mixed_grad, sums,
    ) = layer(
        stream, mixed, lse, above,
        (
            proj_weight, proj_bias, second_gain, second_shift, expand_weight, expand_bias,
            shrink_weight, shrink_bias,
        ),
    )
    if lax.axis_size("seq") == 8 and lax.axis_size("batch") == 4:
        found = gradients(
            dict(
                active=active, second=second, mixed=mixed, normed=normed, tok=tok, skp=skp,
                upstream=up_by_core, hidden=hidden_by_core, branch=branch_by_core, wins=wins,
                grads=mixed_grad, id_col=id_col, id_row=id_row, stream=stream,
                middle_grad=middle_grad, gain=first_gain, attn_weight=attn_weight,
                skip_weight=skip_weight,
            ),
            sums,
        )
        (shrink, expand, proj, attn, skip, tok_grad, skip_grad), vectors = results(found)
        weight_parts = (skip, attn, proj, expand, shrink)
    else:
        before, after = rims(mixed_grad, rim)
        blank = jnp.zeros((rows - rim, mixed_grad.shape[1]), mixed_grad.dtype)
        grad_window = jnp.concatenate([blank, before, mixed_grad, after, blank], axis=0)
        stats = grad_window[:, features:]
        triple, triple_sum = attend_back(wins, grad_window, stats, id_col, id_row)
        tok_grad, skip_grad, stream_by_core, stream_sums = stream_back(
            triple, attn_weight, stream, middle_grad, first_gain, skip_weight
        )
        vector_list = (
            stream_sums[2],
            stream_sums[0],
            stream_sums[1],
            jnp.concatenate([triple_sum[0, :features], triple_sum[0, 2 * features :]]),
            sums[5],
            sums[6],
            sums[7],
            sums[9:13].reshape(-1),
            sums[8],
        )
        joined = jnp.concatenate([tok, skp], axis=1)
        weight_parts, vectors = summed(
            dict(active=active, second=second, mixed=mixed, normed=normed, joined=joined),
            dict(
                upstream=up_by_core,
                hidden=hidden_by_core,
                branch=branch_by_core,
                triple=triple,
                stream=stream_by_core,
            ),
            vector_list,
        )
    return (
        result[None],
        tok_grad[None],
        skip_grad[None],
        weight_parts[0],
        vectors[0],
        vectors[1],
        vectors[2],
        weight_parts[1],
        vectors[3],
        weight_parts[2],
        vectors[4],
        vectors[5],
        vectors[6],
        weight_parts[3],
        vectors[7],
        weight_parts[4],
        vectors[8],
    )


def solution(mesh):
    in_specs = (
        P("batch", "seq", None),
        P("batch", "seq", None),
        P("batch", None),
        P("batch", "seq", None),
        P(),
        P(),
        P(),
        P(),
        P(),
        P(),
        P(),
        P(),
        P(),
        P(),
        P(),
        P(),
        P(),
        P(),
    )
    out_specs = (
        P("batch", "seq", None),
        P("batch", "seq", None),
        P("batch", "seq", None),
        P("seq", "batch"),
        P(("seq", "batch")),
        P(("seq", "batch")),
        P(("seq", "batch")),
        P("seq", "batch"),
        P(("seq", "batch")),
        P("seq", "batch"),
        P(("seq", "batch")),
        P(("seq", "batch")),
        P(("seq", "batch")),
        P("seq", "batch"),
        P(("seq", "batch")),
        P("seq", "batch"),
        P(("seq", "batch")),
    )
    return jax.shard_map(
        on_device, mesh=mesh, in_specs=in_specs, out_specs=out_specs, check_vma=False
    )
```

```python
import jax
import jax.numpy as jnp
from jax import lax
from jax.experimental import pallas as pl
from jax.experimental.pallas import tpu as pltpu
from jax.sharding import PartitionSpec as P

SEQ, BATCH = "seq", "batch"
HEADS = 16
HEAD_DIM = 72
ITEM_MOST = 322
LANES = 128
MESH = pl.DeviceIdType.MESH
SCALE2 = HEAD_DIM**-0.5 * 1.4426950408889634
VMEM_MOST = 60 * 2**20


ROOT2 = 2.0**0.5


def dot(left, right):
    return jnp.dot(left, right, preferred_element_type=jnp.float32)


def dot_nt(left, right):
    return lax.dot_general(
        left, right, (((1,), (1,)), ((), ())), preferred_element_type=jnp.float32
    )


def dot_tn(left, right):
    return lax.dot_general(
        left, right, (((0,), (0,)), ((), ())), preferred_element_type=jnp.float32
    )


def vector(ref, first=0, count=None):
    count = ref.shape[0] if count is None else count
    return ref[pl.ds(first, count)].astype(jnp.float32).reshape(1, count)


def whole():
    return pl.BlockSpec(memory_space=pltpu.VMEM)


def anywhere():
    return pl.BlockSpec(memory_space=pl.ANY)


def params():
    return pltpu.CompilerParams(vmem_limit_bytes=60 * 2**20)


def erf(value):
    v = jnp.clip(value, -3.832506856900711, 3.832506856900711)
    s = v * v
    top = 0.00022905065861350646
    for a in (0.0034082910107109506, 0.050955695062380861, 0.18520832239976145, 1.128379143519084):
        top = top * s + a
    low = -1.1791602954361697e-7
    for a in (0.000023547966471313185, 0.0010179625278914885, 0.014070470171167667):
        low = low * s + a
    low = (low * s + 0.11098505178285362) * s + 0.49746925110067538
    return v * top / (low * s + 1.0)


def row_norm(value):
    centred = value - jnp.mean(value, axis=-1, keepdims=True)
    scale = lax.rsqrt(jnp.mean(centred * centred, axis=-1, keepdims=True) + 1e-05)
    return centred * scale, scale


def norm_back(unit, scale, gain, cotangent):
    inner = cotangent * gain
    mean = jnp.mean(inner, axis=-1, keepdims=True)
    along = jnp.mean(inner * unit, axis=-1, keepdims=True)
    return scale * (inner - mean - unit * along)


def column_sum(value):
    return jnp.sum(value, axis=0, keepdims=True)


MARKS = (HEAD_DIM, HEAD_DIM + 16, HEAD_DIM + 32)


def lanes_of(shape):
    return lax.broadcasted_iota(jnp.int32, shape, len(shape) - 1)


def marked(lane):
    return (lane == MARKS[0]) | (lane == MARKS[1]) | (lane == MARKS[2])


def head_tile(value, h, ones):
    rows = value.shape[0]
    lane = lanes_of((rows, LANES - HEAD_DIM)) + HEAD_DIM
    rest = jnp.where(marked(lane) & ones, 1.0, 0.0).astype(value.dtype)
    return jnp.concatenate([value[:, HEAD_DIM * h : HEAD_DIM * (h + 1)], rest], axis=1)


def project(rows_ref, weight_ref, bias, part, store):
    features = rows_ref.shape[1]
    value = dot(rows_ref[...], weight_ref[...])
    if part != 1:
        at = 0 if part == 0 else features
        value = value + vector(bias, at, features)
    value = value.astype(jnp.bfloat16)
    for h in range(HEADS):
        store(part, h, head_tile(value, h, part > 0))


HIDE = -1e30


def forward_kernel(
    tok, skp, skip_weight, skip_bias, gain, shift, weight, bias, id_col, id_row, upstream, shrink,
    stream, normed, wins, mixed, lse, active_grad, window, halo, held, held_skip, hide, own_part,
    gathered, shrink_tile, grad_tile, sems, out_sems, sent, came, wide_sems,
):
    rows, features = tok.shape
    rim = halo.shape[0] // 2
    span = 3 * rows
    blocks = rows // LANES
    reach = span - (blocks - 1) * LANES
    seq, size, batch = lax.axis_index(SEQ), lax.axis_size(SEQ), lax.axis_index(BATCH)
    after, before = (jnp.minimum(seq + 1, size - 1), batch), (jnp.maximum(seq - 1, 0), batch)
    skip_copies = [
        pltpu.make_async_copy(
            skip_weight.at[:, pl.ds(384 * n, 384)], held_skip.at[n], sems.at[n]
        )
        for n in range(3)
    ]
    copies = [
        pltpu.make_async_copy(
            weight.at[:, pl.ds(features * p, features)], held.at[p], sems.at[3 + p]
        )
        for p in range(3)
    ]
    for copy in skip_copies + copies:
        copy.start()

    barrier = pltpu.get_barrier_semaphore()

    def greet(device):
        pl.semaphore_signal(barrier, 1, device_id=device, device_id_type=MESH)

    pl.when(seq < size - 1)(lambda: greet(after))
    pl.when(seq > 0)(lambda: greet(before))
    pl.semaphore_wait(
        barrier, (seq < size - 1).astype(jnp.int32) + (seq > 0).astype(jnp.int32)
    )

    for n, copy in enumerate(skip_copies):
        copy.wait()
        at = slice(384 * n, 384 * n + 384)
        stream[:, at] = (
            dot(tok[...], held_skip[n, :features])
            + dot(skp[...], held_skip[n, features:])
            + vector(skip_bias, 384 * n, 384)
        )
    unit, _ = row_norm(stream[...])
    normed[...] = (unit * vector(gain) + vector(shift)).astype(jnp.bfloat16)

    near = rim // 32 * 16
    parts = ((0, near), (near, rim - near))

    def send(part, side):
        first, count = parts[part]
        start = (rows - first - count, first)[side]
        return pltpu.make_async_remote_copy(
            src_ref=normed.at[pl.ds(start, count)],
            dst_ref=halo.at[pl.ds(2 * first + side * count, count)],
            send_sem=sent.at[part, side],
            recv_sem=came.at[part, side],
            device_id=(after, before)[side],
            device_id_type=MESH,
        )

    sends = (seq < size - 1, seq > 0)
    for part in range(2):
        for side in range(2):
            pl.when(sends[side])(send(part, side).start)

    pad = rows - rim
    window[:, :, 0:pad] = jnp.zeros((3, HEADS, pad, LANES), jnp.bfloat16)
    window[:, :, span - pad : span] = jnp.zeros((3, HEADS, pad, LANES), jnp.bfloat16)

    def store_own(part, h, value):
        window[part, h, rows : 2 * rows] = value

    for p, copy in enumerate(copies):
        copy.wait()
        project(normed, held.at[p], bias, p, store_own)
    for i in range(blocks):
        same = id_col[rows + i * LANES : rows + (i + 1) * LANES] == (
            id_row[:, i * LANES : i * LANES + reach]
        )
        hide[i] = jnp.where(same, 0.0, HIDE)
    lane = lanes_of((LANES, LANES))

    def queries(h, i):
        return window[0, h, rows + i * LANES : rows + (i + 1) * LANES]

    def own_body(pair, carry):
        jobs = [(2 * pair + k, i) for k in range(2) for i in range(blocks)]
        scores = [
            dot_nt(queries(h, i), window[1, h, rows : 2 * rows]) * SCALE2
            + hide[i, :, rows - i * LANES : 2 * rows - i * LANES]
            for h, i in jobs
        ]
        highest = [jnp.max(value, axis=-1, keepdims=True) for value in scores]
        raised = [
            jnp.exp2(value - most).astype(jnp.bfloat16) for value, most in zip(scores, highest)
        ]
        totals = [dot(value, window[2, h, rows : 2 * rows]) for value, (h, i) in zip(raised, jobs)]
        for total, most, (h, i) in zip(totals, highest, jobs):
            at = slice(i * LANES, (i + 1) * LANES)
            own_part[h, at] = jnp.where(lane == LANES - 1, most, total)
        return carry

    lax.fori_loop(0, HEADS // 2, own_body, 0)

    wide = shrink.shape[0] // 4
    loads = [
        pltpu.make_async_copy(
            shrink.at[pl.ds(wide * t, wide)], shrink_tile.at[t % 2], wide_sems.at[0, t % 2]
        )
        for t in range(4)
    ]
    stores = [
        pltpu.make_async_copy(
            grad_tile.at[t % 2], active_grad.at[:, pl.ds(wide * t, wide)], wide_sems.at[1, t % 2]
        )
        for t in range(4)
    ]
    loads[0].start()
    for t in range(4):
        if t < 3:
            loads[t + 1].start()
        loads[t].wait()
        if t > 1:
            stores[t - 2].wait()
        grad_tile[t % 2] = dot_nt(upstream[...], shrink_tile[t % 2])
        stores[t].start()

    for part, (first, count) in enumerate(parts):
        here = pl.ds(2 * first, 2 * count)
        for side in range(2):
            pl.when(sends[1 - side])(send(part, side).wait_recv)

            @pl.when(jnp.logical_not(sends[1 - side]))
            def _():
                halo[2 * first + side * count : 2 * first + (side + 1) * count] = jnp.zeros(
                    (count, features), jnp.bfloat16
                )

        def store_rim(p, h, value):
            window[p, h, rows - first - count : rows - first] = value[:count]
            window[p, h, 2 * rows + first : 2 * rows + first + count] = value[count:]

        for p in (1, 2, 0):
            project(halo.at[here], held.at[p], bias, p, store_rim)
    out_copies = [
        pltpu.make_async_copy(window.at[p], wins.at[p], out_sems.at[p]) for p in range(3)
    ]
    for copy in out_copies:
        copy.start()
    lse[...] = jnp.zeros_like(lse)

    def rim_body(pair, carry):
        jobs = [(2 * pair + k, i) for k in range(2) for i in range(blocks)]

        def keys(part, h, i):
            return jnp.concatenate(
                [
                    window[part, h, i * LANES : rows],
                    window[part, h, 2 * rows : 2 * rows + (i + 1) * LANES],
                ],
                axis=0,
            )

        def hidden(i):
            return jnp.concatenate(
                [hide[i, :, : rows - i * LANES], hide[i, :, 2 * rows - i * LANES :]], axis=1
            )

        scores = [dot_nt(queries(h, i), keys(1, h, i)) * SCALE2 + hidden(i) for h, i in jobs]
        owns = [own_part[h, i * LANES : (i + 1) * LANES] for h, i in jobs]
        own_most = [value[:, LANES - 1 :] for value in owns]
        highest = [
            jnp.maximum(jnp.max(value, axis=-1, keepdims=True), most)
            for value, most in zip(scores, own_most)
        ]
        raised = [
            jnp.exp2(value - most).astype(jnp.bfloat16) for value, most in zip(scores, highest)
        ]
        totals = [dot(value, keys(2, h, i)) for value, (h, i) in zip(raised, jobs)]
        for total, own, low, most, (h, i) in zip(totals, owns, own_most, highest, jobs):
            at = slice(i * LANES, (i + 1) * LANES)
            total = total + own * jnp.exp2(low - most)
            denominator = total[:, HEAD_DIM : HEAD_DIM + 1]
            gathered[h, at] = (total / denominator).astype(jnp.bfloat16)
            lse[at] = jnp.where(lane == h, most + jnp.log2(denominator), lse[at])
        return carry

    lax.fori_loop(0, HEADS // 2, rim_body, 0)
    for h in range(HEADS):
        mixed[:, HEAD_DIM * h : HEAD_DIM * (h + 1)] = gathered[h, :, :HEAD_DIM]
    for copy in out_copies + stores[2:]:
        copy.wait()
    for part in range(2):
        for side in range(2):
            pl.when(sends[side])(send(part, side).wait_send)


def forward(
    tok, skp, skip_weight, skip_bias, gain, shift, weight, bias, id_col, id_row, upstream, shrink
):
    rows, features = tok.shape
    span = 3 * rows
    rim = (ITEM_MOST - 1 + 15) // 16 * 16
    low, full = jnp.bfloat16, jnp.float32
    return pl.pallas_call(
        forward_kernel,
        out_shape=(
            jax.ShapeDtypeStruct((rows, features), full),
            jax.ShapeDtypeStruct((rows, features), low),
            jax.ShapeDtypeStruct((3, HEADS, span, LANES), low),
            jax.ShapeDtypeStruct((rows, features), low),
            jax.ShapeDtypeStruct((rows, LANES), full),
            jax.ShapeDtypeStruct((rows, shrink.shape[0]), full),
        ),
        in_specs=[
            whole(), whole(), anywhere(), whole(), whole(), whole(), anywhere(), whole(), whole(),
            whole(), whole(), anywhere(),
        ],
        out_specs=(whole(), whole(), anywhere(), whole(), whole(), anywhere()),
        scratch_shapes=[
            pltpu.VMEM((3, HEADS, span, LANES), low),
            pltpu.VMEM((2 * rim, features), low),
            pltpu.VMEM((3, features, features), low),
            pltpu.VMEM((3, 2 * features, 384), low),
            pltpu.VMEM((rows // LANES, LANES, span - rows + LANES), full),
            pltpu.VMEM((HEADS, rows, LANES), full),
            pltpu.VMEM((HEADS, rows, LANES), low),
            pltpu.VMEM((2, shrink.shape[0] // 4, features), low),
            pltpu.VMEM((2, rows, shrink.shape[0] // 4), full),
            pltpu.SemaphoreType.DMA((6,)),
            pltpu.SemaphoreType.DMA((3,)),
            pltpu.SemaphoreType.DMA((2, 2)),
            pltpu.SemaphoreType.DMA((2, 2)),
            pltpu.SemaphoreType.DMA((2, 2)),
        ],
        compiler_params=pltpu.CompilerParams(
            collective_id=1, has_side_effects=True, vmem_limit_bytes=VMEM_MOST
        ),
        name="forward",
    )(
        tok, skp, skip_weight, skip_bias, gain, shift, weight, bias, id_col, id_row, upstream,
        shrink,
    )


def by_core_store(ref, value):
    blank = jnp.zeros((value.shape[0], 32), value.dtype)
    for b in range(4):
        x, c = b // 2, b % 2
        ref[c, 0, :, 256 * x : 256 * x + 256] = value[:, 288 * b : 288 * b + 256]
        rest = value[:, 288 * b + 256 : 288 * b + 288]
        ref[c, 0, :, 512 + LANES * x : 640 + LANES * x] = jnp.concatenate(
            [rest, rest, rest, blank], axis=1
        )


def split3(value):
    first = value.astype(jnp.bfloat16)
    rest = value - first.astype(jnp.float32)
    second = rest.astype(jnp.bfloat16)
    return first, second, (rest - second.astype(jnp.float32)).astype(jnp.bfloat16)


def layer_kernel(
    stream, mixed, lse, upstream, active_grad, proj, proj_bias, gain, shift, expand, expand_bias,
    shrink, shrink_bias, result, active, hidden_by_core, second, branch, branch_by_core, up_by_core,
    middle_grad, mixed_grad, sums, middle, total, second_grad,
    bias_rows,
):
    step, steps = pl.program_id(0), pl.num_programs(0)
    low = jnp.bfloat16
    wide = expand.shape[1]

    @pl.when(step == 0)
    def _():
        middle[...] = (
            stream[...] + dot(mixed[...], proj[...]) + vector(proj_bias)
        )
        unit, _ = row_norm(middle[...])
        second[...] = (unit * vector(gain) + vector(shift)).astype(low)
        total[...] = middle[...] + vector(shrink_bias)
        second_grad[...] = jnp.zeros_like(second_grad)
        for t in range(4):
            bias_rows[t : t + 1] = vector(expand_bias, wide * t, wide)
        by_core_store(up_by_core, upstream[...])

    hidden = dot(second[...], expand[...]) + bias_rows[pl.ds(step, 1)]
    cdf = 0.5 + 0.5 * erf(hidden * (1.0 / ROOT2))
    density = jnp.exp(-0.5 * hidden * hidden) * 0.3989422804014327
    raised = (hidden * cdf).astype(low)
    active[...] = raised
    hidden_grad = (active_grad[...] * (cdf + hidden * density)).astype(low)
    for j in range(3):
        hidden_by_core[0, j] = hidden_grad[:, 384 * j : 384 * (j + 1)]
    sums[pl.ds(9 + step, 1)] = dot(jnp.ones((16, hidden_grad.shape[0]), low), hidden_grad)[0:1]
    total[...] += dot(raised, shrink[...])
    second_grad[...] += dot_nt(hidden_grad, expand[...])

    @pl.when(step == steps - 1)
    def _():
        result[...] = total[...].astype(low)
        unit, scale = row_norm(middle[...])
        cotangent = second_grad[...]
        above = upstream[...].astype(jnp.float32)
        grad = above + norm_back(unit, scale, vector(gain), cotangent)
        middle_grad[...] = grad
        branched = grad.astype(low)
        branch[...] = branched
        by_core_store(branch_by_core, branched)
        sums[0:5] = jnp.zeros((5, sums.shape[1]), jnp.float32)
        ones = jnp.ones((16, branched.shape[0]), low)
        sums[5:6] = dot(ones, branched)[0:1]
        sums[6:7] = column_sum(cotangent * unit)
        sums[7:8] = column_sum(cotangent)
        sums[8:9] = dot(ones, upstream[...])[0:1]
        sums[13:16] = jnp.zeros((3, sums.shape[1]), jnp.float32)
        back = dot_nt(branched, proj[...]).astype(low)
        features = back.shape[1]
        mixed_grad[:, :features] = back
        products = back.astype(jnp.float32) * mixed[...].astype(jnp.float32)
        shape = (features, LANES)
        member = lax.broadcasted_iota(jnp.int32, shape, 0) // HEAD_DIM == lanes_of(shape)
        member = jnp.where(member, 1.0, 0.0).astype(low)
        high = products.astype(low)
        inner = dot(high, member) + dot((products - high.astype(jnp.float32)).astype(low), member)
        pieces = [part[:, :HEADS] for part in split3(lse[...] * (-1.0 / SCALE2)) + split3(-inner)]
        blank = jnp.zeros((back.shape[0], LANES - 6 * HEADS), low)
        mixed_grad[:, features:] = jnp.concatenate(pieces + [blank], axis=1)


def layer(stream, mixed, lse, upstream, active_grad, weights):
    proj, proj_bias, gain, shift, expand, expand_bias, shrink, shrink_bias = weights
    rows, features = stream.shape
    hidden = expand.shape[1]
    wide = hidden // 4
    low = jnp.bfloat16

    def held(shape):
        return pl.BlockSpec(shape, lambda t: (0,) * len(shape))

    narrow = (rows, features)
    split = (2, 1, rows, 768)
    return pl.pallas_call(
        layer_kernel,
        grid=(4,),
        in_specs=[
            held(narrow), held(narrow), held((rows, LANES)), held(narrow),
            pl.BlockSpec((rows, wide), lambda t: (0, t)),
            held((features, features)), whole(), whole(), whole(),
            pl.BlockSpec((features, wide), lambda t: (0, t)),
            whole(),
            pl.BlockSpec((wide, features), lambda t: (t, 0)),
            whole(),
        ],
        out_specs=(
            held(narrow),
            pl.BlockSpec((rows, wide), lambda t: (0, t)),
            pl.BlockSpec((1, 3, rows, 384), lambda t: (t % 2, 0, 0, t // 2)),
            held(narrow), held(narrow), held(split), held(split), held(narrow),
            held((rows, features + LANES)),
            held((16, features)),
        ),
        out_shape=(
            jax.ShapeDtypeStruct(narrow, low),
            jax.ShapeDtypeStruct((rows, hidden), low),
            jax.ShapeDtypeStruct((2, 3, rows, 768), low),
            jax.ShapeDtypeStruct(narrow, low),
            jax.ShapeDtypeStruct(narrow, low),
            jax.ShapeDtypeStruct(split, low),
            jax.ShapeDtypeStruct(split, low),
            jax.ShapeDtypeStruct(narrow, jnp.float32),
            jax.ShapeDtypeStruct((rows, features + LANES), low),
            jax.ShapeDtypeStruct((16, features), jnp.float32),
        ),
        scratch_shapes=[pltpu.VMEM(narrow, jnp.float32)] * 3
        + [pltpu.VMEM((4, wide), jnp.float32)],
        compiler_params=params(),
        name="layer",
    )(
        stream, mixed, lse, upstream, active_grad, proj, proj_bias, gain, shift, expand,
        expand_bias, shrink, shrink_bias,
    )


def back_masks(id_col, id_row, own_hide, rim_hide, rows):
    blocks = rows // LANES
    reach = own_hide.shape[2]

    def hidden(first, keys, width):
        same = id_col[first : first + LANES] == id_row[:, keys : keys + width]
        return jnp.where(same, 0.0, HIDE).astype(own_hide.dtype)

    for i in range(blocks):
        own_hide[i] = hidden(rows + i * LANES, i * LANES, reach)
    for w in range(blocks):
        rim_hide[w] = hidden(w * LANES, rows, rows)
        rim_hide[blocks + w] = hidden(2 * rows + w * LANES, rows, rows)


def with_stats(value, stats, shift):
    return jnp.where(marked(lanes_of(value.shape)), pltpu.roll(stats, shift, 1), value)


def back_head(h, queries, keys, values, grads, stats, own_hide, rim_hide, probs, scored):
    span = queries.shape[0]
    rows = span // 3
    blocks = rows // LANES
    reach = span - rows + LANES
    low, full = jnp.bfloat16, jnp.float32
    queries[...] = with_stats(queries[...], stats, MARKS[0] - h)
    turn = MARKS[0] - 3 * HEADS - h
    grads[...] = with_stats(grads[...], stats, jnp.where(turn < 0, turn + LANES, turn))
    jobs = []
    for i in range(blocks):
        jobs.append(
            (rows + i * LANES, i * LANES, reach, own_hide[i], rows - i * LANES, rows, 0)
        )
    for w in range(blocks):
        width = (w + 1) * LANES
        jobs.append((w * LANES, rows, width, rim_hide[w][:, :width], 0, width, 0))
        first, width = w * LANES, rows - w * LANES
        hide = rim_hide[blocks + w][:, first:]
        jobs.append((2 * rows + first, rows + first, width, hide, 0, width, first))
    scores = [dot_nt(queries[q : q + LANES], keys[k : k + n]) for q, k, n, *_ in jobs]
    inner = [dot_nt(grads[q : q + LANES], values[k : k + n]) for q, k, n, *_ in jobs]
    weights = [
        jnp.exp2(value * SCALE2 + job[3].astype(full)) for value, job in zip(scores, jobs)
    ]
    scores = [(weight * value).astype(low) for weight, value in zip(weights, inner)]
    weights = [weight.astype(low) for weight in weights]
    for weight, score, (q, _, _, _, first, count, place) in zip(weights, scores, jobs):
        probs[q : q + LANES, place : place + count] = weight[:, first : first + count]
        scored[q : q + LANES, place : place + count] = score[:, first : first + count]
    factor = HEAD_DIM**-0.5
    query_grad = jnp.concatenate(
        [dot(scores[i], keys[i * LANES : i * LANES + reach]) * factor for i in range(blocks)], axis=0
    )
    key_grad = dot_tn(scored[...], queries[...]) * factor
    value_grad = dot_tn(probs[...], grads[...])
    return query_grad.astype(low), key_grad.astype(low), value_grad.astype(low)


def heads_apart(row_ref, out):
    value = row_ref[...]
    for h in range(HEADS):
        out[h] = head_tile(value[:, : HEADS * HEAD_DIM], h, False)


def triple_store(apart, triple):
    features = HEADS * HEAD_DIM
    for p in range(3):
        for h in range(HEADS):
            at = features * p + HEAD_DIM * h
            triple[:, at : at + HEAD_DIM] = apart[p, h, :, :HEAD_DIM]


def attend_back_kernel(
    wins, grads_in, stats, id_col, id_row, triple, sums,
    window, grads, own_hide, rim_hide, probs, scored, apart, sems,
):
    span = window.shape[2]
    rows = span // 3
    copy = pltpu.make_async_copy(wins, window, sems.at[0])
    copy.start()
    back_masks(id_col, id_row, own_hide, rim_hide, rows)
    probs[...] = jnp.zeros_like(probs)
    scored[...] = jnp.zeros_like(scored)
    heads_apart(grads_in, grads)
    copy.wait()

    def body(h, carry):
        found = back_head(
            h, window.at[0, h], window.at[1, h], window.at[2, h], grads.at[h], stats[...],
            own_hide, rim_hide, probs, scored,
        )
        for part, value in enumerate(found):
            apart[part, h] = value
        return carry

    lax.fori_loop(0, HEADS, body, 0)
    triple_store(apart, triple)
    sums[...] = column_sum(triple[...].astype(jnp.float32))


def attend_back(wins, grads_in, stats, id_col, id_row):
    span = wins.shape[2]
    rows = span // 3
    features = HEADS * HEAD_DIM
    low = jnp.bfloat16
    return pl.pallas_call(
        attend_back_kernel,
        out_shape=(
            jax.ShapeDtypeStruct((rows, 3 * features), low),
            jax.ShapeDtypeStruct((1, 3 * features), jnp.float32),
        ),
        in_specs=[anywhere(), whole(), whole(), whole(), whole()],
        out_specs=(whole(), whole()),
        scratch_shapes=[
            pltpu.VMEM((3, HEADS, span, LANES), low),
            pltpu.VMEM((HEADS, span, LANES), low),
            pltpu.VMEM((rows // LANES, LANES, span - rows + LANES), low),
            pltpu.VMEM((2 * rows // LANES, LANES, rows), low),
            pltpu.VMEM((span, rows), low),
            pltpu.VMEM((span, rows), low),
            pltpu.VMEM((3, HEADS, rows, LANES), low),
            pltpu.SemaphoreType.DMA((1,)),
        ],
        compiler_params=params(),
        name="attend_back",
    )(wins, grads_in, stats, id_col, id_row)


def stream_back_kernel(
    triple, weight, stream, middle_grad, gain, skip_weight, tok_grad, skip_grad, by_core, sums, held, held_skip, grad, sems,
):
    features = stream.shape[1]
    low = jnp.bfloat16
    copies = [
        pltpu.make_async_copy(weight.at[:, pl.ds(features * p, features)], held.at[p], sems.at[p])
        for p in range(3)
    ]
    copies += [
        pltpu.make_async_copy(
            skip_weight.at[pl.ds(features * p, features)], held_skip.at[p], sems.at[3 + p]
        )
        for p in range(2)
    ]
    for copy in copies:
        copy.start()
    unit, scale = row_norm(stream[...])
    for p in range(3):
        copies[p].wait()
        part = dot_nt(triple[:, features * p : features * (p + 1)], held[p])
        if p == 0:
            grad[...] = part
        else:
            grad[...] += part
    cotangent = grad[...]
    sums[0:1] = column_sum(cotangent * unit)
    sums[1:2] = column_sum(cotangent)
    whole_grad = middle_grad[...] + norm_back(unit, scale, vector(gain), cotangent)
    rounded = whole_grad.astype(low)
    by_core_store(by_core, rounded)
    sums[2:3] = column_sum(rounded.astype(jnp.float32))
    for p, out in enumerate((tok_grad, skip_grad)):
        copies[3 + p].wait()
        out[...] = dot_nt(rounded, held_skip[p]).astype(low)


def stream_back(triple, weight, stream, middle_grad, gain, skip_weight):
    rows, features = stream.shape
    low = jnp.bfloat16
    return pl.pallas_call(
        stream_back_kernel,
        out_shape=(
            jax.ShapeDtypeStruct((rows, features), low),
            jax.ShapeDtypeStruct((rows, features), low),
            jax.ShapeDtypeStruct((2, 1, rows, 768), low),
            jax.ShapeDtypeStruct((8, features), jnp.float32),
        ),
        in_specs=[whole(), anywhere(), whole(), whole(), whole(), anywhere()],
        out_specs=(whole(), whole(), whole(), whole()),
        scratch_shapes=[
            pltpu.VMEM((3, features, features), low),
            pltpu.VMEM((2, features, features), low),
            pltpu.VMEM((rows, features), jnp.float32),
            pltpu.SemaphoreType.DMA((5,)),
        ],
        compiler_params=params(),
        name="stream_back",
    )(triple, weight, stream, middle_grad, gain, skip_weight)


ROWS = 144
THIRD = ROWS // 3


class Unit:
    def __init__(self, left, left_at, right, right_at, tiles, blocks, out, out_at):
        self.left, self.left_at = left, left_at
        self.right, self.right_at = right, right_at
        self.tiles = tiles
        self.blocks = blocks
        self.out, self.out_at = out, out_at
        self.rows = ROWS * tiles if tiles else 2 * ROWS + THIRD
        self.z_of = {(order, place): z for _, order, _, place, z in blocks}


ORDER_OF = (0, 1, 1, 0)
QUARTERS = tuple(
    ((2 * z + y) * ROWS, ORDER_OF[z], y, z // 2, z) for z in range(4) for y in range(2)
)


SHRINK, EXPAND, PROJ, ATTN, SKIP = (0, 1, 2, 3), (4, 5, 6), 7, (8, 9, 10), (11, 12)
START, TURN, SETTLE, HOP, FINISH, LINE, LINE_END, LINE_X, LINE_Y = range(9)
HALO, HEAD, PACK, BACK, NORM, OUT, VECTOR = range(9, 16)


def make_units():
    units = {}
    for z in range(4):
        blocks = [
            (y * 576 + q * ROWS, q // 2, y, q % 2, z) for y in range(2) for q in range(4)
        ]
        units[SHRINK[z]] = Unit("active", z * 1152, "upstream", 0, 0, blocks, "shrink", 0)
    for j in range(3):
        units[EXPAND[j]] = Unit("second", 0, "hidden", j, 3, QUARTERS, "expand", 3 * j)
    units[PROJ] = Unit("mixed", 0, "branch", 0, 0, QUARTERS, "proj", 0)
    for j, (first, tiles) in enumerate(TRIPLE_TILES):
        units[ATTN[j]] = Unit("normed", 0, f"triple{j}", 0, tiles, QUARTERS, "attn", first)
    for k, name in enumerate(("tok", "skp")):
        blocks = [
            (h * 576 + y * 288 + i * ROWS, h, y, i, 2 * k + h)
            for h in range(2)
            for y in range(2)
            for i in range(2)
        ]
        units[SKIP[k]] = Unit(name, 0, "stream_cols", 0, 0, blocks, "skip", 0)
    return units


TRIPLE_TILES = ((0, 3), (3, 2), (5, 2))
GRADS = (
    ("shrink", (576, 288)),
    ("expand", (144, 1152)),
    ("proj", (144, 288)),
    ("attn", (144, 864)),
    ("skip", (288, 288)),
)
PART_SLOTS, FIRST_SLOTS, SECOND_SLOTS, LAST_SLOTS = 4, 4, 4, 5
LINE_FIRST = (PROJ, EXPAND[0], ATTN[0])
X_FIRST = (SHRINK[0], EXPAND[1], ATTN[1])
PLAN = (
    (START, PROJ), (LINE, PROJ, 1, 0), (LINE, PROJ, 1, 1), (LINE, PROJ, 1, 2), (START, SHRINK[0]),
    (START, EXPAND[2]), (START, SHRINK[2]), (LINE, PROJ, 2, 0), (LINE, PROJ, 2, 1), (LINE, PROJ, 3, 0),
    (TURN, SHRINK[0]), (LINE_END, PROJ), (START, EXPAND[0]), (LINE, EXPAND[0], 1, 0),
    (LINE, EXPAND[0], 1, 1), (LINE, EXPAND[0], 1, 2), (START, EXPAND[1]), (HALO,), (HEAD, 2),
    (LINE_X, PROJ), (HEAD, 2), (LINE, EXPAND[0], 2, 0), (TURN, EXPAND[2]), (HEAD, 4), (TURN, SHRINK[2]),
    (LINE, EXPAND[0], 2, 1), (HEAD, 2), (LINE, EXPAND[0], 3, 0), (TURN, EXPAND[1]), (SETTLE, SHRINK[0]),
    (START, SHRINK[1]), (LINE_Y, PROJ), (HEAD, 2), (SETTLE, EXPAND[2]), (START, SHRINK[3]),
    (SETTLE, SHRINK[2]), (HOP, SHRINK[0], 2), (HEAD, 2), (HOP, EXPAND[2], 2), (LINE_END, EXPAND[0]),
    (HEAD, 2), (SETTLE, EXPAND[1]), (HOP, SHRINK[0], 3), (PACK,), (HOP, SHRINK[2], 2),
    (HOP, SHRINK[2], 3), (HOP, EXPAND[2], 3), (START, ATTN[0]), (START, ATTN[1]), (LINE_X, EXPAND[0]),
    (HOP, EXPAND[1], 2), (TURN, SHRINK[1]), (LINE, ATTN[0], 1, 0), (LINE, ATTN[0], 1, 1),
    (LINE, ATTN[0], 1, 2), (START, ATTN[2]), (FINISH, SHRINK[0]), (BACK, 0), (HOP, EXPAND[1], 3),
    (TURN, SHRINK[3]), (BACK, 1), (LINE_Y, EXPAND[0]), (BACK, 2), (TURN, ATTN[1]), (LINE, ATTN[0], 2, 0),
    (NORM,), (SETTLE, SHRINK[1]), (START, SKIP[0]), (LINE, ATTN[0], 2, 1), (FINISH, SHRINK[2]),
    (VECTOR, 0), (FINISH, EXPAND[2]), (FINISH, EXPAND[1]), (TURN, ATTN[2]), (VECTOR, 1),
    (SETTLE, SHRINK[3]), (LINE, ATTN[0], 3, 0), (START, SKIP[1]), (SETTLE, ATTN[1]), (OUT, 0), (OUT, 1),
    (OUT, 2), (TURN, SKIP[0]), (HOP, SHRINK[1], 2), (HOP, SHRINK[1], 3), (HOP, SHRINK[3], 2),
    (SETTLE, ATTN[2]), (VECTOR, 2), (HOP, ATTN[1], 2), (FINISH, SHRINK[1]), (LINE_END, ATTN[0]),
    (HOP, SHRINK[3], 3), (HOP, ATTN[1], 3), (HOP, ATTN[2], 2), (HOP, ATTN[2], 3), (TURN, SKIP[1]),
    (SETTLE, SKIP[0]), (VECTOR, 3), (HOP, SKIP[0], 2), (FINISH, SHRINK[3]), (LINE_X, ATTN[0]),
    (FINISH, ATTN[1]), (SETTLE, SKIP[1]), (FINISH, ATTN[2]), (HOP, SKIP[0], 3), (HOP, SKIP[1], 2),
    (VECTOR, 4), (LINE_Y, ATTN[0]), (HOP, SKIP[1], 3), (FINISH, SKIP[0]), (FINISH, SKIP[1]), (VECTOR, 5),
)


def add_into(target, other):
    target[...] = (target[...].astype(jnp.float32) + other[...].astype(jnp.float32)).astype(
        target.dtype
    )


class Refs(dict):
    __getattr__ = dict.__getitem__


def gradient_kernel(r):
    seq, batch = lax.axis_index(SEQ), lax.axis_index(BATCH)
    z, y = seq // 2, seq % 2
    x, c = batch // 2, batch % 2
    at = {
        "core": (seq, 2 * x + (1 - c)),
        "x": (seq, 2 * (1 - x) + c),
        "y": (2 * z + (1 - y), batch),
        "above": (2 * jnp.minimum(z + 1, 3) + y, batch),
        "below": (2 * jnp.maximum(z - 1, 0) + y, batch),
        "far": (2 * ((z + 2) % 4) + y, batch),
        "next": (jnp.minimum(seq + 1, 7), batch),
        "last": (jnp.maximum(seq - 1, 0), batch),
    }
    at["pair"] = (2 * (z + 1 - 2 * (z % 2)) + y, batch)
    units = make_units()
    low = jnp.bfloat16
    rows, features = r.tok.shape
    ids = {}

    def remote(key, src, dst, side):
        i = ids.setdefault(key, len(ids))
        return pltpu.make_async_remote_copy(
            src_ref=src,
            dst_ref=dst,
            send_sem=r.sent.at[i],
            recv_sem=r.came.at[i],
            device_id=at[side],
            device_id_type=MESH,
        )

    barrier = pltpu.get_barrier_semaphore()

    def greet(side):
        pl.semaphore_signal(barrier, 1, device_id=at[side], device_id_type=MESH)

    for side in ("core", "x", "y", "far"):
        greet(side)
    for side, some in (
        ("above", z < 3),
        ("below", z > 0),
        ("next", (y == 1) & (z < 3)),
        ("last", (y == 0) & (z > 0)),
    ):
        pl.when(some)(lambda side=side: greet(side))
    more = (z < 3).astype(jnp.int32) + (z > 0).astype(jnp.int32)
    diagonal = jnp.where(y == 1, (z < 3).astype(jnp.int32), (z > 0).astype(jnp.int32))
    pl.semaphore_wait(barrier, 4 + more + diagonal)

    rim = (ITEM_MOST - 1 + 15) // 16 * 16
    window = r.window
    halo_up = remote(
        "halo_up", r.grads.at[pl.ds(rows - rim, rim)], window.at[pl.ds(rows - rim, rim)], "next"
    )
    halo_down = remote(
        "halo_down", r.grads.at[pl.ds(0, rim)], window.at[pl.ds(2 * rows, rim)], "last"
    )
    pl.when(seq < 7)(halo_up.start)
    pl.when(seq > 0)(halo_down.start)

    swaps = {}

    def swap(side, name, first):
        key = (side, name, first)
        if key in swaps:
            return
        if side == "left":
            cols = pl.ds(first, features)
            src, dst = r[name].at[:, cols], r["far_" + name].at[:, cols]
        else:
            src, dst = r[name].at[1 - c, first], r["far_" + name].at[first]
        swaps[key] = remote(key, src, dst, "core")
        swaps[key].start()

    def swap_unit(name):
        unit = units[name]
        swap("left", unit.left, unit.left_at)
        swap("right", unit.right, unit.right_at)

    order = [rest[0] for kind, *rest in PLAN if kind == START]
    for name in order:
        unit = units[name]
        swap("left", unit.left, unit.left_at)
        if not unit.right.startswith(("triple", "stream")):
            swap("right", unit.right, unit.right_at)

    slots, loads, here = {}, {}, set()

    def load(side, name, first, busy=None):
        key = (side, name, first)
        if key in slots:
            return
        slot = 1 - slots.get(busy, 1)
        for other in [k for k in slots if k[0] == side and slots[k] == slot]:
            del slots[other]
        slots[key] = slot
        if key not in here:
            swaps[key].wait_recv()
            here.add(key)
        if side == "left":
            cols = pl.ds(first, features)
            near, far = r[name].at[:, cols], r["far_" + name].at[:, cols]
            hold = r.lefts.at[slot]
        else:
            near, far = r[name].at[c, first], r["far_" + name].at[first]
            hold = r.rights.at[slot, :, pl.ds(0, near.shape[-1])]
        loads[key] = []
        for half, src in ((0, near), (1, far)):
            copy = pltpu.make_async_copy(
                src, hold.at[pl.ds(rows * half, rows)], r[side + "_sem"].at[slot, half]
            )
            copy.start()
            loads[key].append(copy)

    def keys_of(name):
        unit = units[name]
        return ("left", unit.left, unit.left_at), ("right", unit.right, unit.right_at)

    started = [name for name in order if name not in LINE_FIRST]
    both = slice(None)

    def axes(u, order):
        return ("x", "y") if order == 0 or started[u] in X_FIRST else ("y", "x")

    def credit(stage, order, side):
        return r.credit.at[(stage * 2 + order) * 2 + ("x", "y").index(side)]

    def take_credit(u, stage, order):
        if u >= (FIRST_SLOTS, SECOND_SLOTS)[stage]:
            pl.semaphore_wait(credit(stage, order, axes(u, order)[stage]), 1)

    def give_credit(u, stage, order):
        then = u + (FIRST_SLOTS, SECOND_SLOTS)[stage]
        if then < len(started):
            side = axes(then, order)[stage]
            pl.semaphore_signal(
                credit(stage, order, side), 1, device_id=at[side], device_id_type=MESH
            )

    def part_of(u, order, *index):
        unit = units[started[u]]
        place = (pl.ds(0, 2), pl.ds(0, unit.rows)) if len(index) < 3 else (pl.ds(0, unit.rows),)
        return r.part.at[(u % PART_SLOTS, order, *index, *place)]

    def moved(u, order, stage):
        land = r.land_one if stage == 0 else r.land_two
        land = land.at[u % (FIRST_SLOTS, SECOND_SLOTS)[stage], order]
        height = pl.ds(0, units[started[u]].rows)
        if stage == 1:
            send = (x, 1 - y) if axes(u, order)[1] == "y" else (1 - x, y)
            return part_of(u, order, *send), part_of(u, order, x, y), land.at[:, height]
        if axes(u, order)[0] == "x":
            send, keep = (1 - x, both), (x, both)
        else:
            send, keep = (both, 1 - y), (both, y)
        return part_of(u, order, *send), part_of(u, order, *keep), land.at[:, :, height]

    def stage_copy(u, order, stage):
        send, _, land = moved(u, order, stage)
        return remote((u, stage, order), send, land, axes(u, order)[stage])

    def compute(name, part, slot):
        unit = units[name]
        left_key, right_key = keys_of(name)
        left, right = r.lefts.at[slots[left_key]], r.rights.at[slots[right_key]]

        def product(n):
            cols = pl.ds(pl.multiple_of(n * 256, 256), 256)
            return dot_tn(left[...], right[:, cols])

        if unit.tiles:

            def body(n, carry):
                tile = product(n).astype(low)
                for i in range(2):
                    g = 2 * n + i
                    x_at = g // unit.tiles
                    t = pl.multiple_of((g - x_at * unit.tiles) * ROWS, 16)
                    for first, order, y_at, place, _ in unit.blocks:
                        part[slot, order, x_at, y_at, place, pl.ds(t, ROWS)] = tile[
                            first : first + ROWS, i * LANES : (i + 1) * LANES
                        ]
                return carry

            lax.fori_loop(0, unit.tiles, body, 0)
            return

        def body(n, carry):
            tile = product(n).astype(low)
            for first, order, y_at, place, _ in unit.blocks:
                for i in range(2):
                    part[slot, order, n, y_at, place, pl.ds(i * ROWS, ROWS)] = tile[
                        first : first + ROWS, i * LANES : (i + 1) * LANES
                    ]
            return carry

        lax.fori_loop(0, 2, body, 0)
        tile = product(2).astype(low)
        lane = lanes_of((THIRD, LANES))
        for first, order, y_at, place, _ in unit.blocks:
            for x_at in range(2):
                pieces = [
                    tile[first + s * THIRD : first + (s + 1) * THIRD, x_at * LANES :][:, :LANES]
                    for s in range(3)
                ]
                packed = jnp.where(
                    lane < 32, pieces[0], jnp.where(lane < 64, pieces[1], pieces[2])
                )
                part[slot, order, x_at, y_at, place, pl.ds(2 * ROWS, THIRD)] = packed

    def wait_sends(u):
        for order in range(2):
            for stage in range(2):
                stage_copy(u, order, stage).wait_send()

    def fetch(name, ahead):
        for key in keys_of(name):
            load(*key)
            for copy in loads.pop(key, ()):
                copy.wait()
        if ahead is not None and ahead not in SKIP:
            for key, busy in zip(keys_of(ahead), keys_of(name)):
                if key in swaps:
                    load(*key, busy)

    def first_stage(u):
        if u >= PART_SLOTS:
            wait_sends(u - PART_SLOTS)
        compute(started[u], r.part, u % PART_SLOTS)
        for order in range(2):
            take_credit(u, 0, order)
            stage_copy(u, order, 0).start()

    def second_stage(u):
        for order in range(2):
            stage_copy(u, order, 0).wait_recv()
            _, keep, land = moved(u, order, 0)
            add_into(keep, land)
            give_credit(u, 0, order)
            take_credit(u, 1, order)
            stage_copy(u, order, 1).start()

    def last_ref(u, order, place):
        return r.ends.at[u % LAST_SLOTS, order, place, pl.ds(0, units[started[u]].rows)]

    def third_stage(u):
        if u >= LAST_SLOTS:
            chain_sends(u - LAST_SLOTS)
        for order in range(2):
            stage_copy(u, order, 1).wait_recv()
            _, keep, land = moved(u, order, 1)
            for place in range(2):
                value = keep.at[place][...].astype(jnp.float32)
                value = value + land.at[place][...].astype(jnp.float32)
                last_ref(u, order, place)[...] = value.astype(low)
            give_credit(u, 1, order)

    def chain_copy(u, order, place, up):
        pool, i = r.chain_at[started[u], order, place, up]
        dst = r[pool].at[i, pl.ds(0, units[started[u]].rows)]
        src = last_ref(u, order, place)
        key = (u, "chain", order, place, up)
        return remote(key, src, dst, "above" if up else "below"), dst

    def hop(u, step):
        for up, me in ((True, step - 1), (False, 4 - step)):
            todo = [
                key
                for key, z_at in sorted(
                    units[started[u]].z_of.items(), key=lambda item: -item[1] if up else item[1]
                )
                if ((z_at > me) if up else (z_at < me))
            ]

            @pl.when(z == me)
            def _():
                for order, place in todo:
                    copy, land = chain_copy(u, order, place, up)
                    if step > 1:
                        copy.wait_recv()
                        add_into(last_ref(u, order, place), land)
                    copy.start()

    def chain_sends(u):
        for (order, place), z_at in units[started[u]].z_of.items():
            for up, some in ((True, z_at > 0), (False, z_at < 3)):
                if some:

                    @pl.when((z < z_at) if up else (z > z_at))
                    def _():
                        chain_copy(u, order, place, up)[0].wait_send()

    def finish(u):
        unit = units[started[u]]
        for (order, place), z_at in unit.z_of.items():

            @pl.when(z == z_at)
            def _():
                value = last_ref(u, order, place)[...].astype(jnp.float32)
                for up, have in ((True, z_at > 0), (False, z_at < 3)):
                    if have:
                        copy, land = chain_copy(u, order, place, up)
                        copy.wait_recv()
                        value = value + land[...].astype(jnp.float32)
                store_out(unit, order, place, value)

    def store_out(unit, order, place, value):
        out = r["out_" + unit.out]
        if unit.tiles:
            for t in range(unit.tiles):
                col = (unit.out_at + t) * LANES
                width = min(LANES, out.shape[1] - col)
                out[:, col : col + width] = value[t * ROWS : (t + 1) * ROWS, :width]
            return
        base = {"shrink": (2 * order + place) * ROWS, "proj": 0, "skip": place * ROWS}[unit.out]
        for i in range(2):
            out[base : base + ROWS, i * LANES : (i + 1) * LANES] = value[i * ROWS : (i + 1) * ROWS]
        for s in range(3):
            out[base + s * THIRD : base + (s + 1) * THIRD, 256:288] = value[
                2 * ROWS : 2 * ROWS + THIRD, s * 32 : (s + 1) * 32
            ]

    def line_ref(name, order, place):
        return r.line.at[0, order, both, both, place, pl.ds(0, units[name].rows)]

    def line_copy(name, order, place, up):
        i = r.line_at[name, order, place, up]
        dst = r.line_land.at[i, both, both, pl.ds(0, units[name].rows)]
        key = (name, "line", order, place, up)
        return remote(key, line_ref(name, order, place), dst, "above" if up else "below"), dst

    def line_hop(name, step, turn):
        for up, me in ((True, step - 1), (False, 4 - step)):
            todo = [
                key
                for key, z_at in sorted(
                    units[name].z_of.items(), key=lambda item: -item[1] if up else item[1]
                )
                if ((z_at > me) if up else (z_at < me))
            ][turn : turn + 1]

            @pl.when(z == me)
            def _():
                for order, place in todo:
                    copy, land = line_copy(name, order, place, up)
                    if step > 1:
                        copy.wait_recv()
                        add_into(line_ref(name, order, place), land)
                    copy.start()

    def line_credit(act):
        for some, side, here, there in ((z < 3, "above", 8, 9), (z > 0, "below", 9, 8)):

            @pl.when(some)
            def _():
                if act is pl.semaphore_wait:
                    pl.semaphore_wait(r.credit.at[here], 1)
                else:
                    pl.semaphore_signal(
                        r.credit.at[there], 1, device_id=at[side], device_id_type=MESH
                    )

    def line_copies(name):
        i = LINE_FIRST.index(name)
        height = pl.ds(0, units[name].rows)
        own = r.line_own.at[i]
        return (
            remote((name, "line_x"), own.at[1 - x, both, height], r.line_x.at[i, both, height], "x"),
            remote((name, "line_y"), own.at[x, 1 - y, height], r.line_y.at[i, height], "y"),
        )

    def line_stage(name, stage):
        i = LINE_FIRST.index(name)
        unit = units[name]
        height = pl.ds(0, unit.rows)
        if stage == "end":
            for (order, place), z_at in unit.z_of.items():

                @pl.when(z == z_at)
                def _():
                    lands = []
                    for up, have in ((True, z_at > 0), (False, z_at < 3)):
                        if have:
                            copy, land = line_copy(name, order, place, up)
                            copy.wait_recv()
                            lands.append(land)
                    for x_at in range(2):
                        for y_at in range(2):
                            value = line_ref(name, order, place)[x_at, y_at].astype(jnp.float32)
                            for land in lands:
                                value = value + land[x_at, y_at].astype(jnp.float32)
                            r.line_own[i, x_at, y_at, height] = value.astype(low)

            line_copies(name)[0].start()
            if i + 1 < len(LINE_FIRST):
                line_credit(pl.semaphore_signal)
        elif stage == "x":
            line_copies(name)[0].wait_recv()
            add_into(r.line_own.at[i, x, both, height], r.line_x.at[i, both, height])
            line_copies(name)[1].start()
        else:
            line_copies(name)[1].wait_recv()
            value = r.line_own[i, x, y, height].astype(jnp.float32)
            value = value + r.line_y[i, height].astype(jnp.float32)
            store_out(unit, 0, 0, value)

    def line_drain(name):
        for (order, place), z_at in units[name].z_of.items():
            for up, some in ((True, z_at > 0), (False, z_at < 3)):
                if some:

                    @pl.when((z < z_at) if up else (z > z_at))
                    def _():
                        line_copy(name, order, place, up)[0].wait_send()

    def head_load(h):
        return pltpu.make_async_copy(
            r.wins.at[:, h], r.head.at[h % 2], r.head_sem.at[h % 2]
        )

    done = {"heads": 0}

    def halo_work():
        head_load(0).start()
        own = pltpu.make_async_copy(r.grads, window.at[pl.ds(rows, rows)], r.chunk_sem.at[0])
        own.start()
        pad = rows - rim
        blank = jnp.zeros((pad, window.shape[1]), low)
        window[0:pad] = blank
        window[3 * rows - pad :] = blank

        @pl.when(seq == 0)
        def _():
            window[pad:rows] = jnp.zeros((rim, window.shape[1]), low)

        @pl.when(seq == 7)
        def _():
            window[2 * rows : 2 * rows + rim] = jnp.zeros((rim, window.shape[1]), low)

        back_masks(r.id_col, r.id_row, r.own_hide, r.rim_hide, rows)
        r.probs[...] = jnp.zeros(r.probs.shape, low)
        r.scored[...] = jnp.zeros(r.scored.shape, low)
        own.wait()
        pl.when(seq > 0)(halo_up.wait_recv)
        pl.when(seq < 7)(halo_down.wait_recv)
        r.stats[...] = window[:, features:]

    def heads_work(count):
        first = done["heads"]
        done["heads"] += count

        def body(h, carry):
            head_load(h).wait()

            @pl.when(h + 1 < HEADS)
            def _():
                head_load(h + 1).start()

            tile = (h * HEAD_DIM) // LANES
            off = h * HEAD_DIM - tile * LANES
            cols = pl.ds(pl.multiple_of(tile * LANES, LANES), 2 * LANES)
            pair = pltpu.roll(window[:, cols], (2 * LANES - off) % (2 * LANES), 1)[:, :LANES]
            r.grad_head[...] = jnp.where(
                lanes_of((3 * rows, LANES)) < HEAD_DIM, pair, jnp.zeros_like(pair)
            )
            head = r.head.at[h % 2]
            found = back_head(
                h, head.at[0], head.at[1], head.at[2], r.grad_head, r.stats[...],
                r.own_hide, r.rim_hide, r.probs, r.scored,
            )
            wide = lanes_of((rows, 2 * LANES))
            inside = (wide >= off) & (wide < off + HEAD_DIM)
            for part, value in enumerate(found):
                moved = pltpu.roll(jnp.concatenate([value, jnp.zeros_like(value)], axis=1), off, 1)
                r.triple[part, :, cols] = jnp.where(inside, moved, r.triple[part, :, cols])
            return carry

        lax.fori_loop(first, first + count, body, 0)

    sums = r.sums

    def pack_work():
        for p in range(3):
            if p != 1:
                row = 3 + p // 2
                sums[row : row + 1] = column_sum(r.triple[p, :, :features].astype(jnp.float32))
        for b in range(4):
            pieces = []
            for p in range(3):
                low_at, high_at = max(864 * b, features * p), min(864 * (b + 1), features * (p + 1))
                if low_at < high_at:
                    pieces.append(
                        r.triple[p, :, low_at - features * p : high_at - features * p]
                    )
            pieces.append(jnp.zeros((rows, 32), low))
            value = jnp.concatenate(pieces, axis=1)
            for j, (first, tiles) in enumerate(TRIPLE_TILES):
                width = tiles * LANES
                r[f"triple{j}"][b % 2, 0, :, width * (b // 2) : width * (b // 2 + 1)] = value[
                    :, first * LANES : first * LANES + width
                ]
        for j in range(len(TRIPLE_TILES)):
            swap("right", f"triple{j}", 0)

    chunks = [(p, first, count) for p in range(3) for first, count in ((0, 768), (768, 384))]

    def weight_load(i):
        slot = i % 2
        if i < 6:
            p, first, count = chunks[i]
            src = r.attn_weight.at[pl.ds(first, count), pl.ds(features * p, features)]
        else:
            count = 768
            src = r.skip_weight.at[pl.ds(768 * (i - 6), 768)]
        return pltpu.make_async_copy(
            src, r.lefts.at[slot, pl.ds(0, count)], r.weight_sem.at[slot]
        )

    def back_work(p):
        if p == 0:
            weight_load(0).start()
        for i in (2 * p, 2 * p + 1):
            _, first, count = chunks[i]
            weight_load(i).wait()
            if i < 5:
                weight_load(i + 1).start()
            part = dot_nt(r.triple[p, :, :features], r.lefts[i % 2, :count])
            cols = slice(first, first + count)
            if p == 0:
                r.normed_grad[:, cols] = part
            else:
                r.normed_grad[:, cols] += part

    def norm_work():
        gain = vector(r.gain)
        sums[0:3] = jnp.zeros((3, features), jnp.float32)
        chunk = r.chunk
        for i in range(rows // LANES):
            here = pl.ds(i * LANES, LANES)
            copies = [
                pltpu.make_async_copy(r[name].at[here], chunk.at[k], r.chunk_sem.at[k])
                for k, name in enumerate(("stream", "middle_grad"))
            ]
            for copy in copies:
                copy.start()
            for copy in copies:
                copy.wait()
            unit, scale = row_norm(chunk[0])
            cotangent = r.normed_grad[here]
            rounded = (chunk[1] + norm_back(unit, scale, gain, cotangent)).astype(low)
            window[here, :features] = rounded
            sums[0:1] += column_sum(rounded.astype(jnp.float32))
            sums[1:2] += column_sum(cotangent * unit)
            sums[2:3] += column_sum(cotangent)
        by_core_store(r.stream_cols, window[0:rows, :features])
        swap("right", "stream_cols", 0)

    def out_copies():
        return [
            pltpu.make_async_copy(
                r.triple.at[k, :, pl.ds(0, features)], r[name], r.chunk_sem.at[k]
            )
            for k, name in enumerate(("out_tok", "out_skp"))
        ]

    def out_work(k):
        i = 6 + k
        if k == 0:
            weight_load(i).start()
        weight_load(i).wait()
        if k < 2:
            weight_load(i + 1).start()
        value = dot_nt(window[0:rows, :features], r.lefts[i % 2, :768]).astype(low)
        for half in range(2):
            base = features * half
            first, last = max(768 * k, base), min(768 * (k + 1), base + features)
            if first < last:
                r.triple[half, :, first - base : last - base] = value[
                    :, first - 768 * k : last - 768 * k
                ]
        if k == 2:
            for copy in out_copies():
                copy.start()

    sides = ("core", "x", "y", "pair", "far")

    def vec_work(step):
        vec, land = r.vec, r.vec_land
        if step == 0:
            vec[0] = r.vec_in[...]
            vec[0, 0:5] = sums[0:5]
        else:
            remote(("vec", step - 1), vec.at[step - 1], land.at[step - 1], sides[step - 1]).wait_recv()
            total = vec[step - 1] + land[step - 1]
            if step == len(sides):
                r.out_vec[...] = total
            else:
                vec[step] = total
        if step < len(sides):
            remote(("vec", step), vec.at[step], land.at[step], sides[step]).start()

    def start(name):
        i = order.index(name)
        fetch(name, order[i + 1] if i + 1 < len(order) else None)
        if name in LINE_FIRST:
            i = LINE_FIRST.index(name)
            if i > 0:
                line_drain(LINE_FIRST[i - 1])
                line_credit(pl.semaphore_wait)
            compute(name, r.line, 0)
        else:
            first_stage(started.index(name))

    def third(name):
        third_stage(started.index(name))
        hop(started.index(name), 1)

    steps = {
        START: start,
        TURN: lambda name: second_stage(started.index(name)),
        SETTLE: third,
        HOP: lambda name, step: hop(started.index(name), step),
        FINISH: lambda name: finish(started.index(name)),
        LINE: line_hop,
        LINE_END: lambda name: line_stage(name, "end"),
        LINE_X: lambda name: line_stage(name, "x"),
        LINE_Y: lambda name: line_stage(name, "y"),
        HALO: halo_work,
        HEAD: heads_work,
        PACK: pack_work,
        BACK: back_work,
        NORM: norm_work,
        OUT: out_work,
        VECTOR: vec_work,
    }
    for kind, *rest in PLAN:
        steps[kind](*rest)
    for copy in out_copies():
        copy.wait()
    for name in LINE_FIRST[-1:]:
        line_drain(name)
    for name in LINE_FIRST:
        for copy in line_copies(name):
            copy.wait_send()
    for copy in swaps.values():
        copy.wait_send()
    count = len(started)
    for u in range(max(0, count - PART_SLOTS), count):
        wait_sends(u)
    for u in range(max(0, count - LAST_SLOTS), count):
        chain_sends(u)
    for step in range(len(sides)):
        remote(("vec", step), r.vec.at[step], r.vec_land.at[step], sides[step]).wait_send()
    pl.when(seq < 7)(halo_up.wait_send)
    pl.when(seq > 0)(halo_down.wait_send)


def gradients(values, vec):
    low, full = jnp.bfloat16, jnp.float32
    rows, features = values["tok"].shape
    names, operands, in_specs, out_shape, out_specs, scratch = [], [], [], [], [], []
    held = ("id_col", "id_row", "gain")
    for name, value in values.items():
        names.append(name)
        operands.append(value)
        in_specs.append(whole() if name in held else anywhere())
    names.append("vec_in")
    operands.append(vec)
    in_specs.append(whole())

    def out(name, shape, dtype, spec):
        names.append(name)
        out_shape.append(jax.ShapeDtypeStruct(shape, dtype))
        out_specs.append(spec)

    for name, shape in GRADS:
        out("out_" + name, shape, full, whole())
    out("out_vec", vec.shape, full, whole())
    out("out_tok", (rows, features), low, anywhere())
    out("out_skp", (rows, features), low, anywhere())
    for name in ("active", "second", "mixed", "normed", "tok", "skp"):
        out("far_" + name, values[name].shape, low, anywhere())
    for name in ("upstream", "hidden", "branch"):
        out("far_" + name, values[name].shape[1:], low, anywhere())
    cores = {f"triple{j}": 2 * LANES * tiles for j, (_, tiles) in enumerate(TRIPLE_TILES)}
    cores["stream_cols"] = 768
    for name, width in cores.items():
        out("far_" + name, (1, rows, width), low, anywhere())

    def add(**kinds):
        names.extend(kinds.keys())
        scratch.extend(kinds.values())

    most = 3 * ROWS
    for name, width in cores.items():
        add(**{name: pltpu.VMEM((2, 1, rows, width), low)})
    add(lefts=pltpu.VMEM((2, 2 * rows, features), low))
    add(rights=pltpu.VMEM((2, 2 * rows, 768), low))
    add(left_sem=pltpu.SemaphoreType.DMA((2, 2)))
    add(right_sem=pltpu.SemaphoreType.DMA((2, 2)))
    add(part=pltpu.VMEM((PART_SLOTS, 2, 2, 2, 2, most, LANES), low))
    add(land_one=pltpu.VMEM((FIRST_SLOTS, 2, 2, 2, most, LANES), low))
    add(land_two=pltpu.VMEM((SECOND_SLOTS, 2, 2, most, LANES), low))
    add(ends=pltpu.VMEM((LAST_SLOTS, 2, 2, most, LANES), low))
    chain_at, sizes = {}, {"chain_short": 0, "chain_long": 0}
    for name, unit in make_units().items():
        if name in LINE_FIRST:
            continue
        pool = "chain_short" if unit.rows <= 2 * ROWS + THIRD else "chain_long"
        for (order, place), z_at in unit.z_of.items():
            for up, have in ((True, z_at > 0), (False, z_at < 3)):
                if have:
                    chain_at[name, order, place, up] = (pool, sizes[pool])
                    sizes[pool] += 1
    add(chain_short=pltpu.VMEM((sizes["chain_short"], 2 * ROWS + THIRD, LANES), low))
    add(chain_long=pltpu.VMEM((sizes["chain_long"], most, LANES), low))
    add(sent=pltpu.SemaphoreType.DMA((256,)))
    add(came=pltpu.SemaphoreType.DMA((256,)))
    span = 3 * rows
    add(window=pltpu.VMEM((span, features + LANES), low))
    add(stats=pltpu.VMEM((span, LANES), low))
    add(head=pltpu.VMEM((2, 3, span, LANES), low))
    add(head_sem=pltpu.SemaphoreType.DMA((2,)))
    add(grad_head=pltpu.VMEM((span, LANES), low))
    add(own_hide=pltpu.VMEM((rows // LANES, LANES, span - rows + LANES), low))
    add(rim_hide=pltpu.VMEM((2 * rows // LANES, LANES, rows), low))
    add(probs=pltpu.VMEM((span, rows), low))
    add(scored=pltpu.VMEM((span, rows), low))
    add(triple=pltpu.VMEM((3, rows, features + LANES), low))
    add(weight_sem=pltpu.SemaphoreType.DMA((2,)))
    add(normed_grad=pltpu.VMEM((rows, features), full))
    add(chunk=pltpu.VMEM((2, LANES, features), full))
    add(chunk_sem=pltpu.SemaphoreType.DMA((2,)))
    add(credit=pltpu.SemaphoreType.REGULAR((10,)))
    lines = len(LINE_FIRST)
    line_at = {}
    for name in LINE_FIRST:
        for (order, place), z_at in make_units()[name].z_of.items():
            for up, have in ((True, z_at > 0), (False, z_at < 3)):
                if have:
                    line_at[name, order, place, up] = len(
                        [key for key in line_at if key[0] == name]
                    )
    add(line=pltpu.VMEM((1, 2, 2, 2, 2, most, LANES), low))
    add(line_land=pltpu.VMEM((6, 2, 2, most, LANES), low))
    add(line_own=pltpu.VMEM((lines, 2, 2, most, LANES), low))
    add(line_x=pltpu.VMEM((lines, 2, most, LANES), low))
    add(line_y=pltpu.VMEM((lines, most, LANES), low))
    add(sums=pltpu.VMEM((8, features), full))
    add(vec=pltpu.VMEM((5, *vec.shape), full))
    add(vec_land=pltpu.VMEM((5, *vec.shape), full))

    def kernel(*refs):
        gradient_kernel(Refs(zip(names, refs), chain_at=chain_at, line_at=line_at))

    found = pl.pallas_call(
        kernel,
        out_shape=out_shape,
        in_specs=in_specs,
        out_specs=out_specs,
        scratch_shapes=scratch,
        compiler_params=pltpu.CompilerParams(
            collective_id=0, has_side_effects=True, vmem_limit_bytes=VMEM_MOST
        ),
        name="gradients",
    )(*operands)
    return dict(zip([name for name, _ in GRADS] + ["vec", "tok", "skp"], found))


VECTORS = ((0, 1), (1, 1), (2, 1), (3, 2), (5, 1), (6, 1), (7, 1), (9, 4), (8, 1))


def results_kernel(*refs):
    count = len(GRADS) + 2
    total, sources, targets = refs[0], refs[1 : 1 + count], refs[1 + count :]
    for source, target in zip(sources, targets):
        target[...] = source[...].T if source.shape != target.shape else source[...]
    features = total.shape[1]
    place = lax.axis_index(SEQ) * lax.axis_size(BATCH) + lax.axis_index(BATCH)
    for (first, rows), target in zip(VECTORS, targets[count:]):
        width = target.shape[0]
        row = place * width // features
        off = place * width - row * features
        line = jnp.broadcast_to(total[pl.ds(first + row, 1)], (8, features))
        target[...] = pltpu.roll(line, (features - off) % features, 1)[0, :width]


def results(found):
    values = [found[name] for name in [*(name for name, _ in GRADS), "tok", "skp"]]
    devices = lax.axis_size(SEQ) * lax.axis_size(BATCH)
    features = found["vec"].shape[1]
    shapes = [values[0].shape[::-1], *(value.shape for value in values[1:])]
    out = [jax.ShapeDtypeStruct(shape, value.dtype) for shape, value in zip(shapes, values)]
    out += [
        jax.ShapeDtypeStruct((rows * features // devices,), jnp.float32) for _, rows in VECTORS
    ]
    got = pl.pallas_call(
        results_kernel,
        out_shape=out,
        in_specs=[whole()] * (1 + len(values)),
        out_specs=[whole()] * len(out),
        compiler_params=params(),
        name="results",
    )(found["vec"], *values)
    return (got[0].T, *got[1 : len(values)]), got[len(values) :]


def unsplit(value):
    blocks = []
    for b in range(4):
        x, c = b // 2, b % 2
        blocks.append(value[c, 0, :, 256 * x : 256 * x + 256])
        blocks.append(value[c, 0, :, 512 + LANES * x : 544 + LANES * x])
    return jnp.concatenate(blocks, axis=1)


def outer_sum(left, right):
    return dot_tn(left, right)


def summed(lefts, rights, vector_list):
    hidden = rights["hidden"]
    _, pieces, rows, width = hidden.shape
    hidden = hidden.reshape(2, pieces, rows, 2, width // 2).transpose(2, 3, 0, 1, 4)
    columns_of = dict(
        joined=unsplit(rights["stream"]),
        normed=rights["triple"],
        mixed=unsplit(rights["branch"]),
        second=hidden.reshape(rows, -1),
        active=unsplit(rights["upstream"]),
    )
    parts = []
    for name in ("joined", "normed", "mixed", "second", "active"):
        gathered = lax.all_gather(lefts[name], BATCH, axis=0, tiled=True)
        columns = lax.all_to_all(
            columns_of[name], BATCH, split_axis=1, concat_axis=0, tiled=True
        )
        parts.append(outer_sum(gathered, columns).astype(jnp.bfloat16))
    parts = lax.psum_scatter(tuple(parts), SEQ, scatter_dimension=0, tiled=True)
    vectors = tuple(
        lax.psum_scatter(vector, (SEQ, BATCH), scatter_dimension=0, tiled=True)
        for vector in vector_list
    )
    return tuple(part.astype(jnp.float32) for part in parts), vectors


def rims(value, width):
    size = lax.axis_size(SEQ)
    up = [(i, i + 1) for i in range(size - 1)]
    down = [(j, i) for i, j in up]
    return (
        lax.ppermute(value[-width:], SEQ, up),
        lax.ppermute(value[:width], SEQ, down),
    )


def on_device(
    tokens,
    skip_tokens,
    segment_ids,
    upstream,
    skip_weight,
    skip_bias,
    first_gain,
    first_shift,
    attn_weight,
    attn_bias,
    proj_weight,
    proj_bias,
    second_gain,
    second_shift,
    expand_weight,
    expand_bias,
    shrink_weight,
    shrink_bias,
):
    _, rows, features = tokens.shape
    rim = (ITEM_MOST - 1 + 15) // 16 * 16
    tok, skp, above = tokens[0], skip_tokens[0], upstream[0]
    position = lax.axis_index(SEQ)
    padded_ids = jnp.pad(segment_ids[0], (rows, rows), constant_values=-1)
    window_ids = lax.dynamic_slice_in_dim(padded_ids, position * rows, 3 * rows, 0)
    id_row, id_col = window_ids[None, :], window_ids[:, None]

    stream, normed, wins, mixed, lse, active_grad = forward(
        tok, skp, skip_weight, skip_bias, first_gain, first_shift, attn_weight, attn_bias, id_col,
        id_row, above, shrink_weight,
    )
    (
        result, active, hidden_by_core, second, branch, branch_by_core, up_by_core, middle_grad,
        mixed_grad, sums,
    ) = layer(
        stream, mixed, lse, above, active_grad,
        (
            proj_weight, proj_bias, second_gain, second_shift, expand_weight, expand_bias,
            shrink_weight, shrink_bias,
        ),
    )
    if lax.axis_size(SEQ) == 8 and lax.axis_size(BATCH) == 4:
        found = gradients(
            dict(
                active=active, second=second, mixed=mixed, normed=normed, tok=tok, skp=skp,
                upstream=up_by_core, hidden=hidden_by_core, branch=branch_by_core, wins=wins,
                grads=mixed_grad, id_col=id_col, id_row=id_row, stream=stream,
                middle_grad=middle_grad, gain=first_gain, attn_weight=attn_weight,
                skip_weight=skip_weight,
            ),
            sums,
        )
        (shrink, expand, proj, attn, skip, tok_grad, skip_grad), vectors = results(found)
        weight_parts = (skip, attn, proj, expand, shrink)
    else:
        before, after = rims(mixed_grad, rim)
        blank = jnp.zeros((rows - rim, mixed_grad.shape[1]), mixed_grad.dtype)
        grad_window = jnp.concatenate([blank, before, mixed_grad, after, blank], axis=0)
        stats = grad_window[:, features:]
        triple, triple_sum = attend_back(wins, grad_window, stats, id_col, id_row)
        tok_grad, skip_grad, stream_by_core, stream_sums = stream_back(
            triple, attn_weight, stream, middle_grad, first_gain, skip_weight
        )
        vector_list = (
            stream_sums[2],
            stream_sums[0],
            stream_sums[1],
            jnp.concatenate([triple_sum[0, :features], triple_sum[0, 2 * features :]]),
            sums[5],
            sums[6],
            sums[7],
            sums[9:13].reshape(-1),
            sums[8],
        )
        joined = jnp.concatenate([tok, skp], axis=1)
        weight_parts, vectors = summed(
            dict(active=active, second=second, mixed=mixed, normed=normed, joined=joined),
            dict(
                upstream=up_by_core,
                hidden=hidden_by_core,
                branch=branch_by_core,
                triple=triple,
                stream=stream_by_core,
            ),
            vector_list,
        )
    return (
        result[None],
        tok_grad[None],
        skip_grad[None],
        weight_parts[0],
        vectors[0],
        vectors[1],
        vectors[2],
        weight_parts[1],
        vectors[3],
        weight_parts[2],
        vectors[4],
        vectors[5],
        vectors[6],
        weight_parts[3],
        vectors[7],
        weight_parts[4],
        vectors[8],
    )


def solution(mesh):
    in_specs = (
        P(BATCH, SEQ, None),
        P(BATCH, SEQ, None),
        P(BATCH, None),
        P(BATCH, SEQ, None),
        P(),
        P(),
        P(),
        P(),
        P(),
        P(),
        P(),
        P(),
        P(),
        P(),
        P(),
        P(),
        P(),
        P(),
    )
    out_specs = (
        P(BATCH, SEQ, None),
        P(BATCH, SEQ, None),
        P(BATCH, SEQ, None),
        P(SEQ, BATCH),
        P((SEQ, BATCH)),
        P((SEQ, BATCH)),
        P((SEQ, BATCH)),
        P(SEQ, BATCH),
        P((SEQ, BATCH)),
        P(SEQ, BATCH),
        P((SEQ, BATCH)),
        P((SEQ, BATCH)),
        P((SEQ, BATCH)),
        P(SEQ, BATCH),
        P((SEQ, BATCH)),
        P(SEQ, BATCH),
        P((SEQ, BATCH)),
    )
    return jax.shard_map(
        on_device, mesh=mesh, in_specs=in_specs, out_specs=out_specs, check_vma=False
    )
```

```python
import jax
import jax.numpy as jnp
from jax import lax
from jax.experimental import pallas as pl
from jax.experimental.pallas import tpu as pltpu
from jax.sharding import PartitionSpec as P

SEQ, BATCH = "seq", "batch"
HEADS = 16
HEAD_DIM = 72
ITEM_MOST = 322
LANES = 128
MESH = pl.DeviceIdType.MESH
SCALE2 = HEAD_DIM**-0.5 * 1.4426950408889634
VMEM_MOST = 60 * 2**20


ROOT2 = 2.0**0.5


def dot(left, right):
    return jnp.dot(left, right, preferred_element_type=jnp.float32)


def dot_nt(left, right):
    return lax.dot_general(
        left, right, (((1,), (1,)), ((), ())), preferred_element_type=jnp.float32
    )


def dot_tn(left, right):
    return lax.dot_general(
        left, right, (((0,), (0,)), ((), ())), preferred_element_type=jnp.float32
    )


def vector(ref, first=0, count=None):
    count = ref.shape[0] if count is None else count
    return ref[pl.ds(first, count)].astype(jnp.float32).reshape(1, count)


def whole():
    return pl.BlockSpec(memory_space=pltpu.VMEM)


def anywhere():
    return pl.BlockSpec(memory_space=pl.ANY)


def params():
    return pltpu.CompilerParams(vmem_limit_bytes=60 * 2**20)


def erf(value):
    v = jnp.clip(value, -3.832506856900711, 3.832506856900711)
    s = v * v
    top = 0.00022905065861350646
    for a in (0.0034082910107109506, 0.050955695062380861, 0.18520832239976145, 1.128379143519084):
        top = top * s + a
    low = -1.1791602954361697e-7
    for a in (0.000023547966471313185, 0.0010179625278914885, 0.014070470171167667):
        low = low * s + a
    low = (low * s + 0.11098505178285362) * s + 0.49746925110067538
    return v * top / (low * s + 1.0)


def row_norm(value):
    centred = value - jnp.mean(value, axis=-1, keepdims=True)
    scale = lax.rsqrt(jnp.mean(centred * centred, axis=-1, keepdims=True) + 1e-05)
    return centred * scale, scale


def norm_back(unit, scale, gain, cotangent):
    inner = cotangent * gain
    mean = jnp.mean(inner, axis=-1, keepdims=True)
    along = jnp.mean(inner * unit, axis=-1, keepdims=True)
    return scale * (inner - mean - unit * along)


def column_sum(value):
    return jnp.sum(value, axis=0, keepdims=True)


MARKS = (HEAD_DIM, HEAD_DIM + 16, HEAD_DIM + 32)


def lanes_of(shape):
    return lax.broadcasted_iota(jnp.int32, shape, len(shape) - 1)


def marked(lane):
    return (lane == MARKS[0]) | (lane == MARKS[1]) | (lane == MARKS[2])


def head_tile(value, h, ones):
    rows = value.shape[0]
    lane = lanes_of((rows, LANES - HEAD_DIM)) + HEAD_DIM
    rest = jnp.where(marked(lane) & ones, 1.0, 0.0).astype(value.dtype)
    return jnp.concatenate([value[:, HEAD_DIM * h : HEAD_DIM * (h + 1)], rest], axis=1)


def project(rows_ref, weight_ref, bias, part, store):
    features = rows_ref.shape[1]
    value = dot(rows_ref[...], weight_ref[...])
    if part != 1:
        at = 0 if part == 0 else features
        value = value + vector(bias, at, features)
    value = value.astype(jnp.bfloat16)
    for h in range(HEADS):
        store(part, h, head_tile(value, h, part > 0))


HIDE = -1e30


def forward_kernel(
    tok, skp, skip_weight, skip_bias, gain, shift, weight, bias, segment_ids, upstream, shrink,
    stream, normed, wins, mixed, lse, active_grad, id_col, id_row, window, halo, held, held_skip, hide, own_part,
    gathered, shrink_tile, grad_tile, sems, out_sems, sent, came, wide_sems,
):
    rows, features = tok.shape
    rim = halo.shape[0] // 2
    span = 3 * rows
    blocks = rows // LANES
    reach = span - (blocks - 1) * LANES
    seq, size, batch = lax.axis_index(SEQ), lax.axis_size(SEQ), lax.axis_index(BATCH)
    after, before = (jnp.minimum(seq + 1, size - 1), batch), (jnp.maximum(seq - 1, 0), batch)
    skip_copies = [
        pltpu.make_async_copy(
            skip_weight.at[:, pl.ds(384 * n, 384)], held_skip.at[n], sems.at[n]
        )
        for n in range(3)
    ]
    copies = [
        pltpu.make_async_copy(
            weight.at[:, pl.ds(features * p, features)], held.at[p], sems.at[3 + p]
        )
        for p in range(3)
    ]
    for copy in skip_copies + copies:
        copy.start()

    barrier = pltpu.get_barrier_semaphore()

    def greet(device):
        pl.semaphore_signal(barrier, 1, device_id=device, device_id_type=MESH)

    pl.when(seq < size - 1)(lambda: greet(after))
    pl.when(seq > 0)(lambda: greet(before))
    pl.semaphore_wait(
        barrier, (seq < size - 1).astype(jnp.int32) + (seq > 0).astype(jnp.int32)
    )

    for n, copy in enumerate(skip_copies):
        copy.wait()
        at = slice(384 * n, 384 * n + 384)
        stream[:, at] = (
            dot(tok[...], held_skip[n, :features])
            + dot(skp[...], held_skip[n, features:])
            + vector(skip_bias, 384 * n, 384)
        )
    unit, _ = row_norm(stream[...])
    normed[...] = (unit * vector(gain) + vector(shift)).astype(jnp.bfloat16)

    near = rim // 48 * 32
    parts = ((0, near), (near, rim - near))

    def send(part, side):
        first, count = parts[part]
        start = (rows - first - count, first)[side]
        return pltpu.make_async_remote_copy(
            src_ref=normed.at[pl.ds(start, count)],
            dst_ref=halo.at[pl.ds(2 * first + side * count, count)],
            send_sem=sent.at[part, side],
            recv_sem=came.at[part, side],
            device_id=(after, before)[side],
            device_id_type=MESH,
        )

    sends = (seq < size - 1, seq > 0)
    for part in range(2):
        for side in range(2):
            pl.when(sends[side])(send(part, side).start)

    pad = rows - rim
    window[:, :, 0:pad] = jnp.zeros((3, HEADS, pad, LANES), jnp.bfloat16)
    window[:, :, span - pad : span] = jnp.zeros((3, HEADS, pad, LANES), jnp.bfloat16)

    def store_own(part, h, value):
        window[part, h, rows : 2 * rows] = value

    for p, copy in enumerate(copies):
        copy.wait()
        project(normed, held.at[p], bias, p, store_own)
    for k in range(3):
        block = seq - 1 + k
        first = jnp.minimum(jnp.maximum(block, 0), size - 1) * rows
        numbers = segment_ids[:, pl.ds(pl.multiple_of(first, LANES), rows)].astype(jnp.float32)
        inside = (block >= 0) & (block < size)
        id_row[:, rows * k : rows * (k + 1)] = jnp.where(inside, numbers, -1.0)
    id_col[...] = jnp.broadcast_to(id_row[...], (8, span)).T[:, :1]
    for i in range(blocks):
        same = id_col[rows + i * LANES : rows + (i + 1) * LANES] == (
            id_row[:, i * LANES : i * LANES + reach]
        )
        hide[i] = jnp.where(same, 0.0, HIDE)
    lane = lanes_of((LANES, LANES))

    def queries(h, i):
        return window[0, h, rows + i * LANES : rows + (i + 1) * LANES]

    def own_body(pair, carry):
        jobs = [(2 * pair + k, i) for k in range(2) for i in range(blocks)]
        scores = [
            dot_nt(queries(h, i), window[1, h, rows : 2 * rows]) * SCALE2
            + hide[i, :, rows - i * LANES : 2 * rows - i * LANES]
            for h, i in jobs
        ]
        highest = [jnp.max(value, axis=-1, keepdims=True) for value in scores]
        raised = [
            jnp.exp2(value - most).astype(jnp.bfloat16) for value, most in zip(scores, highest)
        ]
        totals = [dot(value, window[2, h, rows : 2 * rows]) for value, (h, i) in zip(raised, jobs)]
        for total, most, (h, i) in zip(totals, highest, jobs):
            at = slice(i * LANES, (i + 1) * LANES)
            own_part[h, at] = jnp.where(lane == LANES - 1, most, total)
        return carry

    lax.fori_loop(0, HEADS // 2, own_body, 0)

    wide = shrink.shape[0] // 4
    loads = [
        pltpu.make_async_copy(
            shrink.at[pl.ds(wide * t, wide)], shrink_tile.at[t % 2], wide_sems.at[0, t % 2]
        )
        for t in range(4)
    ]
    stores = [
        pltpu.make_async_copy(
            grad_tile.at[t % 2], active_grad.at[:, pl.ds(wide * t, wide)], wide_sems.at[1, t % 2]
        )
        for t in range(4)
    ]
    loads[0].start()
    for t in range(4):
        if t < 3:
            loads[t + 1].start()
        loads[t].wait()
        if t > 1:
            stores[t - 2].wait()
        grad_tile[t % 2] = dot_nt(upstream[...], shrink_tile[t % 2])
        stores[t].start()

    for part, (first, count) in enumerate(parts):
        here = pl.ds(2 * first, 2 * count)
        for side in range(2):
            pl.when(sends[1 - side])(send(part, side).wait_recv)

            @pl.when(jnp.logical_not(sends[1 - side]))
            def _():
                halo[2 * first + side * count : 2 * first + (side + 1) * count] = jnp.zeros(
                    (count, features), jnp.bfloat16
                )

        def store_rim(p, h, value):
            window[p, h, rows - first - count : rows - first] = value[:count]
            window[p, h, 2 * rows + first : 2 * rows + first + count] = value[count:]

        for p in (1, 2, 0):
            project(halo.at[here], held.at[p], bias, p, store_rim)
    out_copies = [
        pltpu.make_async_copy(window.at[p], wins.at[p], out_sems.at[p]) for p in range(3)
    ]
    for copy in out_copies:
        copy.start()
    lse[...] = jnp.zeros_like(lse)

    def rim_body(pair, carry):
        jobs = [(2 * pair + k, i) for k in range(2) for i in range(blocks)]

        def keys(part, h, i):
            return jnp.concatenate(
                [
                    window[part, h, i * LANES : rows],
                    window[part, h, 2 * rows : 2 * rows + (i + 1) * LANES],
                ],
                axis=0,
            )

        def hidden(i):
            return jnp.concatenate(
                [hide[i, :, : rows - i * LANES], hide[i, :, 2 * rows - i * LANES :]], axis=1
            )

        scores = [dot_nt(queries(h, i), keys(1, h, i)) * SCALE2 + hidden(i) for h, i in jobs]
        owns = [own_part[h, i * LANES : (i + 1) * LANES] for h, i in jobs]
        own_most = [value[:, LANES - 1 :] for value in owns]
        highest = [
            jnp.maximum(jnp.max(value, axis=-1, keepdims=True), most)
            for value, most in zip(scores, own_most)
        ]
        raised = [
            jnp.exp2(value - most).astype(jnp.bfloat16) for value, most in zip(scores, highest)
        ]
        totals = [dot(value, keys(2, h, i)) for value, (h, i) in zip(raised, jobs)]
        for total, own, low, most, (h, i) in zip(totals, owns, own_most, highest, jobs):
            at = slice(i * LANES, (i + 1) * LANES)
            total = total + own * jnp.exp2(low - most)
            denominator = total[:, HEAD_DIM : HEAD_DIM + 1]
            gathered[h, at] = (total / denominator).astype(jnp.bfloat16)
            lse[at] = jnp.where(lane == h, most + jnp.log2(denominator), lse[at])
        return carry

    lax.fori_loop(0, HEADS // 2, rim_body, 0)
    for h in range(HEADS):
        mixed[:, HEAD_DIM * h : HEAD_DIM * (h + 1)] = gathered[h, :, :HEAD_DIM]
    for copy in out_copies + stores[2:]:
        copy.wait()
    for part in range(2):
        for side in range(2):
            pl.when(sends[side])(send(part, side).wait_send)


def forward(
    tok, skp, skip_weight, skip_bias, gain, shift, weight, bias, segment_ids, upstream, shrink
):
    rows, features = tok.shape
    span = 3 * rows
    rim = (ITEM_MOST - 1 + 15) // 16 * 16
    low, full = jnp.bfloat16, jnp.float32
    return pl.pallas_call(
        forward_kernel,
        out_shape=(
            jax.ShapeDtypeStruct((rows, features), full),
            jax.ShapeDtypeStruct((rows, features), low),
            jax.ShapeDtypeStruct((3, HEADS, span, LANES), low),
            jax.ShapeDtypeStruct((rows, features), low),
            jax.ShapeDtypeStruct((rows, LANES), full),
            jax.ShapeDtypeStruct((rows, shrink.shape[0]), full),
            jax.ShapeDtypeStruct((span, 1), full),
            jax.ShapeDtypeStruct((1, span), full),
        ),
        in_specs=[
            whole(), whole(), anywhere(), whole(), whole(), whole(), anywhere(), whole(), whole(),
            whole(), anywhere(),
        ],
        out_specs=(
            whole(), whole(), anywhere(), whole(), whole(), anywhere(), whole(), whole(),
        ),
        scratch_shapes=[
            pltpu.VMEM((3, HEADS, span, LANES), low),
            pltpu.VMEM((2 * rim, features), low),
            pltpu.VMEM((3, features, features), low),
            pltpu.VMEM((3, 2 * features, 384), low),
            pltpu.VMEM((rows // LANES, LANES, span - rows + LANES), full),
            pltpu.VMEM((HEADS, rows, LANES), full),
            pltpu.VMEM((HEADS, rows, LANES), low),
            pltpu.VMEM((2, shrink.shape[0] // 4, features), low),
            pltpu.VMEM((2, rows, shrink.shape[0] // 4), full),
            pltpu.SemaphoreType.DMA((6,)),
            pltpu.SemaphoreType.DMA((3,)),
            pltpu.SemaphoreType.DMA((2, 2)),
            pltpu.SemaphoreType.DMA((2, 2)),
            pltpu.SemaphoreType.DMA((2, 2)),
        ],
        compiler_params=pltpu.CompilerParams(
            collective_id=1, has_side_effects=True, vmem_limit_bytes=VMEM_MOST
        ),
        name="forward",
    )(
        tok, skp, skip_weight, skip_bias, gain, shift, weight, bias, segment_ids, upstream, shrink,
    )


def by_core_store(ref, value):
    blank = jnp.zeros((value.shape[0], 32), value.dtype)
    for b in range(4):
        x, c = b // 2, b % 2
        ref[c, 0, :, 256 * x : 256 * x + 256] = value[:, 288 * b : 288 * b + 256]
        rest = value[:, 288 * b + 256 : 288 * b + 288]
        ref[c, 0, :, 512 + LANES * x : 640 + LANES * x] = jnp.concatenate(
            [rest, rest, rest, blank], axis=1
        )


def split3(value):
    first = value.astype(jnp.bfloat16)
    rest = value - first.astype(jnp.float32)
    second = rest.astype(jnp.bfloat16)
    return first, second, (rest - second.astype(jnp.float32)).astype(jnp.bfloat16)


def layer_kernel(
    stream, mixed, lse, upstream, active_grad, proj, proj_bias, gain, shift, expand, expand_bias,
    shrink, shrink_bias, result, active, hidden_by_core, second, branch, branch_by_core, up_by_core,
    middle_grad, mixed_grad, sums, middle, total, second_grad,
    bias_rows,
):
    step, steps = pl.program_id(0), pl.num_programs(0)
    low = jnp.bfloat16
    wide = expand.shape[1]

    @pl.when(step == 0)
    def _():
        middle[...] = (
            stream[...] + dot(mixed[...], proj[...]) + vector(proj_bias)
        )
        unit, _ = row_norm(middle[...])
        second[...] = (unit * vector(gain) + vector(shift)).astype(low)
        total[...] = middle[...] + vector(shrink_bias)
        second_grad[...] = jnp.zeros_like(second_grad)
        for t in range(4):
            bias_rows[t : t + 1] = vector(expand_bias, wide * t, wide)
        by_core_store(up_by_core, upstream[...])

    hidden = dot(second[...], expand[...]) + bias_rows[pl.ds(step, 1)]
    cdf = 0.5 + 0.5 * erf(hidden * (1.0 / ROOT2))
    density = jnp.exp(-0.5 * hidden * hidden) * 0.3989422804014327
    raised = (hidden * cdf).astype(low)
    active[...] = raised
    hidden_grad = (active_grad[...] * (cdf + hidden * density)).astype(low)
    for j in range(3):
        hidden_by_core[0, j] = hidden_grad[:, 384 * j : 384 * (j + 1)]
    sums[pl.ds(9 + step, 1)] = dot(jnp.ones((16, hidden_grad.shape[0]), low), hidden_grad)[0:1]
    total[...] += dot(raised, shrink[...])
    second_grad[...] += dot_nt(hidden_grad, expand[...])

    @pl.when(step == steps - 1)
    def _():
        result[...] = total[...].astype(low)
        unit, scale = row_norm(middle[...])
        cotangent = second_grad[...]
        above = upstream[...].astype(jnp.float32)
        grad = above + norm_back(unit, scale, vector(gain), cotangent)
        middle_grad[...] = grad
        branched = grad.astype(low)
        branch[...] = branched
        by_core_store(branch_by_core, branched)
        sums[0:5] = jnp.zeros((5, sums.shape[1]), jnp.float32)
        ones = jnp.ones((16, branched.shape[0]), low)
        sums[5:6] = dot(ones, branched)[0:1]
        sums[6:7] = column_sum(cotangent * unit)
        sums[7:8] = column_sum(cotangent)
        sums[8:9] = dot(ones, upstream[...])[0:1]
        sums[13:16] = jnp.zeros((3, sums.shape[1]), jnp.float32)
        back = dot_nt(branched, proj[...]).astype(low)
        features = back.shape[1]
        mixed_grad[:, :features] = back
        products = back.astype(jnp.float32) * mixed[...].astype(jnp.float32)
        shape = (features, LANES)
        member = lax.broadcasted_iota(jnp.int32, shape, 0) // HEAD_DIM == lanes_of(shape)
        member = jnp.where(member, 1.0, 0.0).astype(low)
        high = products.astype(low)
        inner = dot(high, member) + dot((products - high.astype(jnp.float32)).astype(low), member)
        pieces = [part[:, :HEADS] for part in split3(lse[...] * (-1.0 / SCALE2)) + split3(-inner)]
        blank = jnp.zeros((back.shape[0], LANES - 6 * HEADS), low)
        mixed_grad[:, features:] = jnp.concatenate(pieces + [blank], axis=1)


def layer(stream, mixed, lse, upstream, active_grad, weights):
    proj, proj_bias, gain, shift, expand, expand_bias, shrink, shrink_bias = weights
    rows, features = stream.shape
    hidden = expand.shape[1]
    wide = hidden // 4
    low = jnp.bfloat16

    def held(shape):
        return pl.BlockSpec(shape, lambda t: (0,) * len(shape))

    narrow = (rows, features)
    split = (2, 1, rows, 768)
    return pl.pallas_call(
        layer_kernel,
        grid=(4,),
        in_specs=[
            held(narrow), held(narrow), held((rows, LANES)), held(narrow),
            pl.BlockSpec((rows, wide), lambda t: (0, t)),
            held((features, features)), whole(), whole(), whole(),
            pl.BlockSpec((features, wide), lambda t: (0, t)),
            whole(),
            pl.BlockSpec((wide, features), lambda t: (t, 0)),
            whole(),
        ],
        out_specs=(
            held(narrow),
            pl.BlockSpec((rows, wide), lambda t: (0, t)),
            pl.BlockSpec((1, 3, rows, 384), lambda t: (t % 2, 0, 0, t // 2)),
            held(narrow), held(narrow), held(split), held(split), held(narrow),
            held((rows, features + LANES)),
            held((16, features)),
        ),
        out_shape=(
            jax.ShapeDtypeStruct(narrow, low),
            jax.ShapeDtypeStruct((rows, hidden), low),
            jax.ShapeDtypeStruct((2, 3, rows, 768), low),
            jax.ShapeDtypeStruct(narrow, low),
            jax.ShapeDtypeStruct(narrow, low),
            jax.ShapeDtypeStruct(split, low),
            jax.ShapeDtypeStruct(split, low),
            jax.ShapeDtypeStruct(narrow, jnp.float32),
            jax.ShapeDtypeStruct((rows, features + LANES), low),
            jax.ShapeDtypeStruct((16, features), jnp.float32),
        ),
        scratch_shapes=[pltpu.VMEM(narrow, jnp.float32)] * 3
        + [pltpu.VMEM((4, wide), jnp.float32)],
        compiler_params=params(),
        name="layer",
    )(
        stream, mixed, lse, upstream, active_grad, proj, proj_bias, gain, shift, expand,
        expand_bias, shrink, shrink_bias,
    )


def back_masks(id_col, id_row, own_hide, rim_hide, rows):
    blocks = rows // LANES
    reach = own_hide.shape[2]

    def hidden(first, keys, width):
        same = id_col[first : first + LANES] == id_row[:, keys : keys + width]
        return jnp.where(same, 0.0, HIDE).astype(own_hide.dtype)

    for i in range(blocks):
        own_hide[i] = hidden(rows + i * LANES, i * LANES, reach)
    for w in range(blocks):
        rim_hide[w] = hidden(w * LANES, rows, rows)
        rim_hide[blocks + w] = hidden(2 * rows + w * LANES, rows, rows)


def with_stats(value, stats, shift):
    return jnp.where(marked(lanes_of(value.shape)), pltpu.roll(stats, shift, 1), value)


def back_head(h, queries, keys, values, grads, stats, own_hide, rim_hide, probs, scored):
    span = queries.shape[0]
    rows = span // 3
    blocks = rows // LANES
    reach = span - rows + LANES
    low, full = jnp.bfloat16, jnp.float32
    queries[...] = with_stats(queries[...], stats, MARKS[0] - h)
    turn = MARKS[0] - 3 * HEADS - h
    grads[...] = with_stats(grads[...], stats, jnp.where(turn < 0, turn + LANES, turn))
    jobs = []
    for i in range(blocks):
        jobs.append(
            (rows + i * LANES, i * LANES, reach, own_hide[i], rows - i * LANES, rows, 0)
        )
    for w in range(blocks):
        width = (w + 1) * LANES
        jobs.append((w * LANES, rows, width, rim_hide[w][:, :width], 0, width, 0))
        first, width = w * LANES, rows - w * LANES
        hide = rim_hide[blocks + w][:, first:]
        jobs.append((2 * rows + first, rows + first, width, hide, 0, width, first))
    scores = [dot_nt(queries[q : q + LANES], keys[k : k + n]) for q, k, n, *_ in jobs]
    inner = [dot_nt(grads[q : q + LANES], values[k : k + n]) for q, k, n, *_ in jobs]
    weights = [
        jnp.exp2(value * SCALE2 + job[3].astype(full)) for value, job in zip(scores, jobs)
    ]
    scores = [(weight * value).astype(low) for weight, value in zip(weights, inner)]
    weights = [weight.astype(low) for weight in weights]
    for weight, score, (q, _, _, _, first, count, place) in zip(weights, scores, jobs):
        probs[q : q + LANES, place : place + count] = weight[:, first : first + count]
        scored[q : q + LANES, place : place + count] = score[:, first : first + count]
    factor = HEAD_DIM**-0.5
    query_grad = jnp.concatenate(
        [dot(scores[i], keys[i * LANES : i * LANES + reach]) * factor for i in range(blocks)], axis=0
    )
    key_grad = dot_tn(scored[...], queries[...]) * factor
    value_grad = dot_tn(probs[...], grads[...])
    return query_grad.astype(low), key_grad.astype(low), value_grad.astype(low)


def heads_apart(row_ref, out):
    value = row_ref[...]
    for h in range(HEADS):
        out[h] = head_tile(value[:, : HEADS * HEAD_DIM], h, False)


def triple_store(apart, triple):
    features = HEADS * HEAD_DIM
    for p in range(3):
        for h in range(HEADS):
            at = features * p + HEAD_DIM * h
            triple[:, at : at + HEAD_DIM] = apart[p, h, :, :HEAD_DIM]


def attend_back_kernel(
    wins, grads_in, stats, id_col, id_row, triple, sums,
    window, grads, own_hide, rim_hide, probs, scored, apart, sems,
):
    span = window.shape[2]
    rows = span // 3
    copy = pltpu.make_async_copy(wins, window, sems.at[0])
    copy.start()
    back_masks(id_col, id_row, own_hide, rim_hide, rows)
    probs[...] = jnp.zeros_like(probs)
    scored[...] = jnp.zeros_like(scored)
    heads_apart(grads_in, grads)
    copy.wait()

    def body(h, carry):
        found = back_head(
            h, window.at[0, h], window.at[1, h], window.at[2, h], grads.at[h], stats[...],
            own_hide, rim_hide, probs, scored,
        )
        for part, value in enumerate(found):
            apart[part, h] = value
        return carry

    lax.fori_loop(0, HEADS, body, 0)
    triple_store(apart, triple)
    sums[...] = column_sum(triple[...].astype(jnp.float32))


def attend_back(wins, grads_in, stats, id_col, id_row):
    span = wins.shape[2]
    rows = span // 3
    features = HEADS * HEAD_DIM
    low = jnp.bfloat16
    return pl.pallas_call(
        attend_back_kernel,
        out_shape=(
            jax.ShapeDtypeStruct((rows, 3 * features), low),
            jax.ShapeDtypeStruct((1, 3 * features), jnp.float32),
        ),
        in_specs=[anywhere(), whole(), whole(), whole(), whole()],
        out_specs=(whole(), whole()),
        scratch_shapes=[
            pltpu.VMEM((3, HEADS, span, LANES), low),
            pltpu.VMEM((HEADS, span, LANES), low),
            pltpu.VMEM((rows // LANES, LANES, span - rows + LANES), low),
            pltpu.VMEM((2 * rows // LANES, LANES, rows), low),
            pltpu.VMEM((span, rows), low),
            pltpu.VMEM((span, rows), low),
            pltpu.VMEM((3, HEADS, rows, LANES), low),
            pltpu.SemaphoreType.DMA((1,)),
        ],
        compiler_params=params(),
        name="attend_back",
    )(wins, grads_in, stats, id_col, id_row)


def stream_back_kernel(
    triple, weight, stream, middle_grad, gain, skip_weight, tok_grad, skip_grad, by_core, sums, held, held_skip, grad, sems,
):
    features = stream.shape[1]
    low = jnp.bfloat16
    copies = [
        pltpu.make_async_copy(weight.at[:, pl.ds(features * p, features)], held.at[p], sems.at[p])
        for p in range(3)
    ]
    copies += [
        pltpu.make_async_copy(
            skip_weight.at[pl.ds(features * p, features)], held_skip.at[p], sems.at[3 + p]
        )
        for p in range(2)
    ]
    for copy in copies:
        copy.start()
    unit, scale = row_norm(stream[...])
    for p in range(3):
        copies[p].wait()
        part = dot_nt(triple[:, features * p : features * (p + 1)], held[p])
        if p == 0:
            grad[...] = part
        else:
            grad[...] += part
    cotangent = grad[...]
    sums[0:1] = column_sum(cotangent * unit)
    sums[1:2] = column_sum(cotangent)
    whole_grad = middle_grad[...] + norm_back(unit, scale, vector(gain), cotangent)
    rounded = whole_grad.astype(low)
    by_core_store(by_core, rounded)
    sums[2:3] = column_sum(rounded.astype(jnp.float32))
    for p, out in enumerate((tok_grad, skip_grad)):
        copies[3 + p].wait()
        out[...] = dot_nt(rounded, held_skip[p]).astype(low)


def stream_back(triple, weight, stream, middle_grad, gain, skip_weight):
    rows, features = stream.shape
    low = jnp.bfloat16
    return pl.pallas_call(
        stream_back_kernel,
        out_shape=(
            jax.ShapeDtypeStruct((rows, features), low),
            jax.ShapeDtypeStruct((rows, features), low),
            jax.ShapeDtypeStruct((2, 1, rows, 768), low),
            jax.ShapeDtypeStruct((8, features), jnp.float32),
        ),
        in_specs=[whole(), anywhere(), whole(), whole(), whole(), anywhere()],
        out_specs=(whole(), whole(), whole(), whole()),
        scratch_shapes=[
            pltpu.VMEM((3, features, features), low),
            pltpu.VMEM((2, features, features), low),
            pltpu.VMEM((rows, features), jnp.float32),
            pltpu.SemaphoreType.DMA((5,)),
        ],
        compiler_params=params(),
        name="stream_back",
    )(triple, weight, stream, middle_grad, gain, skip_weight)


ROWS = 144
THIRD = ROWS // 3


class Unit:
    def __init__(self, left, left_at, right, right_at, tiles, blocks, out, out_at):
        self.left, self.left_at = left, left_at
        self.right, self.right_at = right, right_at
        self.tiles = tiles
        self.blocks = blocks
        self.out, self.out_at = out, out_at
        self.rows = ROWS * tiles if tiles else 2 * ROWS + THIRD
        self.z_of = {(order, place): z for _, order, _, place, z in blocks}


ORDER_OF = (0, 1, 1, 0)
QUARTERS = tuple(
    ((2 * z + y) * ROWS, ORDER_OF[z], y, z // 2, z) for z in range(4) for y in range(2)
)


SHRINK, EXPAND, PROJ, ATTN, SKIP = (0, 1, 2, 3), (4, 5, 6), 7, (8, 9, 10), (11, 12)
START, TURN, SETTLE, HOP, FINISH, LINE, LINE_END, LINE_X, LINE_Y = range(9)
HALO, HEAD, PACK, BACK, NORM, OUT, VECTOR = range(9, 16)


def make_units():
    units = {}
    for z in range(4):
        blocks = [
            (y * 576 + q * ROWS, q // 2, y, q % 2, z) for y in range(2) for q in range(4)
        ]
        units[SHRINK[z]] = Unit("active", z * 1152, "upstream", 0, 0, blocks, "shrink", 0)
    for j in range(3):
        units[EXPAND[j]] = Unit("second", 0, "hidden", j, 3, QUARTERS, "expand", 3 * j)
    units[PROJ] = Unit("mixed", 0, "branch", 0, 0, QUARTERS, "proj", 0)
    for j, (first, tiles) in enumerate(TRIPLE_TILES):
        units[ATTN[j]] = Unit("normed", 0, f"triple{j}", 0, tiles, QUARTERS, "attn", first)
    for k, name in enumerate(("tok", "skp")):
        blocks = [
            (h * 576 + y * 288 + i * ROWS, h, y, i, 2 * k + h)
            for h in range(2)
            for y in range(2)
            for i in range(2)
        ]
        units[SKIP[k]] = Unit(name, 0, "stream_cols", 0, 0, blocks, "skip", 0)
    return units


TRIPLE_TILES = ((0, 3), (3, 2), (5, 2))
GRADS = (
    ("shrink", (576, 288)),
    ("expand", (144, 1152)),
    ("proj", (144, 288)),
    ("attn", (144, 864)),
    ("skip", (288, 288)),
)
PART_SLOTS, FIRST_SLOTS, SECOND_SLOTS, LAST_SLOTS = 4, 4, 4, 5
LINE_FIRST = (PROJ, EXPAND[0], ATTN[0])
X_FIRST = (SHRINK[0], EXPAND[1], ATTN[1])
PLAN = (
    (START, PROJ), (LINE, PROJ, 1, 0), (LINE, PROJ, 1, 1), (LINE, PROJ, 1, 2), (START, SHRINK[0]),
    (START, EXPAND[2]), (START, SHRINK[2]), (LINE, PROJ, 2, 0), (LINE, PROJ, 2, 1), (LINE, PROJ, 3, 0),
    (TURN, SHRINK[0]), (LINE_END, PROJ), (START, EXPAND[0]), (LINE, EXPAND[0], 1, 0),
    (LINE, EXPAND[0], 1, 1), (LINE, EXPAND[0], 1, 2), (START, EXPAND[1]), (HALO,), (HEAD, 2),
    (LINE_X, PROJ), (HEAD, 2), (LINE, EXPAND[0], 2, 0), (TURN, EXPAND[2]), (HEAD, 4), (TURN, SHRINK[2]),
    (LINE, EXPAND[0], 2, 1), (HEAD, 2), (LINE, EXPAND[0], 3, 0), (TURN, EXPAND[1]), (SETTLE, SHRINK[0]),
    (START, SHRINK[1]), (LINE_Y, PROJ), (HEAD, 2), (SETTLE, EXPAND[2]), (START, SHRINK[3]),
    (SETTLE, SHRINK[2]), (HOP, SHRINK[0], 2), (HEAD, 2), (HOP, EXPAND[2], 2), (LINE_END, EXPAND[0]),
    (HEAD, 2), (SETTLE, EXPAND[1]), (HOP, SHRINK[0], 3), (PACK,), (HOP, SHRINK[2], 2),
    (HOP, SHRINK[2], 3), (HOP, EXPAND[2], 3), (START, ATTN[0]), (START, ATTN[1]), (LINE_X, EXPAND[0]),
    (HOP, EXPAND[1], 2), (TURN, SHRINK[1]), (LINE, ATTN[0], 1, 0), (LINE, ATTN[0], 1, 1),
    (LINE, ATTN[0], 1, 2), (START, ATTN[2]), (FINISH, SHRINK[0]), (BACK, 0), (HOP, EXPAND[1], 3),
    (TURN, SHRINK[3]), (BACK, 1), (LINE_Y, EXPAND[0]), (BACK, 2), (TURN, ATTN[1]), (LINE, ATTN[0], 2, 0),
    (NORM,), (SETTLE, SHRINK[1]), (START, SKIP[0]), (LINE, ATTN[0], 2, 1), (FINISH, SHRINK[2]),
    (VECTOR, 0), (FINISH, EXPAND[2]), (FINISH, EXPAND[1]), (TURN, ATTN[2]), (VECTOR, 1),
    (SETTLE, SHRINK[3]), (LINE, ATTN[0], 3, 0), (START, SKIP[1]), (SETTLE, ATTN[1]), (OUT, 0), (OUT, 1),
    (OUT, 2), (TURN, SKIP[0]), (HOP, SHRINK[1], 2), (HOP, SHRINK[1], 3), (HOP, SHRINK[3], 2),
    (SETTLE, ATTN[2]), (VECTOR, 2), (HOP, ATTN[1], 2), (FINISH, SHRINK[1]), (LINE_END, ATTN[0]),
    (HOP, SHRINK[3], 3), (HOP, ATTN[1], 3), (HOP, ATTN[2], 2), (HOP, ATTN[2], 3), (TURN, SKIP[1]),
    (SETTLE, SKIP[0]), (VECTOR, 3), (HOP, SKIP[0], 2), (FINISH, SHRINK[3]), (LINE_X, ATTN[0]),
    (FINISH, ATTN[1]), (SETTLE, SKIP[1]), (FINISH, ATTN[2]), (HOP, SKIP[0], 3), (HOP, SKIP[1], 2),
    (VECTOR, 4), (LINE_Y, ATTN[0]), (HOP, SKIP[1], 3), (FINISH, SKIP[0]), (FINISH, SKIP[1]), (VECTOR, 5),
)


def add_into(target, other):
    target[...] = (target[...].astype(jnp.float32) + other[...].astype(jnp.float32)).astype(
        target.dtype
    )


class Refs(dict):
    __getattr__ = dict.__getitem__


def gradient_kernel(r):
    seq, batch = lax.axis_index(SEQ), lax.axis_index(BATCH)
    z, y = seq // 2, seq % 2
    x, c = batch // 2, batch % 2
    at = {
        "core": (seq, 2 * x + (1 - c)),
        "x": (seq, 2 * (1 - x) + c),
        "y": (2 * z + (1 - y), batch),
        "above": (2 * jnp.minimum(z + 1, 3) + y, batch),
        "below": (2 * jnp.maximum(z - 1, 0) + y, batch),
        "far": (2 * ((z + 2) % 4) + y, batch),
        "next": (jnp.minimum(seq + 1, 7), batch),
        "last": (jnp.maximum(seq - 1, 0), batch),
    }
    at["pair"] = (2 * (z + 1 - 2 * (z % 2)) + y, batch)
    units = make_units()
    low = jnp.bfloat16
    rows, features = r.tok.shape
    ids = {}

    def remote(key, src, dst, side):
        i = ids.setdefault(key, len(ids))
        return pltpu.make_async_remote_copy(
            src_ref=src,
            dst_ref=dst,
            send_sem=r.sent.at[i],
            recv_sem=r.came.at[i],
            device_id=at[side],
            device_id_type=MESH,
        )

    barrier = pltpu.get_barrier_semaphore()

    def greet(side):
        pl.semaphore_signal(barrier, 1, device_id=at[side], device_id_type=MESH)

    for side in ("core", "x", "y", "far"):
        greet(side)
    for side, some in (
        ("above", z < 3),
        ("below", z > 0),
        ("next", (y == 1) & (z < 3)),
        ("last", (y == 0) & (z > 0)),
    ):
        pl.when(some)(lambda side=side: greet(side))
    more = (z < 3).astype(jnp.int32) + (z > 0).astype(jnp.int32)
    diagonal = jnp.where(y == 1, (z < 3).astype(jnp.int32), (z > 0).astype(jnp.int32))
    pl.semaphore_wait(barrier, 4 + more + diagonal)

    rim = (ITEM_MOST - 1 + 15) // 16 * 16
    window = r.window
    halo_up = remote(
        "halo_up", r.grads.at[pl.ds(rows - rim, rim)], window.at[pl.ds(rows - rim, rim)], "next"
    )
    halo_down = remote(
        "halo_down", r.grads.at[pl.ds(0, rim)], window.at[pl.ds(2 * rows, rim)], "last"
    )
    pl.when(seq < 7)(halo_up.start)
    pl.when(seq > 0)(halo_down.start)

    swaps = {}

    def swap(side, name, first):
        key = (side, name, first)
        if key in swaps:
            return
        if side == "left":
            cols = pl.ds(first, features)
            src, dst = r[name].at[:, cols], r["far_" + name].at[:, cols]
        else:
            src, dst = r[name].at[1 - c, first], r["far_" + name].at[first]
        swaps[key] = remote(key, src, dst, "core")
        swaps[key].start()

    def swap_unit(name):
        unit = units[name]
        swap("left", unit.left, unit.left_at)
        swap("right", unit.right, unit.right_at)

    order = [rest[0] for kind, *rest in PLAN if kind == START]
    for name in order:
        unit = units[name]
        swap("left", unit.left, unit.left_at)
        if not unit.right.startswith(("triple", "stream")):
            swap("right", unit.right, unit.right_at)

    slots, loads, here = {}, {}, set()

    def load(side, name, first, busy=None):
        key = (side, name, first)
        if key in slots:
            return
        slot = 1 - slots.get(busy, 1)
        for other in [k for k in slots if k[0] == side and slots[k] == slot]:
            del slots[other]
        slots[key] = slot
        if key not in here:
            swaps[key].wait_recv()
            here.add(key)
        if side == "left":
            cols = pl.ds(first, features)
            near, far = r[name].at[:, cols], r["far_" + name].at[:, cols]
            hold = r.lefts.at[slot]
        else:
            near, far = r[name].at[c, first], r["far_" + name].at[first]
            hold = r.rights.at[slot, :, pl.ds(0, near.shape[-1])]
        loads[key] = []
        for half, src in ((0, near), (1, far)):
            copy = pltpu.make_async_copy(
                src, hold.at[pl.ds(rows * half, rows)], r[side + "_sem"].at[slot, half]
            )
            copy.start()
            loads[key].append(copy)

    def keys_of(name):
        unit = units[name]
        return ("left", unit.left, unit.left_at), ("right", unit.right, unit.right_at)

    started = [name for name in order if name not in LINE_FIRST]
    both = slice(None)

    def axes(u, order):
        return ("x", "y") if order == 0 or started[u] in X_FIRST else ("y", "x")

    def credit(stage, order, side):
        return r.credit.at[(stage * 2 + order) * 2 + ("x", "y").index(side)]

    def take_credit(u, stage, order):
        if u >= (FIRST_SLOTS, SECOND_SLOTS)[stage]:
            pl.semaphore_wait(credit(stage, order, axes(u, order)[stage]), 1)

    def give_credit(u, stage, order):
        then = u + (FIRST_SLOTS, SECOND_SLOTS)[stage]
        if then < len(started):
            side = axes(then, order)[stage]
            pl.semaphore_signal(
                credit(stage, order, side), 1, device_id=at[side], device_id_type=MESH
            )

    def part_of(u, order, *index):
        unit = units[started[u]]
        place = (pl.ds(0, 2), pl.ds(0, unit.rows)) if len(index) < 3 else (pl.ds(0, unit.rows),)
        return r.part.at[(u % PART_SLOTS, order, *index, *place)]

    def moved(u, order, stage):
        land = r.land_one if stage == 0 else r.land_two
        land = land.at[u % (FIRST_SLOTS, SECOND_SLOTS)[stage], order]
        height = pl.ds(0, units[started[u]].rows)
        if stage == 1:
            send = (x, 1 - y) if axes(u, order)[1] == "y" else (1 - x, y)
            return part_of(u, order, *send), part_of(u, order, x, y), land.at[:, height]
        if axes(u, order)[0] == "x":
            send, keep = (1 - x, both), (x, both)
        else:
            send, keep = (both, 1 - y), (both, y)
        return part_of(u, order, *send), part_of(u, order, *keep), land.at[:, :, height]

    def stage_copy(u, order, stage):
        send, _, land = moved(u, order, stage)
        return remote((u, stage, order), send, land, axes(u, order)[stage])

    def compute(name, part, slot):
        unit = units[name]
        left_key, right_key = keys_of(name)
        left, right = r.lefts.at[slots[left_key]], r.rights.at[slots[right_key]]

        def product(n):
            cols = pl.ds(pl.multiple_of(n * 256, 256), 256)
            return dot_tn(left[...], right[:, cols])

        if unit.tiles:

            def body(n, carry):
                tile = product(n).astype(low)
                for i in range(2):
                    g = 2 * n + i
                    x_at = g // unit.tiles
                    t = pl.multiple_of((g - x_at * unit.tiles) * ROWS, 16)
                    for first, order, y_at, place, _ in unit.blocks:
                        part[slot, order, x_at, y_at, place, pl.ds(t, ROWS)] = tile[
                            first : first + ROWS, i * LANES : (i + 1) * LANES
                        ]
                return carry

            lax.fori_loop(0, unit.tiles, body, 0)
            return

        def body(n, carry):
            tile = product(n).astype(low)
            for first, order, y_at, place, _ in unit.blocks:
                for i in range(2):
                    part[slot, order, n, y_at, place, pl.ds(i * ROWS, ROWS)] = tile[
                        first : first + ROWS, i * LANES : (i + 1) * LANES
                    ]
            return carry

        lax.fori_loop(0, 2, body, 0)
        tile = product(2).astype(low)
        lane = lanes_of((THIRD, LANES))
        for first, order, y_at, place, _ in unit.blocks:
            for x_at in range(2):
                pieces = [
                    tile[first + s * THIRD : first + (s + 1) * THIRD, x_at * LANES :][:, :LANES]
                    for s in range(3)
                ]
                packed = jnp.where(
                    lane < 32, pieces[0], jnp.where(lane < 64, pieces[1], pieces[2])
                )
                part[slot, order, x_at, y_at, place, pl.ds(2 * ROWS, THIRD)] = packed

    def wait_sends(u):
        for order in range(2):
            for stage in range(2):
                stage_copy(u, order, stage).wait_send()

    def fetch(name, ahead):
        for key in keys_of(name):
            load(*key)
            for copy in loads.pop(key, ()):
                copy.wait()
        if ahead is not None and ahead not in SKIP:
            for key, busy in zip(keys_of(ahead), keys_of(name)):
                if key in swaps:
                    load(*key, busy)

    def first_stage(u):
        if u >= PART_SLOTS:
            wait_sends(u - PART_SLOTS)
        compute(started[u], r.part, u % PART_SLOTS)
        for order in range(2):
            take_credit(u, 0, order)
            stage_copy(u, order, 0).start()

    def second_stage(u):
        for order in range(2):
            stage_copy(u, order, 0).wait_recv()
            _, keep, land = moved(u, order, 0)
            add_into(keep, land)
            give_credit(u, 0, order)
            take_credit(u, 1, order)
            stage_copy(u, order, 1).start()

    def last_ref(u, order, place):
        return r.ends.at[u % LAST_SLOTS, order, place, pl.ds(0, units[started[u]].rows)]

    def third_stage(u):
        if u >= LAST_SLOTS:
            chain_sends(u - LAST_SLOTS)
        for order in range(2):
            stage_copy(u, order, 1).wait_recv()
            _, keep, land = moved(u, order, 1)
            for place in range(2):
                value = keep.at[place][...].astype(jnp.float32)
                value = value + land.at[place][...].astype(jnp.float32)
                last_ref(u, order, place)[...] = value.astype(low)
            give_credit(u, 1, order)

    def chain_copy(u, order, place, up):
        pool, i = r.chain_at[started[u], order, place, up]
        dst = r[pool].at[i, pl.ds(0, units[started[u]].rows)]
        src = last_ref(u, order, place)
        key = (u, "chain", order, place, up)
        return remote(key, src, dst, "above" if up else "below"), dst

    def hop(u, step):
        for up, me in ((True, step - 1), (False, 4 - step)):
            todo = [
                key
                for key, z_at in sorted(
                    units[started[u]].z_of.items(), key=lambda item: -item[1] if up else item[1]
                )
                if ((z_at > me) if up else (z_at < me))
            ]

            @pl.when(z == me)
            def _():
                for order, place in todo:
                    copy, land = chain_copy(u, order, place, up)
                    if step > 1:
                        copy.wait_recv()
                        add_into(last_ref(u, order, place), land)
                    copy.start()

    def chain_sends(u):
        for (order, place), z_at in units[started[u]].z_of.items():
            for up, some in ((True, z_at > 0), (False, z_at < 3)):
                if some:

                    @pl.when((z < z_at) if up else (z > z_at))
                    def _():
                        chain_copy(u, order, place, up)[0].wait_send()

    def finish(u):
        unit = units[started[u]]
        for (order, place), z_at in unit.z_of.items():

            @pl.when(z == z_at)
            def _():
                value = last_ref(u, order, place)[...].astype(jnp.float32)
                for up, have in ((True, z_at > 0), (False, z_at < 3)):
                    if have:
                        copy, land = chain_copy(u, order, place, up)
                        copy.wait_recv()
                        value = value + land[...].astype(jnp.float32)
                store_out(unit, order, place, value)

    def store_out(unit, order, place, value):
        out = r["out_" + unit.out]
        if unit.tiles:
            for t in range(unit.tiles):
                col = (unit.out_at + t) * LANES
                width = min(LANES, out.shape[1] - col)
                out[:, col : col + width] = value[t * ROWS : (t + 1) * ROWS, :width]
            return
        base = {"shrink": (2 * order + place) * ROWS, "proj": 0, "skip": place * ROWS}[unit.out]
        for i in range(2):
            out[base : base + ROWS, i * LANES : (i + 1) * LANES] = value[i * ROWS : (i + 1) * ROWS]
        for s in range(3):
            out[base + s * THIRD : base + (s + 1) * THIRD, 256:288] = value[
                2 * ROWS : 2 * ROWS + THIRD, s * 32 : (s + 1) * 32
            ]

    def line_ref(name, order, place):
        return r.line.at[0, order, both, both, place, pl.ds(0, units[name].rows)]

    def line_copy(name, order, place, up):
        i = r.line_at[name, order, place, up]
        dst = r.line_land.at[i, both, both, pl.ds(0, units[name].rows)]
        key = (name, "line", order, place, up)
        return remote(key, line_ref(name, order, place), dst, "above" if up else "below"), dst

    def line_hop(name, step, turn):
        for up, me in ((True, step - 1), (False, 4 - step)):
            todo = [
                key
                for key, z_at in sorted(
                    units[name].z_of.items(), key=lambda item: -item[1] if up else item[1]
                )
                if ((z_at > me) if up else (z_at < me))
            ][turn : turn + 1]

            @pl.when(z == me)
            def _():
                for order, place in todo:
                    copy, land = line_copy(name, order, place, up)
                    if step > 1:
                        copy.wait_recv()
                        add_into(line_ref(name, order, place), land)
                    copy.start()

    def line_credit(act):
        for some, side, here, there in ((z < 3, "above", 8, 9), (z > 0, "below", 9, 8)):

            @pl.when(some)
            def _():
                if act is pl.semaphore_wait:
                    pl.semaphore_wait(r.credit.at[here], 1)
                else:
                    pl.semaphore_signal(
                        r.credit.at[there], 1, device_id=at[side], device_id_type=MESH
                    )

    def line_copies(name):
        i = LINE_FIRST.index(name)
        height = pl.ds(0, units[name].rows)
        own = r.line_own.at[i]
        return (
            remote((name, "line_x"), own.at[1 - x, both, height], r.line_x.at[i, both, height], "x"),
            remote((name, "line_y"), own.at[x, 1 - y, height], r.line_y.at[i, height], "y"),
        )

    def line_stage(name, stage):
        i = LINE_FIRST.index(name)
        unit = units[name]
        height = pl.ds(0, unit.rows)
        if stage == "end":
            for (order, place), z_at in unit.z_of.items():

                @pl.when(z == z_at)
                def _():
                    lands = []
                    for up, have in ((True, z_at > 0), (False, z_at < 3)):
                        if have:
                            copy, land = line_copy(name, order, place, up)
                            copy.wait_recv()
                            lands.append(land)
                    for x_at in range(2):
                        for y_at in range(2):
                            value = line_ref(name, order, place)[x_at, y_at].astype(jnp.float32)
                            for land in lands:
                                value = value + land[x_at, y_at].astype(jnp.float32)
                            r.line_own[i, x_at, y_at, height] = value.astype(low)

            line_copies(name)[0].start()
            if i + 1 < len(LINE_FIRST):
                line_credit(pl.semaphore_signal)
        elif stage == "x":
            line_copies(name)[0].wait_recv()
            add_into(r.line_own.at[i, x, both, height], r.line_x.at[i, both, height])
            line_copies(name)[1].start()
        else:
            line_copies(name)[1].wait_recv()
            value = r.line_own[i, x, y, height].astype(jnp.float32)
            value = value + r.line_y[i, height].astype(jnp.float32)
            store_out(unit, 0, 0, value)

    def line_drain(name):
        for (order, place), z_at in units[name].z_of.items():
            for up, some in ((True, z_at > 0), (False, z_at < 3)):
                if some:

                    @pl.when((z < z_at) if up else (z > z_at))
                    def _():
                        line_copy(name, order, place, up)[0].wait_send()

    def head_load(h):
        return pltpu.make_async_copy(
            r.wins.at[:, h], r.head.at[h % 2], r.head_sem.at[h % 2]
        )

    done = {"heads": 0}

    def halo_work():
        head_load(0).start()
        own = pltpu.make_async_copy(r.grads, window.at[pl.ds(rows, rows)], r.chunk_sem.at[0])
        own.start()
        pad = rows - rim
        blank = jnp.zeros((pad, window.shape[1]), low)
        window[0:pad] = blank
        window[3 * rows - pad :] = blank

        @pl.when(seq == 0)
        def _():
            window[pad:rows] = jnp.zeros((rim, window.shape[1]), low)

        @pl.when(seq == 7)
        def _():
            window[2 * rows : 2 * rows + rim] = jnp.zeros((rim, window.shape[1]), low)

        back_masks(r.id_col, r.id_row, r.own_hide, r.rim_hide, rows)
        r.probs[...] = jnp.zeros(r.probs.shape, low)
        r.scored[...] = jnp.zeros(r.scored.shape, low)
        own.wait()
        pl.when(seq > 0)(halo_up.wait_recv)
        pl.when(seq < 7)(halo_down.wait_recv)
        r.stats[...] = window[:, features:]

    def heads_work(count):
        first = done["heads"]
        done["heads"] += count

        def body(h, carry):
            head_load(h).wait()

            @pl.when(h + 1 < HEADS)
            def _():
                head_load(h + 1).start()

            tile = (h * HEAD_DIM) // LANES
            off = h * HEAD_DIM - tile * LANES
            cols = pl.ds(pl.multiple_of(tile * LANES, LANES), 2 * LANES)
            pair = pltpu.roll(window[:, cols], (2 * LANES - off) % (2 * LANES), 1)[:, :LANES]
            r.grad_head[...] = jnp.where(
                lanes_of((3 * rows, LANES)) < HEAD_DIM, pair, jnp.zeros_like(pair)
            )
            head = r.head.at[h % 2]
            found = back_head(
                h, head.at[0], head.at[1], head.at[2], r.grad_head, r.stats[...],
                r.own_hide, r.rim_hide, r.probs, r.scored,
            )
            wide = lanes_of((rows, 2 * LANES))
            inside = (wide >= off) & (wide < off + HEAD_DIM)
            for part, value in enumerate(found):
                moved = pltpu.roll(jnp.concatenate([value, jnp.zeros_like(value)], axis=1), off, 1)
                r.triple[part, :, cols] = jnp.where(inside, moved, r.triple[part, :, cols])
            return carry

        lax.fori_loop(first, first + count, body, 0)

    sums = r.sums

    def pack_work():
        for p in range(3):
            if p != 1:
                row = 3 + p // 2
                sums[row : row + 1] = column_sum(r.triple[p, :, :features].astype(jnp.float32))
        for b in range(4):
            pieces = []
            for p in range(3):
                low_at, high_at = max(864 * b, features * p), min(864 * (b + 1), features * (p + 1))
                if low_at < high_at:
                    pieces.append(
                        r.triple[p, :, low_at - features * p : high_at - features * p]
                    )
            pieces.append(jnp.zeros((rows, 32), low))
            value = jnp.concatenate(pieces, axis=1)
            for j, (first, tiles) in enumerate(TRIPLE_TILES):
                width = tiles * LANES
                r[f"triple{j}"][b % 2, 0, :, width * (b // 2) : width * (b // 2 + 1)] = value[
                    :, first * LANES : first * LANES + width
                ]
        for j in range(len(TRIPLE_TILES)):
            swap("right", f"triple{j}", 0)

    chunks = [(p, first, count) for p in range(3) for first, count in ((0, 768), (768, 384))]

    def weight_load(i):
        slot = i % 2
        if i < 6:
            p, first, count = chunks[i]
            src = r.attn_weight.at[pl.ds(first, count), pl.ds(features * p, features)]
        else:
            count = 768
            src = r.skip_weight.at[pl.ds(768 * (i - 6), 768)]
        return pltpu.make_async_copy(
            src, r.lefts.at[slot, pl.ds(0, count)], r.weight_sem.at[slot]
        )

    def back_work(p):
        if p == 0:
            weight_load(0).start()
        for i in (2 * p, 2 * p + 1):
            _, first, count = chunks[i]
            weight_load(i).wait()
            if i < 5:
                weight_load(i + 1).start()
            part = dot_nt(r.triple[p, :, :features], r.lefts[i % 2, :count])
            cols = slice(first, first + count)
            if p == 0:
                r.normed_grad[:, cols] = part
            else:
                r.normed_grad[:, cols] += part

    def norm_work():
        gain = vector(r.gain)
        sums[0:3] = jnp.zeros((3, features), jnp.float32)
        chunk = r.chunk
        for i in range(rows // LANES):
            here = pl.ds(i * LANES, LANES)
            copies = [
                pltpu.make_async_copy(r[name].at[here], chunk.at[k], r.chunk_sem.at[k])
                for k, name in enumerate(("stream", "middle_grad"))
            ]
            for copy in copies:
                copy.start()
            for copy in copies:
                copy.wait()
            unit, scale = row_norm(chunk[0])
            cotangent = r.normed_grad[here]
            rounded = (chunk[1] + norm_back(unit, scale, gain, cotangent)).astype(low)
            window[here, :features] = rounded
            sums[0:1] += column_sum(rounded.astype(jnp.float32))
            sums[1:2] += column_sum(cotangent * unit)
            sums[2:3] += column_sum(cotangent)
        by_core_store(r.stream_cols, window[0:rows, :features])
        swap("right", "stream_cols", 0)

    def out_copies():
        return [
            pltpu.make_async_copy(
                r.triple.at[k, :, pl.ds(0, features)], r[name], r.chunk_sem.at[k]
            )
            for k, name in enumerate(("out_tok", "out_skp"))
        ]

    def out_work(k):
        i = 6 + k
        if k == 0:
            weight_load(i).start()
        weight_load(i).wait()
        if k < 2:
            weight_load(i + 1).start()
        value = dot_nt(window[0:rows, :features], r.lefts[i % 2, :768]).astype(low)
        for half in range(2):
            base = features * half
            first, last = max(768 * k, base), min(768 * (k + 1), base + features)
            if first < last:
                r.triple[half, :, first - base : last - base] = value[
                    :, first - 768 * k : last - 768 * k
                ]
        if k == 2:
            for copy in out_copies():
                copy.start()

    sides = ("core", "x", "y", "pair", "far")

    def vec_work(step):
        vec, land = r.vec, r.vec_land
        if step == 0:
            vec[0] = r.vec_in[...]
            vec[0, 0:5] = sums[0:5]
        else:
            remote(("vec", step - 1), vec.at[step - 1], land.at[step - 1], sides[step - 1]).wait_recv()
            total = vec[step - 1] + land[step - 1]
            if step == len(sides):
                r.out_vec[...] = total
            else:
                vec[step] = total
        if step < len(sides):
            remote(("vec", step), vec.at[step], land.at[step], sides[step]).start()

    def start(name):
        i = order.index(name)
        fetch(name, order[i + 1] if i + 1 < len(order) else None)
        if name in LINE_FIRST:
            i = LINE_FIRST.index(name)
            if i > 0:
                line_drain(LINE_FIRST[i - 1])
                line_credit(pl.semaphore_wait)
            compute(name, r.line, 0)
        else:
            first_stage(started.index(name))

    def third(name):
        third_stage(started.index(name))
        hop(started.index(name), 1)

    steps = {
        START: start,
        TURN: lambda name: second_stage(started.index(name)),
        SETTLE: third,
        HOP: lambda name, step: hop(started.index(name), step),
        FINISH: lambda name: finish(started.index(name)),
        LINE: line_hop,
        LINE_END: lambda name: line_stage(name, "end"),
        LINE_X: lambda name: line_stage(name, "x"),
        LINE_Y: lambda name: line_stage(name, "y"),
        HALO: halo_work,
        HEAD: heads_work,
        PACK: pack_work,
        BACK: back_work,
        NORM: norm_work,
        OUT: out_work,
        VECTOR: vec_work,
    }
    for kind, *rest in PLAN:
        steps[kind](*rest)
    for copy in out_copies():
        copy.wait()
    for name in LINE_FIRST[-1:]:
        line_drain(name)
    for name in LINE_FIRST:
        for copy in line_copies(name):
            copy.wait_send()
    for copy in swaps.values():
        copy.wait_send()
    count = len(started)
    for u in range(max(0, count - PART_SLOTS), count):
        wait_sends(u)
    for u in range(max(0, count - LAST_SLOTS), count):
        chain_sends(u)
    for step in range(len(sides)):
        remote(("vec", step), r.vec.at[step], r.vec_land.at[step], sides[step]).wait_send()
    pl.when(seq < 7)(halo_up.wait_send)
    pl.when(seq > 0)(halo_down.wait_send)


def gradients(values, vec):
    low, full = jnp.bfloat16, jnp.float32
    rows, features = values["tok"].shape
    names, operands, in_specs, out_shape, out_specs, scratch = [], [], [], [], [], []
    held = ("id_col", "id_row", "gain")
    for name, value in values.items():
        names.append(name)
        operands.append(value)
        in_specs.append(whole() if name in held else anywhere())
    names.append("vec_in")
    operands.append(vec)
    in_specs.append(whole())

    def out(name, shape, dtype, spec):
        names.append(name)
        out_shape.append(jax.ShapeDtypeStruct(shape, dtype))
        out_specs.append(spec)

    for name, shape in GRADS:
        out("out_" + name, shape, full, whole())
    out("out_vec", vec.shape, full, whole())
    out("out_tok", (rows, features), low, anywhere())
    out("out_skp", (rows, features), low, anywhere())
    for name in ("active", "second", "mixed", "normed", "tok", "skp"):
        out("far_" + name, values[name].shape, low, anywhere())
    for name in ("upstream", "hidden", "branch"):
        out("far_" + name, values[name].shape[1:], low, anywhere())
    cores = {f"triple{j}": 2 * LANES * tiles for j, (_, tiles) in enumerate(TRIPLE_TILES)}
    cores["stream_cols"] = 768
    for name, width in cores.items():
        out("far_" + name, (1, rows, width), low, anywhere())

    def add(**kinds):
        names.extend(kinds.keys())
        scratch.extend(kinds.values())

    most = 3 * ROWS
    for name, width in cores.items():
        add(**{name: pltpu.VMEM((2, 1, rows, width), low)})
    add(lefts=pltpu.VMEM((2, 2 * rows, features), low))
    add(rights=pltpu.VMEM((2, 2 * rows, 768), low))
    add(left_sem=pltpu.SemaphoreType.DMA((2, 2)))
    add(right_sem=pltpu.SemaphoreType.DMA((2, 2)))
    add(part=pltpu.VMEM((PART_SLOTS, 2, 2, 2, 2, most, LANES), low))
    add(land_one=pltpu.VMEM((FIRST_SLOTS, 2, 2, 2, most, LANES), low))
    add(land_two=pltpu.VMEM((SECOND_SLOTS, 2, 2, most, LANES), low))
    add(ends=pltpu.VMEM((LAST_SLOTS, 2, 2, most, LANES), low))
    chain_at, sizes = {}, {"chain_short": 0, "chain_long": 0}
    for name, unit in make_units().items():
        if name in LINE_FIRST:
            continue
        pool = "chain_short" if unit.rows <= 2 * ROWS + THIRD else "chain_long"
        for (order, place), z_at in unit.z_of.items():
            for up, have in ((True, z_at > 0), (False, z_at < 3)):
                if have:
                    chain_at[name, order, place, up] = (pool, sizes[pool])
                    sizes[pool] += 1
    add(chain_short=pltpu.VMEM((sizes["chain_short"], 2 * ROWS + THIRD, LANES), low))
    add(chain_long=pltpu.VMEM((sizes["chain_long"], most, LANES), low))
    add(sent=pltpu.SemaphoreType.DMA((256,)))
    add(came=pltpu.SemaphoreType.DMA((256,)))
    span = 3 * rows
    add(window=pltpu.VMEM((span, features + LANES), low))
    add(stats=pltpu.VMEM((span, LANES), low))
    add(head=pltpu.VMEM((2, 3, span, LANES), low))
    add(head_sem=pltpu.SemaphoreType.DMA((2,)))
    add(grad_head=pltpu.VMEM((span, LANES), low))
    add(own_hide=pltpu.VMEM((rows // LANES, LANES, span - rows + LANES), low))
    add(rim_hide=pltpu.VMEM((2 * rows // LANES, LANES, rows), low))
    add(probs=pltpu.VMEM((span, rows), low))
    add(scored=pltpu.VMEM((span, rows), low))
    add(triple=pltpu.VMEM((3, rows, features + LANES), low))
    add(weight_sem=pltpu.SemaphoreType.DMA((2,)))
    add(normed_grad=pltpu.VMEM((rows, features), full))
    add(chunk=pltpu.VMEM((2, LANES, features), full))
    add(chunk_sem=pltpu.SemaphoreType.DMA((2,)))
    add(credit=pltpu.SemaphoreType.REGULAR((10,)))
    lines = len(LINE_FIRST)
    line_at = {}
    for name in LINE_FIRST:
        for (order, place), z_at in make_units()[name].z_of.items():
            for up, have in ((True, z_at > 0), (False, z_at < 3)):
                if have:
                    line_at[name, order, place, up] = len(
                        [key for key in line_at if key[0] == name]
                    )
    add(line=pltpu.VMEM((1, 2, 2, 2, 2, most, LANES), low))
    add(line_land=pltpu.VMEM((6, 2, 2, most, LANES), low))
    add(line_own=pltpu.VMEM((lines, 2, 2, most, LANES), low))
    add(line_x=pltpu.VMEM((lines, 2, most, LANES), low))
    add(line_y=pltpu.VMEM((lines, most, LANES), low))
    add(sums=pltpu.VMEM((8, features), full))
    add(vec=pltpu.VMEM((5, *vec.shape), full))
    add(vec_land=pltpu.VMEM((5, *vec.shape), full))

    def kernel(*refs):
        gradient_kernel(Refs(zip(names, refs), chain_at=chain_at, line_at=line_at))

    found = pl.pallas_call(
        kernel,
        out_shape=out_shape,
        in_specs=in_specs,
        out_specs=out_specs,
        scratch_shapes=scratch,
        compiler_params=pltpu.CompilerParams(
            collective_id=0, has_side_effects=True, vmem_limit_bytes=VMEM_MOST
        ),
        name="gradients",
    )(*operands)
    return dict(zip([name for name, _ in GRADS] + ["vec", "tok", "skp"], found))


VECTORS = ((0, 1), (1, 1), (2, 1), (3, 2), (5, 1), (6, 1), (7, 1), (9, 4), (8, 1))


def results_kernel(*refs):
    count = len(GRADS) + 2
    total, sources, targets = refs[0], refs[1 : 1 + count], refs[1 + count :]
    for source, target in zip(sources, targets):
        target[...] = source[...].T if source.shape != target.shape else source[...]
    features = total.shape[1]
    place = lax.axis_index(SEQ) * lax.axis_size(BATCH) + lax.axis_index(BATCH)
    for (first, rows), target in zip(VECTORS, targets[count:]):
        width = target.shape[0]
        row = place * width // features
        off = place * width - row * features
        line = jnp.broadcast_to(total[pl.ds(first + row, 1)], (8, features))
        target[...] = pltpu.roll(line, (features - off) % features, 1)[0, :width]


def results(found):
    values = [found[name] for name in [*(name for name, _ in GRADS), "tok", "skp"]]
    devices = lax.axis_size(SEQ) * lax.axis_size(BATCH)
    features = found["vec"].shape[1]
    shapes = [values[0].shape[::-1], *(value.shape for value in values[1:])]
    out = [jax.ShapeDtypeStruct(shape, value.dtype) for shape, value in zip(shapes, values)]
    out += [
        jax.ShapeDtypeStruct((rows * features // devices,), jnp.float32) for _, rows in VECTORS
    ]
    got = pl.pallas_call(
        results_kernel,
        out_shape=out,
        in_specs=[whole()] * (1 + len(values)),
        out_specs=[whole()] * len(out),
        compiler_params=params(),
        name="results",
    )(found["vec"], *values)
    return (got[0].T, *got[1 : len(values)]), got[len(values) :]


def unsplit(value):
    blocks = []
    for b in range(4):
        x, c = b // 2, b % 2
        blocks.append(value[c, 0, :, 256 * x : 256 * x + 256])
        blocks.append(value[c, 0, :, 512 + LANES * x : 544 + LANES * x])
    return jnp.concatenate(blocks, axis=1)


def outer_sum(left, right):
    return dot_tn(left, right)


def summed(lefts, rights, vector_list):
    hidden = rights["hidden"]
    _, pieces, rows, width = hidden.shape
    hidden = hidden.reshape(2, pieces, rows, 2, width // 2).transpose(2, 3, 0, 1, 4)
    columns_of = dict(
        joined=unsplit(rights["stream"]),
        normed=rights["triple"],
        mixed=unsplit(rights["branch"]),
        second=hidden.reshape(rows, -1),
        active=unsplit(rights["upstream"]),
    )
    parts = []
    for name in ("joined", "normed", "mixed", "second", "active"):
        gathered = lax.all_gather(lefts[name], BATCH, axis=0, tiled=True)
        columns = lax.all_to_all(
            columns_of[name], BATCH, split_axis=1, concat_axis=0, tiled=True
        )
        parts.append(outer_sum(gathered, columns).astype(jnp.bfloat16))
    parts = lax.psum_scatter(tuple(parts), SEQ, scatter_dimension=0, tiled=True)
    vectors = tuple(
        lax.psum_scatter(vector, (SEQ, BATCH), scatter_dimension=0, tiled=True)
        for vector in vector_list
    )
    return tuple(part.astype(jnp.float32) for part in parts), vectors


def rims(value, width):
    size = lax.axis_size(SEQ)
    up = [(i, i + 1) for i in range(size - 1)]
    down = [(j, i) for i, j in up]
    return (
        lax.ppermute(value[-width:], SEQ, up),
        lax.ppermute(value[:width], SEQ, down),
    )


def on_device(
    tokens,
    skip_tokens,
    segment_ids,
    upstream,
    skip_weight,
    skip_bias,
    first_gain,
    first_shift,
    attn_weight,
    attn_bias,
    proj_weight,
    proj_bias,
    second_gain,
    second_shift,
    expand_weight,
    expand_bias,
    shrink_weight,
    shrink_bias,
):
    _, rows, features = tokens.shape
    rim = (ITEM_MOST - 1 + 15) // 16 * 16
    tok, skp, above = tokens[0], skip_tokens[0], upstream[0]
    position = lax.axis_index(SEQ)

    stream, normed, wins, mixed, lse, active_grad, id_col, id_row = forward(
        tok, skp, skip_weight, skip_bias, first_gain, first_shift, attn_weight, attn_bias,
        segment_ids, above, shrink_weight,
    )
    (
        result, active, hidden_by_core, second, branch, branch_by_core, up_by_core, middle_grad,
        mixed_grad, sums,
    ) = layer(
        stream, mixed, lse, above, active_grad,
        (
            proj_weight, proj_bias, second_gain, second_shift, expand_weight, expand_bias,
            shrink_weight, shrink_bias,
        ),
    )
    if lax.axis_size(SEQ) == 8 and lax.axis_size(BATCH) == 4:
        found = gradients(
            dict(
                active=active, second=second, mixed=mixed, normed=normed, tok=tok, skp=skp,
                upstream=up_by_core, hidden=hidden_by_core, branch=branch_by_core, wins=wins,
                grads=mixed_grad, id_col=id_col, id_row=id_row, stream=stream,
                middle_grad=middle_grad, gain=first_gain, attn_weight=attn_weight,
                skip_weight=skip_weight,
            ),
            sums,
        )
        (shrink, expand, proj, attn, skip, tok_grad, skip_grad), vectors = results(found)
        weight_parts = (skip, attn, proj, expand, shrink)
    else:
        before, after = rims(mixed_grad, rim)
        blank = jnp.zeros((rows - rim, mixed_grad.shape[1]), mixed_grad.dtype)
        grad_window = jnp.concatenate([blank, before, mixed_grad, after, blank], axis=0)
        stats = grad_window[:, features:]
        triple, triple_sum = attend_back(wins, grad_window, stats, id_col, id_row)
        tok_grad, skip_grad, stream_by_core, stream_sums = stream_back(
            triple, attn_weight, stream, middle_grad, first_gain, skip_weight
        )
        vector_list = (
            stream_sums[2],
            stream_sums[0],
            stream_sums[1],
            jnp.concatenate([triple_sum[0, :features], triple_sum[0, 2 * features :]]),
            sums[5],
            sums[6],
            sums[7],
            sums[9:13].reshape(-1),
            sums[8],
        )
        joined = jnp.concatenate([tok, skp], axis=1)
        weight_parts, vectors = summed(
            dict(active=active, second=second, mixed=mixed, normed=normed, joined=joined),
            dict(
                upstream=up_by_core,
                hidden=hidden_by_core,
                branch=branch_by_core,
                triple=triple,
                stream=stream_by_core,
            ),
            vector_list,
        )
    return (
        result[None],
        tok_grad[None],
        skip_grad[None],
        weight_parts[0],
        vectors[0],
        vectors[1],
        vectors[2],
        weight_parts[1],
        vectors[3],
        weight_parts[2],
        vectors[4],
        vectors[5],
        vectors[6],
        weight_parts[3],
        vectors[7],
        weight_parts[4],
        vectors[8],
    )


def solution(mesh):
    in_specs = (
        P(BATCH, SEQ, None),
        P(BATCH, SEQ, None),
        P(BATCH, None),
        P(BATCH, SEQ, None),
        P(),
        P(),
        P(),
        P(),
        P(),
        P(),
        P(),
        P(),
        P(),
        P(),
        P(),
        P(),
        P(),
        P(),
    )
    out_specs = (
        P(BATCH, SEQ, None),
        P(BATCH, SEQ, None),
        P(BATCH, SEQ, None),
        P(SEQ, BATCH),
        P((SEQ, BATCH)),
        P((SEQ, BATCH)),
        P((SEQ, BATCH)),
        P(SEQ, BATCH),
        P((SEQ, BATCH)),
        P(SEQ, BATCH),
        P((SEQ, BATCH)),
        P((SEQ, BATCH)),
        P((SEQ, BATCH)),
        P(SEQ, BATCH),
        P((SEQ, BATCH)),
        P(SEQ, BATCH),
        P((SEQ, BATCH)),
    )
    return jax.shard_map(
        on_device, mesh=mesh, in_specs=in_specs, out_specs=out_specs, check_vma=False
    )
```
